128 devices in a mesh: wide: 32 (over z, x, core), narrow: 4 (over y).
Axes of the slice: x: 4, y: 4, z: 4, core: 2. Of those that a mesh axis runs over, the one named last changes fastest.
Arguments:
- tokens: bfloat16 [131072, 512], P(('wide', 'narrow')), may hold values from -6 to 6
- rotation: int32 [131072], P(('wide', 'narrow')), may hold values from 0 to 131071, as said below
- qkv_weight: bfloat16 [512, 1536], replicated, may hold values from -0.25 to 0.25
- proj_weight: bfloat16 [512, 512], replicated, may hold values from -0.25 to 0.25
- up_weight: bfloat16 [512, 2048], P(None, 'narrow'), may hold values from -0.25 to 0.25
- down_weight: bfloat16 [2048, 512], P('narrow'), may hold values from -0.125 to 0.125
- cotangent: bfloat16 [131072, 512], P(('wide', 'narrow')), may hold values from -6 to 6
Outputs:
- output: bfloat16 [131072, 512], P(('wide', 'narrow'))
- grad_tokens: bfloat16 [131072, 512], P(('wide', 'narrow'))
- grad_qkv: float32 [512, 1536], replicated
- grad_proj: float32 [512, 512], replicated
- grad_up: float32 [512, 2048], P(None, 'narrow')
- grad_down: float32 [2048, 512], P('narrow')
The draws below stay inside these ranges and needn't reach their ends.
Inputs may be any that keep to these rules, and one draw needn't show every extreme that they name: rotation is a permutation. A particle held by a device goes to a device with the same narrow index, and at most 48 particles go from one device to one device; that many do in every draw.
All inputs are finite; a program needn't handle non-finite values.
Results may differ from the reference program's by a relative error of at most 0.024.
Values may be sent and summed in bfloat16 or wider, within the bound.
No kernel may reach another device: no remote copies, remote signals or barrier semaphores. Data moves between devices by JAX's collectives and lax.ppermute only.
A program may use at most 192 MiB of HBM per device.

```python
import jax
import jax.numpy as jnp
from jax import lax

D = 512
HD = 64
FF = 2048
BALL = 256
TOK_DEV = 1024
TOKENS = 131072
N_WIDE = 32
N_NARROW = 4


def draw_rotation(key, part):
    key = jax.random.fold_in(key, 11)
    group_size = N_NARROW
    peers = N_WIDE
    average = TOK_DEV // N_WIDE
    spread = average // 2
    keys = jax.random.split(key, 6)
    amplitude = jax.random.randint(keys[0], (peers // 2,), -spread, spread + 1)
    amplitude = amplitude.at[0].set(spread)
    symbols = jnp.stack([average + amplitude, average - amplitude], axis=1).reshape(peers)
    symbols = symbols[jax.random.permutation(keys[1], peers)]
    row_perm = jax.vmap(lambda item: jax.random.permutation(item, peers))(jax.random.split(keys[2], group_size))
    col_perm = jax.vmap(lambda item: jax.random.permutation(item, peers))(jax.random.split(keys[3], group_size))
    counts = symbols[(row_perm[:, :, None] + col_perm[:, None, :]) % peers]
    row_cum = jnp.cumsum(counts, axis=2)
    slots = jnp.arange(TOK_DEV, dtype=jnp.int32)
    target = jnp.sum((slots[None, None, :, None] >= row_cum[:, :, None, :]).astype(jnp.int32), axis=3)
    row_start = row_cum - counts
    rank_in = slots[None, None, :] - jnp.take_along_axis(row_start, target, axis=2)
    col_start = jnp.cumsum(counts, axis=1) - counts
    offset = jnp.take_along_axis(col_start, target, axis=2) + rank_in
    landing = jax.vmap(lambda item: jax.random.permutation(item, TOK_DEV))(jax.random.split(keys[4], group_size * peers))
    landing = landing.reshape(group_size, peers, TOK_DEV)
    narrow_index = jnp.arange(group_size, dtype=jnp.int32)[:, None, None]
    local_slot = landing[narrow_index, target, offset]
    global_slot = (target * group_size + narrow_index) * TOK_DEV + local_slot
    shuffle = jax.vmap(lambda item: jax.random.permutation(item, TOK_DEV))(jax.random.split(keys[5], group_size * peers))
    shuffle = shuffle.reshape(group_size, peers, TOK_DEV)
    per_row = jnp.take_along_axis(global_slot, shuffle, axis=2)
    return jnp.transpose(per_row, (1, 0, 2)).reshape(TOKENS).astype(jnp.int32)


def levels(own_key, dims, cuts, least, largest):
    def one(position, parts):
        heights = jax.random.uniform(jax.random.fold_in(jax.random.fold_in(own_key, 6), position), (parts,), jnp.float32, least / len(cuts), largest / len(cuts))
        return jnp.repeat(jnp.exp(heights), dims[position] // parts).reshape((-1,) + (1,) * (len(dims) - position - 1))

    factor_of = one(*cuts[0])
    for cut in cuts[1:]:
        factor_of = factor_of * one(*cut)
    return factor_of


def bell_draw(rng, shape, width, reach, cuts=(), kind=jnp.bfloat16):
    values = width * jax.random.normal(rng, shape, jnp.float32)
    if cuts:
        values = values * levels(rng, shape, cuts, -0.22, 0.18)
    return jnp.clip(values, -reach, reach).astype(kind)


def setup_inputs(seed: int = 0) -> dict:
    key_of = jax.random.split(jax.random.key(seed), 8)
    return {
        "tokens": bell_draw(key_of[0], (TOKENS, D), 1.0, 6.0, ((0, 128),)),
        "rotation": draw_rotation(jax.random.fold_in(key_of[7], 71), 0),
        "qkv_weight": bell_draw(key_of[2], (D, 3 * D), D ** -0.5, 0.25),
        "proj_weight": bell_draw(key_of[3], (D, D), D ** -0.5, 0.25),
        "up_weight": bell_draw(key_of[4], (D, FF), D ** -0.5, 0.25, ((1, 4),)),
        "down_weight": bell_draw(key_of[5], (FF, D), FF ** -0.5, 0.125, ((0, 4),)),
        "cotangent": bell_draw(key_of[6], (TOKENS, D), 1.0, 6.0, ((0, 128),)),
    }


epsilon = 1e-06

def row_scale(values):
    return lax.rsqrt(lax.optimization_barrier(jnp.mean(values * values, axis=-1, keepdims=True)) + epsilon)

def norm_back(values, scaling, gradient):
    unit = values * scaling
    return scaling * (gradient - unit * lax.optimization_barrier(jnp.mean(gradient * unit, axis=-1, keepdims=True)))

def gelu_tanh(values):
    return jax.nn.gelu(values, approximate=True)

def split_heads(block):
    row_count, columns = block.shape
    return block.reshape(row_count // BALL, BALL, columns // HD, HD).astype(jnp.float32)

def attend(packed):
    columns = packed.shape[1] // 3
    queries = split_heads(packed[:, :columns])
    key_rows = split_heads(packed[:, columns:2 * columns])
    values = split_heads(packed[:, 2 * columns:])
    scaling = HD ** (-0.5)
    scores = jnp.einsum('bqhd,bkhd->bhqk', queries, key_rows) * scaling
    weights = jax.nn.softmax(scores, axis=-1)
    rounded = lax.optimization_barrier(weights.astype(jnp.bfloat16)).astype(jnp.float32)
    result = jnp.einsum('bhqk,bkhd->bqhd', rounded, values)
    return result.reshape(packed.shape[0], columns).astype(jnp.bfloat16)

def attend_back(packed, grad_out):
    columns = packed.shape[1] // 3
    queries = split_heads(packed[:, :columns])
    key_rows = split_heads(packed[:, columns:2 * columns])
    values = split_heads(packed[:, 2 * columns:])
    scaling = HD ** (-0.5)
    scores = jnp.einsum('bqhd,bkhd->bhqk', queries, key_rows) * scaling
    weights = jax.nn.softmax(scores, axis=-1)
    rounded = lax.optimization_barrier(weights.astype(jnp.bfloat16)).astype(jnp.float32)
    upstream = split_heads(grad_out)
    grad_values = jnp.einsum('bhqk,bqhd->bkhd', rounded, upstream)
    dprob = jnp.einsum('bqhd,bkhd->bhqk', upstream, values)
    dscore = weights * (dprob - lax.optimization_barrier(jnp.sum(dprob * weights, axis=-1, keepdims=True))) * scaling
    dscore = lax.optimization_barrier(dscore.astype(jnp.bfloat16)).astype(jnp.float32)
    grad_queries = jnp.einsum('bhqk,bkhd->bqhd', dscore, key_rows)
    grad_keys = jnp.einsum('bhqk,bqhd->bkhd', dscore, queries)
    row_count = packed.shape[0]
    joined = [grad_queries.reshape(row_count, columns), grad_keys.reshape(row_count, columns), grad_values.reshape(row_count, columns)]
    return jnp.concatenate(joined, axis=1).astype(jnp.bfloat16)

def blockwise(action, *arrays):
    count = arrays[0].shape[0] // TOK_DEV
    stacked = tuple((array.reshape(count, TOK_DEV, array.shape[1]) for array in arrays))
    result = lax.map(lambda items: action(*items), stacked)
    return result.reshape(count * TOK_DEV, result.shape[2])

def reference(tokens, rotation, qkv_weight, proj_weight, up_weight, down_weight, cotangent):
    half_width = D // 2
    residual = tokens.astype(jnp.float32)
    first_scale = row_scale(residual)
    normed = (residual * first_scale).astype(jnp.bfloat16)
    packed = jnp.dot(normed, qkv_weight, preferred_element_type=jnp.float32).astype(jnp.bfloat16)
    local_part = packed[:, :3 * half_width]
    moved_source = packed[:, 3 * half_width:]
    moved_part = jnp.zeros_like(moved_source).at[rotation].set(moved_source)
    local_heads = blockwise(attend, local_part)
    moved_heads = blockwise(attend, moved_part)[rotation]
    mixed_heads = jnp.concatenate([local_heads, moved_heads], axis=1)
    middle = (residual + jnp.dot(mixed_heads, proj_weight, preferred_element_type=jnp.float32)).astype(jnp.bfloat16)
    middle_f = middle.astype(jnp.float32)
    second_scale = row_scale(middle_f)
    second_normed = (middle_f * second_scale).astype(jnp.bfloat16)
    pre_act = jnp.dot(second_normed, up_weight, preferred_element_type=jnp.float32)
    activated = gelu_tanh(pre_act).astype(jnp.bfloat16)
    output = (middle_f + jnp.dot(activated, down_weight, preferred_element_type=jnp.float32)).astype(jnp.bfloat16)
    grad_act = jnp.dot(cotangent, down_weight.T, preferred_element_type=jnp.float32).astype(jnp.bfloat16)
    pullback = jax.vjp(gelu_tanh, pre_act)[1]
    grad_pre = pullback(grad_act.astype(jnp.float32))[0].astype(jnp.bfloat16)
    grad_down = jnp.dot(activated.T, cotangent, preferred_element_type=jnp.float32)
    grad_up = jnp.dot(second_normed.T, grad_pre, preferred_element_type=jnp.float32)
    grad_second = jnp.dot(grad_pre, up_weight.T, preferred_element_type=jnp.float32)
    grad_middle = (cotangent.astype(jnp.float32) + norm_back(middle_f, second_scale, grad_second)).astype(jnp.bfloat16)
    grad_heads = jnp.dot(grad_middle, proj_weight.T, preferred_element_type=jnp.float32).astype(jnp.bfloat16)
    grad_proj = jnp.dot(mixed_heads.T, grad_middle, preferred_element_type=jnp.float32)
    grad_local = blockwise(attend_back, local_part, grad_heads[:, :half_width])
    moved_upstream = grad_heads[:, half_width:]
    moved_grad = jnp.zeros_like(moved_upstream).at[rotation].set(moved_upstream)
    grad_moved = blockwise(attend_back, moved_part, moved_grad)[rotation]
    grad_packed = jnp.concatenate([grad_local, grad_moved], axis=1)
    grad_qkv = jnp.dot(normed.T, grad_packed, preferred_element_type=jnp.float32)
    grad_first = jnp.dot(grad_packed, qkv_weight.T, preferred_element_type=jnp.float32)
    grad_tokens = (grad_middle.astype(jnp.float32) + norm_back(residual, first_scale, grad_first)).astype(jnp.bfloat16)
    return (output, grad_tokens, grad_qkv, grad_proj, grad_up, grad_down)
```

```python
import jax
import jax.numpy as jnp
from jax import lax
from jax.experimental import pallas as pl
from jax.experimental.pallas import tpu as pltpu
from jax.sharding import PartitionSpec as P

HEADS = 8
BALL = 256
EPSILON = 1e-06
LANES = 128
VMEM_BYTES = 56 * 1024 * 1024

F32 = jnp.float32
BF16 = jnp.bfloat16


def mm(left, right):
    return lax.dot_general(left, right, (((1,), (0,)), ((), ())), preferred_element_type=F32)


def mm_nt(left, right):
    return lax.dot_general(left, right, (((1,), (1,)), ((), ())), preferred_element_type=F32)


def mm_tn(left, right):
    return lax.dot_general(left, right, (((0,), (0,)), ((), ())), preferred_element_type=F32)


def iota(shape, dimension):
    return lax.broadcasted_iota(jnp.int32, shape, dimension)


def row_scale(values):
    return lax.rsqrt(jnp.mean(values * values, axis=-1, keepdims=True) + EPSILON)


def norm_back(values, scaling, gradient):
    unit = values * scaling
    return scaling * (gradient - unit * jnp.mean(gradient * unit, axis=-1, keepdims=True))


def flip(block):
    return block.astype(F32).T.astype(BF16)


def as_column(row):
    return jnp.broadcast_to(row, (8, row.shape[1])).T[:, :1]


def onehot(condition):
    return jnp.where(condition, 1.0, 0.0).astype(BF16)


def head_mask(columns, head, head_size, value):
    lane = iota((1, columns), 1)
    inside = (lane >= head * head_size) & (lane < (head + 1) * head_size)
    return jnp.where(inside, value, 0.0).astype(BF16)


def ball_weights(queries, key_rows, head, head_size):
    columns = queries.shape[1]
    asked = queries * head_mask(columns, head, head_size, head_size ** (-0.5))
    scores = mm_nt(key_rows, asked)
    raised = jnp.exp(scores - jnp.max(scores, axis=0, keepdims=True))
    return raised * (1.0 / jnp.sum(raised, axis=0, keepdims=True)), asked


def ball_attend(packed, head_size):
    columns = packed.shape[1] // 3
    queries, key_rows = packed[:, :columns], packed[:, columns : 2 * columns]
    values_t = flip(packed[:, 2 * columns :])
    parts = []
    for head in range(columns // head_size):
        weights, _ = ball_weights(queries, key_rows, head, head_size)
        own = values_t[head * head_size : (head + 1) * head_size]
        parts.append(mm(own, weights.astype(BF16)))
    return jnp.concatenate(parts, axis=0).T.astype(BF16)


def ball_attend_back(packed, grad_out, head_size):
    columns = packed.shape[1] // 3
    queries, key_rows = packed[:, :columns], packed[:, columns : 2 * columns]
    values = packed[:, 2 * columns :]
    keys_t = flip(key_rows * jnp.asarray(head_size ** (-0.5), BF16))
    asked_all, upstream_all, rounded_all, dscore_all, grad_queries = [], [], [], [], []
    for head in range(columns // head_size):
        weights, asked = ball_weights(queries, key_rows, head, head_size)
        upstream = grad_out * head_mask(columns, head, head_size, 1.0)
        dprob = mm_nt(values, upstream)
        dscore = weights * (dprob - jnp.sum(dprob * weights, axis=0, keepdims=True))
        dscore = dscore.astype(BF16)
        own = keys_t[head * head_size : (head + 1) * head_size]
        grad_queries.append(mm(own, dscore))
        asked_all.append(asked)
        upstream_all.append(upstream)
        rounded_all.append(weights.astype(BF16))
        dscore_all.append(dscore)
    grad_values = mm(
        jnp.concatenate(rounded_all, axis=1), jnp.concatenate(upstream_all, axis=0)
    )
    grad_keys = mm(jnp.concatenate(dscore_all, axis=1), jnp.concatenate(asked_all, axis=0))
    grad_queries = jnp.concatenate(grad_queries, axis=0).T
    return jnp.concatenate([grad_queries, grad_keys, grad_values], axis=1).astype(BF16)


def call(kernel, outs, *args, scratch=(), flops=0, name=None):
    size = sum(a.size * a.dtype.itemsize for a in args)
    size += sum(o.size * o.dtype.itemsize for o in outs)
    return pl.pallas_call(
        kernel,
        out_shape=outs,
        in_specs=[pl.BlockSpec(memory_space=pltpu.VMEM)] * len(args),
        out_specs=[pl.BlockSpec(memory_space=pltpu.VMEM)] * len(outs),
        scratch_shapes=list(scratch),
        compiler_params=pltpu.CompilerParams(vmem_limit_bytes=VMEM_BYTES),
        cost_estimate=pl.CostEstimate(flops=flops, bytes_accessed=size, transcendentals=0),
        name=name,
    )(*args)


def shape(dims, dtype=BF16):
    return jax.ShapeDtypeStruct(dims, dtype)


def route_kernel(peers, group_size, capacity, rot_ref, tok_ref, send_ref, pos_ref, slot_ref):
    row_count = tok_ref.shape[0]
    rotation = rot_ref[...]
    target = rotation // (row_count * group_size)
    position = rotation % row_count + 1
    high = (position // 256).astype(F32)
    low = (position % 256).astype(F32)
    step = 256
    earlier = onehot(iota((step, step), 0) < iota((step, step), 1))
    carry = jnp.zeros((peers, 1), F32)
    sums_high = jnp.zeros((peers, LANES), F32)
    sums_low = jnp.zeros((peers, LANES), F32)
    slots = []
    for start in range(0, row_count, step):
        part = slice(start, start + step)
        chosen = jnp.where(iota((peers, step), 0) == target[:, part], 1.0, 0.0)
        before = mm(chosen.astype(BF16), earlier) + carry
        carry = carry + jnp.sum(chosen, axis=1, keepdims=True)
        rank = jnp.sum(chosen * before, axis=0, keepdims=True)
        slots.append(target[:, part] * capacity + rank.astype(jnp.int32))
        place = onehot(iota((LANES, step), 0) == rank.astype(jnp.int32))
        sums_high = sums_high + mm_nt((chosen * high[:, part]).astype(BF16), place)
        sums_low = sums_low + mm_nt((chosen * low[:, part]).astype(BF16), place)
    pos_ref[...] = (sums_high * 256.0 + sums_low).astype(jnp.int32) - 1
    slot = jnp.concatenate(slots, axis=1)
    slot_ref[...] = slot
    tokens = tok_ref[...]
    for start in range(0, peers * capacity, step):
        pick = onehot(iota((step, row_count), 0) + start == slot)
        send_ref[start : start + step, :] = mm(pick, tokens).astype(BF16)


def arrived_row(pos_ref, capacity):
    peers = pos_ref.shape[0]
    slots = peers * capacity
    position = pos_ref[...] + 1
    high = (position // 256).astype(F32).astype(BF16)
    low = (position % 256).astype(F32).astype(BF16)
    place = onehot(iota((LANES, slots), 0) == iota((LANES, slots), 1) % capacity)
    spread = mm(high, place) * 256.0 + mm(low, place)
    own = iota((peers, slots), 0) == iota((peers, slots), 1) // capacity
    return jnp.sum(jnp.where(own, spread, 0.0), axis=0, keepdims=True).astype(jnp.int32) - 1


def first_local_kernel(head_size, tok_ref, wq_ref, cot_ref, down_ref, nrm_ref, pk_ref, heads_ref, act_ref):
    row_count = tok_ref.shape[0]
    weight = wq_ref[...]
    for start in range(0, row_count, BALL):
        rows = slice(start, start + BALL)
        residual = tok_ref[rows, :].astype(F32)
        normed = (residual * row_scale(residual)).astype(BF16)
        nrm_ref[rows, :] = normed
        packed = mm(normed, weight).astype(BF16)
        pk_ref[rows, :] = packed
        heads_ref[rows, :] = ball_attend(packed, head_size)
        act_ref[rows, :] = mm_nt(cot_ref[rows, :], down_ref[...]).astype(BF16)


def moved_kernel(head_size, capacity, got_ref, pos_ref, wq_ref, nrm_ref, pk_ref, row_ref, out_ref, heads_ref):
    row_count = nrm_ref.shape[0]
    slots = got_ref.shape[0]
    arrived = arrived_row(pos_ref, capacity)
    row_ref[...] = arrived
    weight = wq_ref[...]
    got = got_ref[...]
    for start in range(0, row_count, BALL):
        rows = slice(start, start + BALL)
        pick = onehot(iota((BALL, slots), 0) + start == arrived)
        residual = mm(pick, got)
        normed = (residual * row_scale(residual)).astype(BF16)
        nrm_ref[rows, :] = normed
        packed = mm(normed, weight).astype(BF16)
        pk_ref[rows, :] = packed
        heads_ref[rows, :] = ball_attend(packed, head_size)
    back_rows(arrived, heads_ref, out_ref)


def back_rows(arrived, rows_ref, out_ref):
    slots, step = out_ref.shape[0], 256
    row_count = rows_ref.shape[0]
    arrived_col = as_column(arrived.astype(F32)).astype(jnp.int32)
    moved = rows_ref[...]
    for start in range(0, slots, step):
        pick = onehot(iota((step, row_count), 1) == arrived_col[start : start + step])
        out_ref[start : start + step, :] = mm(pick, moved).astype(BF16)


def middle_kernel(
    tok_ref, local_ref, ret_ref, slot_ref, proj_ref, up_ref, cot_ref, act_ref,
    mix_ref, mid_ref, sn_ref, gated_ref, pre_ref, gm_ref, gl_ref, send_ref, gh_ref,
):
    row_count, width = tok_ref.shape
    half = width // 2
    slots = ret_ref.shape[0]
    chunks = up_ref.shape[0] // width
    slot = slot_ref[...]
    slot_col = as_column(slot.astype(F32)).astype(jnp.int32)
    rate = 0.7978845608028654
    cubic = 0.044715 * rate
    for start in range(0, row_count, BALL):
        rows = slice(start, start + BALL)
        pick = onehot(iota((BALL, slots), 1) == slot_col[rows])
        moved = mm(pick, ret_ref[...]).astype(BF16)
        mixed = jnp.concatenate([local_ref[rows, :], moved], axis=1)
        mix_ref[rows, :] = mixed
        middle = (tok_ref[rows, :].astype(F32) + mm(mixed, proj_ref[...])).astype(BF16)
        mid_ref[rows, :] = middle
        middle_f = middle.astype(F32)
        second_scale = row_scale(middle_f)
        normed = (middle_f * second_scale).astype(BF16)
        sn_ref[rows, :] = normed
        grad_second = jnp.zeros((BALL, width), F32)
        for chunk in range(chunks):
            columns = slice(chunk * width, (chunk + 1) * width)
            up = up_ref[columns, :]
            pre = mm(normed, up)
            square = pre * pre
            curve = jnp.tanh(pre * (rate + cubic * square))
            upper = 0.5 + 0.5 * curve
            gated_ref[rows, columns] = (pre * upper).astype(BF16)
            slope = upper + pre * (0.5 - 0.5 * (curve * curve)) * (rate + 3.0 * cubic * square)
            grad_pre = (act_ref[rows, columns].astype(F32) * slope).astype(BF16)
            pre_ref[rows, columns] = grad_pre
            grad_second = grad_second + mm_nt(grad_pre, up)
        grad_middle = (
            cot_ref[rows, :].astype(F32) + norm_back(middle_f, second_scale, grad_second)
        ).astype(BF16)
        gm_ref[rows, :] = grad_middle
        grad_heads = mm_nt(grad_middle, proj_ref[...]).astype(BF16)
        gl_ref[rows, :] = grad_heads[:, :half]
        gh_ref[rows, :] = grad_heads[:, half:]
    moved_grad = gh_ref[...]
    for start in range(0, slots, 256):
        pick = onehot(iota((256, row_count), 0) + start == slot)
        send_ref[start : start + 256, :] = mm(pick, moved_grad).astype(BF16)


def weights_kernel(mid_ref, gated_ref, down_ref, cot_ref, sn_ref, pre_ref, out_ref, gup_ref, gdown_ref):
    row_count = mid_ref.shape[0]
    for start in range(0, row_count, BALL):
        rows = slice(start, start + BALL)
        mixed = mm(gated_ref[rows, :], down_ref[...])
        out_ref[rows, :] = (mid_ref[rows, :].astype(F32) + mixed).astype(BF16)
    width = sn_ref.shape[1]
    normed_t = flip(sn_ref[...])
    cot_t = flip(cot_ref[...])
    for start in range(0, pre_ref.shape[1], width):
        columns = slice(start, start + width)
        gup_ref[columns, :] = mm(normed_t, pre_ref[:, columns]).astype(BF16)
        gdown_ref[columns, :] = mm(cot_t, gated_ref[:, columns]).astype(BF16)


def local_back_kernel(head_size, pk_ref, gl_ref, nrm_ref, wq_ref, mix_ref, gm_ref, first_ref, gq_ref, gp_ref, gpk_ref):
    row_count = pk_ref.shape[0]
    for start in range(0, row_count, BALL):
        rows = slice(start, start + BALL)
        grad_packed = ball_attend_back(pk_ref[rows, :], gl_ref[rows, :], head_size)
        gpk_ref[rows, :] = grad_packed
        first_ref[rows, :] = mm_nt(grad_packed, wq_ref[...])
    gq_ref[...] = mm(flip(nrm_ref[...]), gpk_ref[...]).astype(BF16)
    gp_ref[...] = mm(flip(mix_ref[...]), gm_ref[...]).astype(BF16)


def moved_back_kernel(head_size, got_ref, row_ref, pk_ref, wq_ref, gpk_ref, out_ref, first_ref):
    row_count = pk_ref.shape[0]
    slots = got_ref.shape[0]
    arrived = row_ref[...]
    for start in range(0, row_count, BALL):
        rows = slice(start, start + BALL)
        pick = onehot(iota((BALL, slots), 0) + start == arrived)
        grad_out = mm(pick, got_ref[...]).astype(BF16)
        grad_packed = ball_attend_back(pk_ref[rows, :], grad_out, head_size)
        gpk_ref[rows, :] = grad_packed
        first_ref[rows, :] = mm_nt(grad_packed, wq_ref[...]).astype(BF16)
    back_rows(arrived, first_ref, out_ref)


def moved_weights_kernel(nrm_ref, gpk_ref, gq_ref):
    gq_ref[...] = mm(flip(nrm_ref[...]), gpk_ref[...]).astype(BF16)


def last_kernel(tok_ref, gm_ref, first_ref, ret_ref, slot_ref, out_ref):
    row_count = tok_ref.shape[0]
    slots = ret_ref.shape[0]
    slot_col = as_column(slot_ref[...].astype(F32)).astype(jnp.int32)
    for start in range(0, row_count, BALL):
        rows = slice(start, start + BALL)
        pick = onehot(iota((BALL, slots), 1) == slot_col[rows])
        grad_first = first_ref[rows, :] + mm(pick, ret_ref[...])
        residual = tok_ref[rows, :].astype(F32)
        out_ref[rows, :] = (
            gm_ref[rows, :].astype(F32) + norm_back(residual, row_scale(residual), grad_first)
        ).astype(BF16)


def exchange(rows, peers):
    slots, columns = rows.shape
    sent = rows.reshape(peers, slots // peers, columns)
    got = lax.all_to_all(sent, "wide", split_axis=0, concat_axis=0, tiled=True)
    return got.reshape(slots, columns)


def bind(kernel, *fixed):
    def bound(*refs):
        kernel(*fixed, *refs)

    return bound


def body(tokens, rotation, qkv_weight, proj_weight, up_weight, down_weight, cotangent):
    rows, width = tokens.shape
    half = width // 2
    head_size = width // HEADS
    peers = lax.axis_size("wide")
    group_size = lax.axis_size("narrow")
    capacity = rows // peers + rows // peers // 2
    slots = peers * capacity
    hidden = group_size * up_weight.shape[1]
    unit = 2 * rows * width * width

    send, send_pos, slot = call(
        bind(route_kernel, peers, group_size, capacity),
        [shape((slots, width)), shape((peers, LANES), jnp.int32), shape((1, rows), jnp.int32)],
        rotation.reshape(1, rows), tokens, flops=3 * unit, name="route",
    )
    got_pos = exchange(send_pos, peers)
    got = exchange(send, peers)
    all_up = lax.all_gather(up_weight, "narrow", axis=0, tiled=True)
    all_down = lax.all_gather(down_weight, "narrow", axis=0, tiled=True)

    normed, packed, local_heads, grad_act = call(
        bind(first_local_kernel, head_size),
        [shape((rows, width)), shape((rows, 3 * half)), shape((rows, half)), shape((rows, hidden))],
        tokens, qkv_weight[:, : 3 * half], cotangent, all_down, flops=8 * unit, name="first_local",
    )
    moved_weight = qkv_weight[:, 3 * half :]
    moved_normed, moved_packed, arrived, outgoing = call(
        bind(moved_kernel, head_size, capacity),
        [shape((rows, width)), shape((rows, 3 * half)), shape((1, slots), jnp.int32), shape((slots, half))],
        got, got_pos, moved_weight,
        scratch=[pltpu.VMEM((rows, half), BF16)], flops=8 * unit, name="moved",
    )
    returned = exchange(outgoing, peers)
    mixed_heads, middle, second_normed, activated, grad_pre, grad_middle, grad_local, send_grad = call(
        middle_kernel,
        [
            shape((rows, width)), shape((rows, width)), shape((rows, width)),
            shape((rows, hidden)), shape((rows, hidden)),
            shape((rows, width)), shape((rows, half)), shape((slots, half)),
        ],
        tokens, local_heads, returned, slot, proj_weight, all_up, cotangent, grad_act,
        scratch=[pltpu.VMEM((rows, half), BF16)], flops=16 * unit, name="middle",
    )
    got_grad = exchange(send_grad, peers)
    output, grad_up, grad_down = call(
        weights_kernel,
        [shape((rows, width)), shape((hidden, width)), shape((hidden, width))],
        middle, activated, all_down, cotangent, second_normed, grad_pre,
        flops=12 * unit, name="mlp_weights",
    )
    first_local, qkv_local, proj_share = call(
        bind(local_back_kernel, head_size),
        [shape((rows, width), F32), shape((width, 3 * half)), shape((width, width))],
        packed, grad_local, normed, qkv_weight[:, : 3 * half], mixed_heads, grad_middle,
        scratch=[pltpu.VMEM((rows, 3 * half), BF16)], flops=12 * unit, name="local_back",
    )
    moved_grad_packed, grad_outgoing = call(
        bind(moved_back_kernel, head_size),
        [shape((rows, 3 * half)), shape((slots, width))],
        got_grad, arrived, moved_packed, moved_weight,
        scratch=[pltpu.VMEM((rows, width), BF16)], flops=12 * unit, name="moved_back",
    )
    grad_returned = exchange(grad_outgoing, peers)
    (qkv_moved,) = call(
        moved_weights_kernel, [shape((width, 3 * half))], moved_normed, moved_grad_packed,
        flops=2 * unit, name="moved_weights",
    )
    (grad_tokens,) = call(
        last_kernel, [shape((rows, width))],
        tokens, grad_middle, first_local, grad_returned, slot, flops=3 * unit, name="last",
    )

    up_part = lax.psum_scatter(grad_up, "narrow", scatter_dimension=0, tiled=True)
    down_part = lax.psum_scatter(grad_down, "narrow", scatter_dimension=0, tiled=True)
    up_sum, down_sum = lax.psum((up_part, down_part), "wide")
    qkv_sum, proj_sum, moved_sum = lax.psum((qkv_local, proj_share, qkv_moved), ("wide", "narrow"))
    grad_qkv = jnp.concatenate([qkv_sum, moved_sum], axis=1).astype(F32)
    return (
        output, grad_tokens, grad_qkv, proj_sum.astype(F32),
        up_sum.astype(F32), down_sum.astype(F32).T,
    )


def solution(mesh):
    return jax.shard_map(
        body,
        mesh=mesh,
        in_specs=(
            P(("wide", "narrow"), None),
            P(("wide", "narrow")),
            P(),
            P(),
            P(None, "narrow"),
            P("narrow", None),
            P(("wide", "narrow"), None),
        ),
        out_specs=(
            P(("wide", "narrow"), None),
            P(("wide", "narrow"), None),
            P(),
            P(),
            P(None, "narrow"),
            P("narrow", None),
        ),
        check_vma=False,
    )
```

```python
import jax
import jax.numpy as jnp
from jax import lax
from jax.experimental import pallas as pl
from jax.experimental.pallas import tpu as pltpu
from jax.sharding import Mesh
from jax.sharding import PartitionSpec as P

HEADS = 8
BALL = 256
EPSILON = 1e-06
LANES = 128
VMEM_BYTES = 60 * 1024 * 1024
SMALL_BYTES = 16 * 1024 * 1024

LONG = 10**11

F32 = jnp.float32
BF16 = jnp.bfloat16


def mm(left, right):
    return lax.dot_general(left, right, (((1,), (0,)), ((), ())), preferred_element_type=F32)


def mm_nt(left, right):
    return lax.dot_general(left, right, (((1,), (1,)), ((), ())), preferred_element_type=F32)


def mm_tn(left, right):
    return lax.dot_general(left, right, (((0,), (0,)), ((), ())), preferred_element_type=F32)


def iota(shape, dimension):
    return lax.broadcasted_iota(jnp.int32, shape, dimension)


def row_scale(values):
    return lax.rsqrt(jnp.mean(values * values, axis=-1, keepdims=True) + EPSILON)


def norm_back(values, scaling, gradient):
    unit = values * scaling
    return scaling * (gradient - unit * jnp.mean(gradient * unit, axis=-1, keepdims=True))


def flip(block):
    return block.astype(F32).T.astype(BF16)


def as_column(row):
    return jnp.broadcast_to(row, (8, row.shape[1])).T[:, :1]


def onehot(condition):
    return jnp.where(condition, 1.0, 0.0).astype(BF16)


def head_mask(columns, head, head_size, value):
    lane = iota((1, columns), 1)
    inside = (lane >= head * head_size) & (lane < (head + 1) * head_size)
    return jnp.where(inside, value, 0.0).astype(BF16)


def ball_weights(queries, key_rows, head, head_size):
    columns = queries.shape[1]
    asked = queries * head_mask(columns, head, head_size, head_size ** (-0.5))
    scores = mm_nt(key_rows, asked)
    raised = jnp.exp(scores - jnp.max(scores, axis=0, keepdims=True))
    return raised * (1.0 / jnp.sum(raised, axis=0, keepdims=True)), asked


def ball_attend(packed, head_size):
    columns = packed.shape[1] // 3
    queries, key_rows = packed[:, :columns], packed[:, columns : 2 * columns]
    values_t = flip(packed[:, 2 * columns :])
    parts = []
    for head in range(columns // head_size):
        weights, _ = ball_weights(queries, key_rows, head, head_size)
        own = values_t[head * head_size : (head + 1) * head_size]
        parts.append(mm(own, weights.astype(BF16)))
    return jnp.concatenate(parts, axis=0).T.astype(BF16)


def ball_attend_back(packed, grad_out, head_size):
    columns = packed.shape[1] // 3
    queries, key_rows = packed[:, :columns], packed[:, columns : 2 * columns]
    values = packed[:, 2 * columns :]
    keys_t = flip(key_rows * jnp.asarray(head_size ** (-0.5), BF16))
    asked_all, upstream_all, rounded_all, dscore_all, grad_queries = [], [], [], [], []
    for head in range(columns // head_size):
        weights, asked = ball_weights(queries, key_rows, head, head_size)
        upstream = grad_out * head_mask(columns, head, head_size, 1.0)
        dprob = mm_nt(values, upstream)
        dscore = weights * (dprob - jnp.sum(dprob * weights, axis=0, keepdims=True))
        dscore = dscore.astype(BF16)
        own = keys_t[head * head_size : (head + 1) * head_size]
        grad_queries.append(mm(own, dscore))
        asked_all.append(asked)
        upstream_all.append(upstream)
        rounded_all.append(weights.astype(BF16))
        dscore_all.append(dscore)
    grad_values = mm(
        jnp.concatenate(rounded_all, axis=1), jnp.concatenate(upstream_all, axis=0)
    )
    grad_keys = mm(jnp.concatenate(dscore_all, axis=1), jnp.concatenate(asked_all, axis=0))
    grad_queries = jnp.concatenate(grad_queries, axis=0).T
    return jnp.concatenate([grad_queries, grad_keys, grad_values], axis=1).astype(BF16)


def shape(dims, dtype=BF16):
    return jax.ShapeDtypeStruct(dims, dtype)


def by_row(columns, rows=BALL):
    return pl.BlockSpec((rows, columns), lambda step: (step, 0))


def by_column(rows, columns):
    return pl.BlockSpec((rows, columns), lambda step: (0, step))


def whole(rows, columns, row=0, column=0):
    return pl.BlockSpec((rows, columns), lambda step: (row, column))


FLAG = pl.BlockSpec(memory_space=pltpu.SMEM)
ANY = pl.BlockSpec(memory_space=pl.ANY)


def call(kernel, steps, ins, outs, scratch=(), flops=0, name=None, vmem=SMALL_BYTES):
    return pl.pallas_call(
        kernel,
        grid=(steps,),
        out_shape=[out for out, _ in outs],
        in_specs=[spec for _, spec in ins],
        out_specs=[spec for _, spec in outs],
        scratch_shapes=list(scratch),
        compiler_params=pltpu.CompilerParams(vmem_limit_bytes=vmem),
        cost_estimate=pl.CostEstimate(flops=flops, bytes_accessed=0, transcendentals=0),
        name=name,
    )(*[array for array, _ in ins])


def is_first():
    return pl.program_id(0) == 0


def is_last():
    return pl.program_id(0) == pl.num_programs(0) - 1


def route_kernel(peers, group_size, capacity, stride, rot_ref, tok_ref, send_ref, slot_ref, wide_ref, place_ref):
    row_count = tok_ref.shape[0]
    step = BALL

    @pl.when(is_first())
    def _():
        rotation = rot_ref[...]
        target = rotation // (row_count * group_size)
        position = rotation % row_count + 1
        high = (position // 256).astype(F32)
        low = (position % 256).astype(F32)
        earlier = onehot(iota((step, step), 0) < iota((step, step), 1))
        carry = jnp.zeros((peers, 1), F32)
        sums_high = jnp.zeros((peers, LANES), F32)
        sums_low = jnp.zeros((peers, LANES), F32)
        for start in range(0, row_count, step):
            part = slice(start, start + step)
            chosen = jnp.where(iota((peers, step), 0) == target[:, part], 1.0, 0.0)
            before = mm(chosen.astype(BF16), earlier) + carry
            carry = carry + jnp.sum(chosen, axis=1, keepdims=True)
            rank = jnp.sum(chosen * before, axis=0, keepdims=True).astype(jnp.int32)
            slot_ref[:, part] = target[:, part] * capacity + rank
            wide_ref[:, part] = target[:, part] * stride + rank
            place = onehot(iota((LANES, step), 0) == rank)
            sums_high = sums_high + mm_nt((chosen * high[:, part]).astype(BF16), place)
            sums_low = sums_low + mm_nt((chosen * low[:, part]).astype(BF16), place)
        place_ref[:, :LANES] = sums_high.astype(BF16)
        place_ref[:, LANES:] = sums_low.astype(BF16)

    base = pl.program_id(0) * step
    pick = onehot(iota((step, row_count), 0) + base == wide_ref[...])
    rows = mm(pick, tok_ref[...])
    told = onehot(iota((step, peers), 0) + base == iota((step, peers), 1) * stride + capacity)
    extra = mm(told, place_ref[...])
    send_ref[:, : 2 * LANES] = (rows[:, : 2 * LANES] + extra).astype(BF16)
    send_ref[:, 2 * LANES :] = rows[:, 2 * LANES :].astype(BF16)


def arrived_row(place, stride):
    peers = place.shape[0]
    slots = peers * stride
    column = iota((1, slots), 1)
    source = column // stride
    spot = onehot(iota((LANES, slots), 0) == column - source * stride)
    spread = mm(place[:, :LANES], spot) * 256.0 + mm(place[:, LANES:], spot)
    own = iota((peers, slots), 0) == source
    return jnp.sum(jnp.where(own, spread, 0.0), axis=0, keepdims=True).astype(jnp.int32) - 1


def back_rows(arrived, rows_ref, out_ref):
    slots, step = out_ref.shape[0], 256
    row_count = rows_ref.shape[0]
    arrived_col = as_column(arrived.astype(F32)).astype(jnp.int32)
    moved = rows_ref[...]
    for start in range(0, slots, step):
        pick = onehot(iota((step, row_count), 1) == arrived_col[start : start + step])
        out_ref[start : start + step, :] = mm(pick, moved).astype(BF16)


def first_local_kernel(head_size, tok_ref, wq_ref, nrm_ref, pk_ref, heads_ref):
    residual = tok_ref[...].astype(F32)
    normed = (residual * row_scale(residual)).astype(BF16)
    nrm_ref[...] = normed
    packed = mm(normed, wq_ref[...]).astype(BF16)
    pk_ref[...] = packed
    heads_ref[...] = ball_attend(packed, head_size)


def grad_act_kernel(cot_ref, down_ref, act_ref):
    act_ref[...] = mm_nt(cot_ref[...], down_ref[...]).astype(BF16)


def moved_kernel(
    head_size, peers, capacity, _, got_ref, wq_ref, nrm_ref, pk_ref, row_ref, out_ref, wide_ref, heads_ref
):
    slots = got_ref.shape[0]
    stride = slots // peers

    @pl.when(is_first())
    def _():
        told = onehot(iota((peers, slots), 1) == iota((peers, slots), 0) * stride + capacity)
        place = mm(told, got_ref[:, : 2 * LANES]).astype(BF16)
        wide_ref[...] = arrived_row(place, stride)
        row_ref[...] = arrived_row(place, capacity)

    base = pl.multiple_of(pl.program_id(0) * BALL, BALL)
    pick = onehot(iota((BALL, slots), 0) + base == wide_ref[...])
    residual = mm(pick, got_ref[...])
    normed = (residual * row_scale(residual)).astype(BF16)
    nrm_ref[...] = normed
    packed = mm(normed, wq_ref[...]).astype(BF16)
    pk_ref[...] = packed
    heads_ref[pl.ds(base, BALL), :] = ball_attend(packed, head_size)

    @pl.when(is_last())
    def _():
        back_rows(row_ref[...], heads_ref, out_ref)


def middle_kernel(
    tok_ref, local_ref, ret_ref, part_ref, slot_ref, proj_ref, up_ref, cot_ref, act_ref,
    mix_ref, mid_ref, sn_ref, gated_ref, pre_ref, gm_ref, gl_ref, send_ref, gh_ref,
):
    width = tok_ref.shape[1]
    half = width // 2
    slots = ret_ref.shape[0]
    chunks = up_ref.shape[0] // width
    rate = 0.7978845608028654
    cubic = 0.044715 * rate
    slot_col = as_column(part_ref[...].astype(F32)).astype(jnp.int32)
    pick = onehot(iota((BALL, slots), 1) == slot_col)
    moved = mm(pick, ret_ref[...]).astype(BF16)
    mixed = jnp.concatenate([local_ref[...], moved], axis=1)
    mix_ref[...] = mixed
    middle = (tok_ref[...].astype(F32) + mm(mixed, proj_ref[...])).astype(BF16)
    mid_ref[...] = middle
    middle_f = middle.astype(F32)
    second_scale = row_scale(middle_f)
    normed = (middle_f * second_scale).astype(BF16)
    sn_ref[...] = normed
    grad_second = jnp.zeros((BALL, width), F32)
    for chunk in range(chunks):
        columns = slice(chunk * width, (chunk + 1) * width)
        up = up_ref[columns, :]
        pre = mm(normed, up)
        square = pre * pre
        upper = 0.5 + 0.5 * jnp.tanh(pre * (rate + cubic * square))
        gated_ref[:, columns] = (pre * upper).astype(BF16)
        slope = upper * (1.0 + (1.0 - upper) * (pre * (2.0 * rate + 6.0 * cubic * square)))
        grad_pre = (act_ref[:, columns].astype(F32) * slope).astype(BF16)
        pre_ref[:, columns] = grad_pre
        grad_second = grad_second + mm_nt(grad_pre, up)
    grad_middle = (
        cot_ref[...].astype(F32) + norm_back(middle_f, second_scale, grad_second)
    ).astype(BF16)
    gm_ref[...] = grad_middle
    grad_heads = mm_nt(grad_middle, proj_ref[...]).astype(BF16)
    gl_ref[...] = grad_heads[:, :half]
    base = pl.multiple_of(pl.program_id(0) * BALL, BALL)
    gh_ref[pl.ds(base, BALL), :] = grad_heads[:, half:]

    @pl.when(is_last())
    def _():
        moved_grad = gh_ref[...]
        slot = slot_ref[...]
        for start in range(0, slots, BALL):
            pick = onehot(iota((BALL, slot.shape[1]), 0) + start == slot)
            send_ref[start : start + BALL, :] = mm(pick, moved_grad).astype(BF16)


def weights_kernel(
    mid_ref, gated_ref, down_ref, cot_ref, sn_ref, pre_ref,
    out_ref, both_ref, sn_t_ref, cot_t_ref, sum_ref,
):
    @pl.when(is_first())
    def _():
        sn_t_ref[...] = flip(sn_ref[...])
        cot_t_ref[...] = flip(cot_ref[...])
        sum_ref[...] = mid_ref[...].astype(F32)

    gated = gated_ref[...]
    both_ref[0] = mm(sn_t_ref[...], pre_ref[...]).astype(BF16)
    both_ref[1] = mm(cot_t_ref[...], gated).astype(BF16)
    sum_ref[...] += mm(gated, down_ref[...])

    @pl.when(is_last())
    def _():
        out_ref[...] = sum_ref[...].astype(BF16)


def local_back_kernel(
    head_size, pk_ref, gl_ref, nrm_ref, wq_ref, mix_ref, gm_ref,
    first_ref, gq_ref, gp_ref, gpk_ref,
):
    grad_packed = ball_attend_back(pk_ref[...], gl_ref[...], head_size)
    base = pl.multiple_of(pl.program_id(0) * BALL, BALL)
    gpk_ref[pl.ds(base, BALL), :] = grad_packed
    first_ref[...] = mm_nt(grad_packed, wq_ref[...])

    @pl.when(is_last())
    def _():
        gq_ref[...] = mm(flip(nrm_ref[...]), gpk_ref[...]).astype(BF16)
        gp_ref[...] = mm(flip(mix_ref[...]), gm_ref[...]).astype(BF16)


def moved_back_kernel(head_size, _, got_ref, row_ref, pk_ref, wq_ref, gpk_ref, out_ref, first_ref):
    slots = got_ref.shape[0]
    base = pl.multiple_of(pl.program_id(0) * BALL, BALL)
    pick = onehot(iota((BALL, slots), 0) + base == row_ref[...])
    grad_out = mm(pick, got_ref[...]).astype(BF16)
    grad_packed = ball_attend_back(pk_ref[...], grad_out, head_size)
    gpk_ref[...] = grad_packed
    first_ref[pl.ds(base, BALL), :] = mm_nt(grad_packed, wq_ref[...]).astype(BF16)

    @pl.when(is_last())
    def _():
        back_rows(row_ref[...], first_ref, out_ref)


def moved_weights_kernel(core_ref, nrm_ref, gpk_ref, gq_ref, gp_ref, keep_ref, send_ref, all_ref):
    width, third = gq_ref.shape
    all_ref[:, :third] = gq_ref[...]
    all_ref[:, third : 2 * third] = mm(flip(nrm_ref[...]), gpk_ref[...]).astype(BF16)
    all_ref[:, 2 * third :] = gp_ref[...]
    half = width // 2
    core = core_ref[0]
    for side, out_ref in ((core, keep_ref), (1 - core, send_ref)):
        rows = pl.ds(pl.multiple_of(side * half, half), half)
        for block in range(all_ref.shape[1] // width):
            out_ref[block * half : (block + 1) * half, :] = all_ref[rows, block * width : (block + 1) * width]


def add_split_kernel(count, after, spot_ref, *refs):
    ins, outs, sum_ref = refs[: -count - 1], refs[-count - 1 : -1], refs[-1]
    total = ins[0][...].astype(F32)
    for in_ref in ins[1:]:
        total = total + in_ref[...].astype(F32)
    sum_ref[...] = total.astype(BF16)
    size = sum_ref.shape[0] // count
    for shift, out_ref in enumerate(outs):
        start = lax.rem(spot_ref[0] + shift, count) * size
        out_ref[...] = sum_ref[pl.ds(pl.multiple_of(start, size), size), :]


def add_kernel(after, *refs):
    total = refs[0][...].astype(F32)
    for in_ref in refs[1:-1]:
        total = total + in_ref[...].astype(F32)
    refs[-1][...] = total.astype(BF16)


def spread_kernel(after, in_ref, out_ref):
    total = in_ref[0].astype(F32)
    for part in range(1, in_ref.shape[0]):
        total = total + in_ref[part].astype(F32)
    total = total.astype(BF16)
    for part in range(out_ref.shape[0]):
        out_ref[part] = total


def place_kernel(spot_ref, *refs):
    ins, out_ref = refs[:-1], refs[-1]
    count, size = len(ins), ins[0].shape[0]
    for shift, in_ref in enumerate(ins):
        start = lax.rem(spot_ref[0] + (count - shift), count) * size
        out_ref[pl.ds(pl.multiple_of(start, size), size), :] = in_ref[...]


def last_kernel(tok_ref, gm_ref, first_ref, ret_ref, part_ref, out_ref):
    slots = ret_ref.shape[0]
    slot_col = as_column(part_ref[...].astype(F32)).astype(jnp.int32)
    pick = onehot(iota((BALL, slots), 1) == slot_col)
    grad_first = first_ref[...] + mm(pick, ret_ref[...])
    residual = tok_ref[...].astype(F32)
    out_ref[...] = (
        gm_ref[...].astype(F32) + norm_back(residual, row_scale(residual), grad_first)
    ).astype(BF16)


def finish_mlp_kernel(core_ref, mine_ref, other_ref, up_ref, down_ref):
    core = core_ref[0]

    @pl.when(core == 0)
    def _():
        up_ref[...] = mine_ref[...].astype(F32)
        down_ref[...] = other_ref[...].astype(F32).T

    @pl.when(core != 0)
    def _():
        up_ref[...] = other_ref[...].astype(F32)
        down_ref[...] = mine_ref[...].astype(F32).T


def finish_attention_kernel(_, also, core_ref, mine_ref, other_ref, qkv_ref, proj_ref):
    core = core_ref[0]
    width = mine_ref.shape[1]
    half = mine_ref.shape[0] // 4
    for side, part_ref in ((core, mine_ref), (1 - core, other_ref)):
        rows = pl.ds(pl.multiple_of(side * half, half), half)
        for block in range(3):
            qkv_ref[rows, block * width : (block + 1) * width] = part_ref[block * half : (block + 1) * half, :].astype(F32)
        proj_ref[rows, :] = part_ref[3 * half :, :].astype(F32)


def exchange(rows, peers):
    slots, columns = rows.shape
    sent = rows.reshape(peers, slots // peers, columns)
    got = lax.all_to_all(sent, ("z", "x", "core"), split_axis=0, concat_axis=0, tiled=True)
    return got.reshape(slots, columns)


def swap_core(block):
    return lax.ppermute(block, "core", [(0, 1), (1, 0)])


def whole_array(array):
    return array, whole(*array.shape)


def spot_on(axis):
    return lax.axis_index(axis).astype(jnp.int32).reshape(1), FLAG


def shift_by(block, axis, shift):
    count = lax.axis_size(axis)
    return lax.ppermute(block, axis, [(place, (place + shift) % count) for place in range(count)])


def add_split(parts, axis, after):
    count = lax.axis_size(axis)
    rows, columns = parts[0].shape
    out = (shape((rows // count, columns)), whole(rows // count, columns))
    shares = call(
        bind(add_split_kernel, count), 1,
        [(after, ANY), spot_on(axis)] + [whole_array(part) for part in parts], [out] * count,
        scratch=[pltpu.VMEM((rows, columns), BF16)], name="add_split",
    )
    return [shares[0]] + [shift_by(shares[shift], axis, shift) for shift in range(1, count)]


def gather(block, axis):
    count = lax.axis_size(axis)
    rows, columns = block.shape
    parts = [block] + [shift_by(block, axis, shift) for shift in range(1, count)]
    (joined,) = call(
        place_kernel, 1, [spot_on(axis)] + [whole_array(part) for part in parts],
        [(shape((count * rows, columns)), whole(count * rows, columns))], name="gather",
    )
    return joined


def add(parts, after):
    (block,) = call(
        add_kernel, 1, [(after, ANY)] + [whole_array(part) for part in parts],
        [(shape(parts[0].shape), whole(*parts[0].shape))], name="add",
    )
    return block


def sum_by_steps(block, axes, after):
    parts = [block]
    for axis in axes:
        parts = add_split(parts, axis, after)
    share = block = add(parts, after)
    for axis in reversed(axes):
        block = gather(block, axis)
    return block, share


def sum_at_once(block, axes, after):
    count = lax.axis_size(axes)
    rows, columns = block.shape
    parts = block.reshape(count, rows // count, columns)
    parts = lax.all_to_all(parts, axes, split_axis=0, concat_axis=0, tiled=True)
    spread = (shape(parts.shape), pl.BlockSpec(parts.shape, lambda step: (0, 0, 0)))
    (spread,) = call(
        spread_kernel, 1, [(after, ANY), (parts, spread[1])], [spread], name="add_spread",
    )
    told = lax.all_to_all(spread, axes, split_axis=0, concat_axis=0, tiled=True)
    return told.reshape(rows, columns)


def bind(kernel, *fixed):
    def bound(*refs):
        kernel(*fixed, *refs)

    return bound


def body(tokens, rotation, qkv_weight, proj_weight, up_weight, down_weight, cotangent):
    rows, width = tokens.shape
    half = width // 2
    third = 3 * half
    head_size = width // HEADS
    peers = lax.axis_size(("z", "x", "core"))
    group_size = lax.axis_size("narrow")
    capacity = rows // peers + rows // peers // 2
    stride = capacity + 8
    slots = peers * capacity
    wide_slots = peers * stride
    hidden = group_size * up_weight.shape[1]
    balls = rows // BALL
    core = lax.axis_index("core")
    flag = (core.astype(jnp.int32).reshape(1), FLAG)
    own_weight = jnp.where(core == 0, up_weight, down_weight)
    all_weights = lax.all_gather(own_weight, ("core", "narrow"), axis=0, tiled=True)
    all_up = (all_weights, whole(hidden, width))

    send, slot = call(
        bind(route_kernel, peers, group_size, capacity, stride), wide_slots // BALL,
        [(rotation.reshape(1, rows), whole(1, rows)), (tokens, whole(rows, width))],
        [(shape((wide_slots, width)), by_row(width)), (shape((1, rows), jnp.int32), whole(1, rows))],
        scratch=[pltpu.VMEM((1, rows), jnp.int32), pltpu.VMEM((peers, 2 * LANES), BF16)],
        flops=LONG, name="route",
    )
    got = exchange(send, peers)
    part = (slot, by_column(1, BALL))

    normed, packed, local_heads = call(
        bind(first_local_kernel, head_size), balls,
        [(tokens, by_row(width)), (qkv_weight, whole(width, third))],
        [(shape((rows, width)), by_row(width)), (shape((rows, third)), by_row(third)), (shape((rows, half)), by_row(half))],
        name="first_local",
    )
    moved_weight = (qkv_weight, whole(width, third, 0, 1))
    moved_normed, moved_packed, arrived, outgoing = call(
        bind(moved_kernel, head_size, peers, capacity), balls,
        [(local_heads, ANY), (got, whole(wide_slots, width)), moved_weight],
        [
            (shape((rows, width)), by_row(width)), (shape((rows, third)), by_row(third)),
            (shape((1, slots), jnp.int32), whole(1, slots)), (shape((slots, half)), whole(slots, half)),
        ],
        scratch=[pltpu.VMEM((1, wide_slots), jnp.int32), pltpu.VMEM((rows, half), BF16)],
        flops=LONG, name="moved", vmem=VMEM_BYTES,
    )
    returned = exchange(outgoing, peers)
    (grad_act,) = call(
        grad_act_kernel, balls,
        [(cotangent, by_row(width)), (all_weights, whole(hidden, width, 1))],
        [(shape((rows, hidden)), by_row(hidden))],
        name="grad_act",
    )
    mixed_heads, middle, second_normed, activated, grad_pre, grad_middle, grad_local, send_grad = call(
        middle_kernel, balls,
        [
            (tokens, by_row(width)), (local_heads, by_row(half)), (returned, whole(slots, half)),
            part, (slot, whole(1, rows)), (proj_weight, whole(width, width)), all_up,
            (cotangent, by_row(width)), (grad_act, by_row(hidden)),
        ],
        [
            (shape((rows, width)), by_row(width)), (shape((rows, width)), by_row(width)),
            (shape((rows, width)), by_row(width)), (shape((rows, hidden)), by_row(hidden)),
            (shape((rows, hidden)), by_row(hidden)), (shape((rows, width)), by_row(width)),
            (shape((rows, half)), by_row(half)), (shape((slots, half)), whole(slots, half)),
        ],
        scratch=[pltpu.VMEM((rows, half), BF16)], flops=LONG, name="middle", vmem=VMEM_BYTES,
    )
    got_grad = exchange(send_grad, peers)
    output, mlp_both = call(
        weights_kernel, group_size,
        [
            (middle, whole(rows, width)), (activated, by_column(rows, width)),
            (all_weights, pl.BlockSpec((width, width), lambda step: (group_size + step, 0))),
            (cotangent, whole(rows, width)), (second_normed, whole(rows, width)),
            (grad_pre, by_column(rows, width)),
        ],
        [
            (shape((rows, width)), whole(rows, width)),
            (shape((2, hidden, width)), pl.BlockSpec((2, width, width), lambda step: (0, step, 0))),
        ],
        scratch=[pltpu.VMEM((width, rows), BF16), pltpu.VMEM((width, rows), BF16), pltpu.VMEM((rows, width), F32)],
        name="mlp_weights", vmem=VMEM_BYTES,
    )
    first_local, qkv_local, proj_local = call(
        bind(local_back_kernel, head_size), balls,
        [
            (packed, by_row(third)), (grad_local, by_row(half)), (normed, whole(rows, width)),
            (qkv_weight, whole(width, third)), (mixed_heads, whole(rows, width)), (grad_middle, whole(rows, width)),
        ],
        [
            (shape((rows, width), F32), by_row(width)),
            (shape((width, third)), whole(width, third)), (shape((width, width)), whole(width, width)),
        ],
        scratch=[pltpu.VMEM((rows, third), BF16)],
        name="local_back", vmem=VMEM_BYTES,
    )
    moved_grad_packed, grad_outgoing = call(
        bind(moved_back_kernel, head_size), balls,
        [(output, ANY), (got_grad, whole(slots, half)), (arrived, whole(1, slots)), (moved_packed, by_row(third)), moved_weight],
        [(shape((rows, third)), by_row(third)), (shape((slots, width)), whole(slots, width))],
        scratch=[pltpu.VMEM((rows, width), BF16)], flops=LONG, name="moved_back", vmem=VMEM_BYTES,
    )
    grad_returned = exchange(grad_outgoing, peers)
    stacked = (shape((2 * width, width)), whole(2 * width, width))
    keep, send = call(
        moved_weights_kernel, 1,
        [flag, whole_array(moved_normed), whole_array(moved_grad_packed), whole_array(qkv_local), whole_array(proj_local)],
        [stacked, stacked],
        scratch=[pltpu.VMEM((width, 2 * third + width), BF16)], name="moved_weights",
    )
    (grad_tokens,) = call(
        last_kernel, balls,
        [(tokens, by_row(width)), (grad_middle, by_row(width)), (first_local, by_row(width)), (grad_returned, whole(slots, width)), part],
        [(shape((rows, width)), by_row(width))],
        flops=LONG, name="last",
    )

    mlp_part = lax.psum_scatter(
        mlp_both.reshape(2 * hidden, width), ("core", "narrow"), scatter_dimension=0, tiled=True
    )
    pair = add([keep, swap_core(send)], grad_returned)
    mlp_mine, mlp_share = sum_by_steps(mlp_part, ("x", "z"), pair)
    mlp_other = swap_core(mlp_mine)
    grad_up, grad_down = call(
        finish_mlp_kernel, 1, [flag, whole_array(mlp_mine), whole_array(mlp_other)],
        [(shape((width, width), F32), whole(width, width)), (shape((width, width), F32), whole(width, width))],
        name="finish_mlp",
    )
    mine = sum_at_once(pair, ("narrow", "x", "z"), mlp_share)
    grad_qkv, grad_proj = call(
        finish_attention_kernel, 1, [(grad_tokens, ANY), (grad_up, ANY), flag, whole_array(mine), whole_array(swap_core(mine))],
        [(shape((width, 2 * third), F32), whole(width, 2 * third)), (shape((width, width), F32), whole(width, width))],
        name="finish_attention",
    )
    return output, grad_tokens, grad_qkv, grad_proj, grad_up, grad_down


def solution(mesh):
    wide, narrow = mesh.devices.shape
    axes = ("z", "x", "core", "narrow")
    mesh = Mesh(mesh.devices.reshape(wide // 8, 4, 2, narrow), axes)
    rows = axes
    return jax.shard_map(
        body,
        mesh=mesh,
        in_specs=(
            P(rows, None),
            P(rows),
            P(),
            P(),
            P(None, "narrow"),
            P("narrow", None),
            P(rows, None),
        ),
        out_specs=(
            P(rows, None),
            P(rows, None),
            P(),
            P(),
            P(None, "narrow"),
            P("narrow", None),
        ),
        check_vma=False,
    )
```

```python
import jax
import jax.numpy as jnp
from jax import lax
from jax.experimental import pallas as pl
from jax.experimental.pallas import tpu as pltpu
from jax.sharding import Mesh
from jax.sharding import PartitionSpec as P

HEADS = 8
BALL = 256
EPSILON = 1e-06
LANES = 128
VMEM_BYTES = 60 * 1024 * 1024
SMALL_BYTES = 16 * 1024 * 1024

LONG = 10**11

F32 = jnp.float32
BF16 = jnp.bfloat16


def mm(left, right):
    return lax.dot_general(left, right, (((1,), (0,)), ((), ())), preferred_element_type=F32)


def mm_nt(left, right):
    return lax.dot_general(left, right, (((1,), (1,)), ((), ())), preferred_element_type=F32)


def mm_tn(left, right):
    return lax.dot_general(left, right, (((0,), (0,)), ((), ())), preferred_element_type=F32)


def iota(shape, dimension):
    return lax.broadcasted_iota(jnp.int32, shape, dimension)


def row_scale(values):
    return lax.rsqrt(jnp.mean(values * values, axis=-1, keepdims=True) + EPSILON)


def norm_back(values, scaling, gradient):
    unit = values * scaling
    return scaling * (gradient - unit * jnp.mean(gradient * unit, axis=-1, keepdims=True))


def flip(block):
    return block.astype(F32).T.astype(BF16)


def as_column(row):
    return jnp.broadcast_to(row, (8, row.shape[1])).T[:, :1]


def onehot(condition):
    return jnp.where(condition, 1.0, 0.0).astype(BF16)


def head_mask(columns, head, head_size, value):
    lane = iota((1, columns), 1)
    inside = (lane >= head * head_size) & (lane < (head + 1) * head_size)
    return jnp.where(inside, value, 0.0).astype(BF16)


def by_head(rows, head_size, value):
    columns = rows.shape[1]
    heads = [rows * head_mask(columns, head, head_size, value) for head in range(columns // head_size)]
    return jnp.concatenate(heads, axis=0)


def ball_weights(key_rows, asked):
    scores = mm_nt(key_rows, asked)
    raised = jnp.exp(scores - jnp.max(scores, axis=0, keepdims=True))
    return raised * (1.0 / jnp.sum(raised, axis=0, keepdims=True))


def ball_attend(packed, head_size):
    columns = packed.shape[1] // 3
    queries, key_rows = packed[:, :columns], packed[:, columns : 2 * columns]
    rounded = ball_weights(key_rows, by_head(queries, head_size, head_size ** (-0.5))).astype(BF16)
    return per_head(flip(packed[:, 2 * columns :]), rounded, head_size).astype(BF16)


def per_head(rows_t, weights, head_size):
    columns, count = rows_t.shape
    parts = [
        mm(rows_t[head * head_size : (head + 1) * head_size], weights[:, head * count : (head + 1) * count])
        for head in range(columns // head_size)
    ]
    return jnp.concatenate(parts, axis=0).T


def ball_attend_back(packed, grad_out, head_size):
    columns = packed.shape[1] // 3
    queries, key_rows = packed[:, :columns], packed[:, columns : 2 * columns]
    asked = by_head(queries, head_size, head_size ** (-0.5))
    upstream = by_head(grad_out, head_size, 1.0)
    weights = ball_weights(key_rows, asked)
    dprob = mm_nt(packed[:, 2 * columns :], upstream)
    dscore = weights * (dprob - jnp.sum(dprob * weights, axis=0, keepdims=True))
    dscore = dscore.astype(BF16)
    grad_values = mm(weights.astype(BF16), upstream)
    grad_keys = mm(dscore, asked)
    grad_queries = per_head(flip(key_rows * jnp.asarray(head_size ** (-0.5), BF16)), dscore, head_size)
    return jnp.concatenate([grad_queries, grad_keys, grad_values], axis=1).astype(BF16)


def shape(dims, dtype=BF16):
    return jax.ShapeDtypeStruct(dims, dtype)


def by_row(columns, rows=BALL):
    return pl.BlockSpec((rows, columns), lambda step: (step, 0))


def by_column(rows, columns):
    return pl.BlockSpec((rows, columns), lambda step: (0, step))


def whole(rows, columns, row=0, column=0):
    return pl.BlockSpec((rows, columns), lambda step: (row, column))


FLAG = pl.BlockSpec(memory_space=pltpu.SMEM)
ANY = pl.BlockSpec(memory_space=pl.ANY)


def call(kernel, steps, ins, outs, scratch=(), flops=0, name=None, vmem=SMALL_BYTES):
    return pl.pallas_call(
        kernel,
        grid=(steps,),
        out_shape=[out for out, _ in outs],
        in_specs=[spec for _, spec in ins],
        out_specs=[spec for _, spec in outs],
        scratch_shapes=list(scratch),
        compiler_params=pltpu.CompilerParams(vmem_limit_bytes=vmem),
        cost_estimate=pl.CostEstimate(flops=flops, bytes_accessed=0, transcendentals=0),
        name=name,
    )(*[array for array, _ in ins])


def is_first():
    return pl.program_id(0) == 0


def is_last():
    return pl.program_id(0) == pl.num_programs(0) - 1


def route_kernel(peers, group_size, capacity, stride, rot_ref, tok_ref, send_ref, slot_ref, wide_ref, place_ref):
    row_count = tok_ref.shape[0]
    step = BALL

    @pl.when(is_first())
    def _():
        rotation = rot_ref[...]
        target = rotation // (row_count * group_size)
        position = rotation % row_count + 1
        high = (position // 256).astype(F32)
        low = (position % 256).astype(F32)
        earlier = onehot(iota((step, step), 0) < iota((step, step), 1))
        carry = jnp.zeros((peers, 1), F32)
        sums_high = jnp.zeros((peers, LANES), F32)
        sums_low = jnp.zeros((peers, LANES), F32)
        for start in range(0, row_count, step):
            part = slice(start, start + step)
            chosen = jnp.where(iota((peers, step), 0) == target[:, part], 1.0, 0.0)
            before = mm(chosen.astype(BF16), earlier) + carry
            carry = carry + jnp.sum(chosen, axis=1, keepdims=True)
            rank = jnp.sum(chosen * before, axis=0, keepdims=True).astype(jnp.int32)
            slot_ref[:, part] = target[:, part] * capacity + rank
            wide_ref[:, part] = target[:, part] * stride + rank
            place = onehot(iota((LANES, step), 0) == rank)
            sums_high = sums_high + mm_nt((chosen * high[:, part]).astype(BF16), place)
            sums_low = sums_low + mm_nt((chosen * low[:, part]).astype(BF16), place)
        place_ref[:, :LANES] = sums_high.astype(BF16)
        place_ref[:, LANES:] = sums_low.astype(BF16)

    base = pl.program_id(0) * step
    pick = onehot(iota((step, row_count), 0) + base == wide_ref[...])
    rows = mm(pick, tok_ref[...])
    told = onehot(iota((step, peers), 0) + base == iota((step, peers), 1) * stride + capacity)
    extra = mm(told, place_ref[...])
    send_ref[:, : 2 * LANES] = (rows[:, : 2 * LANES] + extra).astype(BF16)
    send_ref[:, 2 * LANES :] = rows[:, 2 * LANES :].astype(BF16)


def arrived_row(place, stride):
    peers = place.shape[0]
    slots = peers * stride
    column = iota((1, slots), 1)
    source = column // stride
    spot = onehot(iota((LANES, slots), 0) == column - source * stride)
    spread = mm(place[:, :LANES], spot) * 256.0 + mm(place[:, LANES:], spot)
    own = iota((peers, slots), 0) == source
    return jnp.sum(jnp.where(own, spread, 0.0), axis=0, keepdims=True).astype(jnp.int32) - 1


def back_rows(arrived, rows_ref, out_ref):
    slots, step = out_ref.shape[0], 256
    row_count = rows_ref.shape[0]
    arrived_col = as_column(arrived.astype(F32)).astype(jnp.int32)
    moved = rows_ref[...]
    for start in range(0, slots, step):
        pick = onehot(iota((step, row_count), 1) == arrived_col[start : start + step])
        out_ref[start : start + step, :] = mm(pick, moved).astype(BF16)


def first_local_kernel(head_size, tok_ref, wq_ref, nrm_ref, pk_ref, heads_ref):
    residual = tok_ref[...].astype(F32)
    normed = (residual * row_scale(residual)).astype(BF16)
    nrm_ref[...] = normed
    packed = mm(normed, wq_ref[...]).astype(BF16)
    pk_ref[...] = packed
    heads_ref[...] = ball_attend(packed, head_size)


def grad_act_kernel(cot_ref, down_ref, act_ref):
    act_ref[...] = mm_nt(cot_ref[...], down_ref[...]).astype(BF16)


def moved_kernel(
    head_size, peers, capacity, _, got_ref, wq_ref, nrm_ref, pk_ref, row_ref, out_ref, wide_ref, heads_ref
):
    slots = got_ref.shape[0]
    stride = slots // peers

    @pl.when(is_first())
    def _():
        told = onehot(iota((peers, slots), 1) == iota((peers, slots), 0) * stride + capacity)
        place = mm(told, got_ref[:, : 2 * LANES]).astype(BF16)
        wide_ref[...] = arrived_row(place, stride)
        row_ref[...] = arrived_row(place, capacity)

    base = pl.multiple_of(pl.program_id(0) * BALL, BALL)
    pick = onehot(iota((BALL, slots), 0) + base == wide_ref[...])
    residual = mm(pick, got_ref[...])
    normed = (residual * row_scale(residual)).astype(BF16)
    nrm_ref[...] = normed
    packed = mm(normed, wq_ref[...]).astype(BF16)
    pk_ref[...] = packed
    heads_ref[pl.ds(base, BALL), :] = ball_attend(packed, head_size)

    @pl.when(is_last())
    def _():
        back_rows(row_ref[...], heads_ref, out_ref)


def middle_kernel(
    tok_ref, local_ref, ret_ref, part_ref, slot_ref, proj_ref, up_ref, cot_ref, act_ref,
    mix_ref, mid_ref, sn_ref, gated_ref, pre_ref, gm_ref, gl_ref, send_ref, gh_ref,
):
    width = tok_ref.shape[1]
    half = width // 2
    slots = ret_ref.shape[0]
    chunks = up_ref.shape[0] // width
    rate = 0.7978845608028654
    cubic = 0.044715 * rate
    slot_col = as_column(part_ref[...].astype(F32)).astype(jnp.int32)
    pick = onehot(iota((BALL, slots), 1) == slot_col)
    moved = mm(pick, ret_ref[...]).astype(BF16)
    mixed = jnp.concatenate([local_ref[...], moved], axis=1)
    mix_ref[...] = mixed
    middle = (tok_ref[...].astype(F32) + mm(mixed, proj_ref[...])).astype(BF16)
    mid_ref[...] = middle
    middle_f = middle.astype(F32)
    second_scale = row_scale(middle_f)
    normed = (middle_f * second_scale).astype(BF16)
    sn_ref[...] = normed
    grad_second = jnp.zeros((BALL, width), F32)
    pres = [mm(normed, up_ref[chunk * width : (chunk + 1) * width, :]) for chunk in range(chunks)]
    for chunk, pre in enumerate(pres):
        columns = slice(chunk * width, (chunk + 1) * width)
        square = pre * pre
        upper = 0.5 + 0.5 * jnp.tanh(pre * (rate + cubic * square))
        gated_ref[:, columns] = (pre * upper).astype(BF16)
        slope = upper * (1.0 + (1.0 - upper) * (pre * (2.0 * rate + 6.0 * cubic * square)))
        grad_pre = (act_ref[:, columns].astype(F32) * slope).astype(BF16)
        pre_ref[:, columns] = grad_pre
        grad_second = grad_second + mm_nt(grad_pre, up_ref[columns, :])
    grad_middle = (
        cot_ref[...].astype(F32) + norm_back(middle_f, second_scale, grad_second)
    ).astype(BF16)
    gm_ref[...] = grad_middle
    grad_heads = mm_nt(grad_middle, proj_ref[...]).astype(BF16)
    gl_ref[...] = grad_heads[:, :half]
    base = pl.multiple_of(pl.program_id(0) * BALL, BALL)
    gh_ref[pl.ds(base, BALL), :] = grad_heads[:, half:]

    @pl.when(is_last())
    def _():
        moved_grad = gh_ref[...]
        slot = slot_ref[...]
        for start in range(0, slots, BALL):
            pick = onehot(iota((BALL, slot.shape[1]), 0) + start == slot)
            send_ref[start : start + BALL, :] = mm(pick, moved_grad).astype(BF16)


def weights_kernel(
    mid_ref, gated_ref, down_ref, cot_ref, sn_ref, pre_ref,
    out_ref, both_ref, sn_t_ref, cot_t_ref, sum_ref,
):
    @pl.when(is_first())
    def _():
        sn_t_ref[...] = flip(sn_ref[...])
        cot_t_ref[...] = flip(cot_ref[...])
        sum_ref[...] = mid_ref[...].astype(F32)

    gated = gated_ref[...]
    both_ref[0] = mm(sn_t_ref[...], pre_ref[...]).astype(BF16)
    both_ref[1] = mm(cot_t_ref[...], gated).astype(BF16)
    sum_ref[...] += mm(gated, down_ref[...])

    @pl.when(is_last())
    def _():
        out_ref[...] = sum_ref[...].astype(BF16)


def local_back_kernel(
    head_size, pk_ref, gl_ref, nrm_ref, wq_ref, mix_ref, gm_ref,
    first_ref, gq_ref, gp_ref, gpk_ref,
):
    grad_packed = ball_attend_back(pk_ref[...], gl_ref[...], head_size)
    base = pl.multiple_of(pl.program_id(0) * BALL, BALL)
    gpk_ref[pl.ds(base, BALL), :] = grad_packed
    first_ref[...] = mm_nt(grad_packed, wq_ref[...])

    @pl.when(is_last())
    def _():
        gq_ref[...] = mm(flip(nrm_ref[...]), gpk_ref[...]).astype(BF16)
        gp_ref[...] = mm(flip(mix_ref[...]), gm_ref[...]).astype(BF16)


def moved_back_kernel(head_size, _, got_ref, row_ref, pk_ref, wq_ref, gpk_ref, out_ref, first_ref):
    slots = got_ref.shape[0]
    base = pl.multiple_of(pl.program_id(0) * BALL, BALL)
    pick = onehot(iota((BALL, slots), 0) + base == row_ref[...])
    grad_out = mm(pick, got_ref[...]).astype(BF16)
    grad_packed = ball_attend_back(pk_ref[...], grad_out, head_size)
    gpk_ref[...] = grad_packed
    first_ref[pl.ds(base, BALL), :] = mm_nt(grad_packed, wq_ref[...]).astype(BF16)

    @pl.when(is_last())
    def _():
        back_rows(row_ref[...], first_ref, out_ref)


def moved_weights_kernel(core_ref, nrm_ref, gpk_ref, gq_ref, gp_ref, keep_ref, send_ref, all_ref):
    width, third = gq_ref.shape
    all_ref[:, :third] = gq_ref[...]
    all_ref[:, third : 2 * third] = mm(flip(nrm_ref[...]), gpk_ref[...]).astype(BF16)
    all_ref[:, 2 * third :] = gp_ref[...]
    half = width // 2
    core = core_ref[0]
    for side, out_ref in ((core, keep_ref), (1 - core, send_ref)):
        rows = pl.ds(pl.multiple_of(side * half, half), half)
        for block in range(all_ref.shape[1] // width):
            out_ref[block * half : (block + 1) * half, :] = all_ref[rows, block * width : (block + 1) * width]


def add_split_kernel(count, after, spot_ref, *refs):
    ins, outs, sum_ref = refs[: -count - 1], refs[-count - 1 : -1], refs[-1]
    total = ins[0][...].astype(F32)
    for in_ref in ins[1:]:
        total = total + in_ref[...].astype(F32)
    sum_ref[...] = total.astype(BF16)
    size = sum_ref.shape[0] // count
    for shift, out_ref in enumerate(outs):
        start = lax.rem(spot_ref[0] + shift, count) * size
        out_ref[...] = sum_ref[pl.ds(pl.multiple_of(start, size), size), :]


def add_kernel(after, *refs):
    total = refs[0][...].astype(F32)
    for in_ref in refs[1:-1]:
        total = total + in_ref[...].astype(F32)
    refs[-1][...] = total.astype(BF16)


def add_parts(in_ref):
    total = in_ref[0].astype(F32)
    for part in range(1, in_ref.shape[0]):
        total = total + in_ref[part].astype(F32)
    return total.astype(BF16)


def spread_kernel(after, also, in_ref, out_ref):
    total = add_parts(in_ref)
    for part in range(out_ref.shape[0]):
        out_ref[part] = total


def place_kernel(spot_ref, *refs):
    ins, out_ref = refs[:-1], refs[-1]
    count, size = len(ins), ins[0].shape[0]
    for shift, in_ref in enumerate(ins):
        start = lax.rem(spot_ref[0] + (count - shift), count) * size
        out_ref[pl.ds(pl.multiple_of(start, size), size), :] = in_ref[...]


def last_kernel(_, tok_ref, gm_ref, first_ref, ret_ref, part_ref, out_ref):
    slots = ret_ref.shape[0]
    slot_col = as_column(part_ref[...].astype(F32)).astype(jnp.int32)
    pick = onehot(iota((BALL, slots), 1) == slot_col)
    grad_first = first_ref[...] + mm(pick, ret_ref[...])
    residual = tok_ref[...].astype(F32)
    out_ref[...] = (
        gm_ref[...].astype(F32) + norm_back(residual, row_scale(residual), grad_first)
    ).astype(BF16)


def finish_mlp_kernel(core_ref, mine_ref, other_ref, up_ref, down_ref):
    core = core_ref[0]

    @pl.when(core == 0)
    def _():
        up_ref[...] = mine_ref[...].astype(F32)
        down_ref[...] = other_ref[...].astype(F32).T

    @pl.when(core != 0)
    def _():
        up_ref[...] = other_ref[...].astype(F32)
        down_ref[...] = mine_ref[...].astype(F32).T


def finish_attention_kernel(core_ref, mine_ref, other_ref, qkv_ref, proj_ref):
    core = core_ref[0]
    width = mine_ref.shape[1]
    half = mine_ref.shape[0] // 4
    for side, part_ref in ((core, mine_ref), (1 - core, other_ref)):
        rows = pl.ds(pl.multiple_of(side * half, half), half)
        for block in range(3):
            qkv_ref[rows, block * width : (block + 1) * width] = part_ref[block * half : (block + 1) * half, :].astype(F32)
        proj_ref[rows, :] = part_ref[3 * half :, :].astype(F32)


def exchange(rows, peers):
    slots, columns = rows.shape
    sent = rows.reshape(peers, slots // peers, columns)
    got = lax.all_to_all(sent, ("z", "x", "core"), split_axis=0, concat_axis=0, tiled=True)
    return got.reshape(slots, columns)


def swap_core(block):
    return lax.ppermute(block, "core", [(0, 1), (1, 0)])


def whole_array(array):
    return array, whole(*array.shape)


def spot_on(axis):
    return lax.axis_index(axis).astype(jnp.int32).reshape(1), FLAG


def shift_by(block, axis, shift):
    count = lax.axis_size(axis)
    return lax.ppermute(block, axis, [(place, (place + shift) % count) for place in range(count)])


def add_split(parts, axis, after):
    count = lax.axis_size(axis)
    rows, columns = parts[0].shape
    out = (shape((rows // count, columns)), whole(rows // count, columns))
    shares = call(
        bind(add_split_kernel, count), 1,
        [(after, ANY), spot_on(axis)] + [whole_array(part) for part in parts], [out] * count,
        scratch=[pltpu.VMEM((rows, columns), BF16)], name="add_split",
    )
    return [shares[0]] + [shift_by(shares[shift], axis, shift) for shift in range(1, count)]


def gather(block, axis):
    count = lax.axis_size(axis)
    rows, columns = block.shape
    parts = [block] + [shift_by(block, axis, shift) for shift in range(1, count)]
    (joined,) = call(
        place_kernel, 1, [spot_on(axis)] + [whole_array(part) for part in parts],
        [(shape((count * rows, columns)), whole(count * rows, columns))], name="gather",
    )
    return joined


def add(parts, after):
    (block,) = call(
        add_kernel, 1, [(after, ANY)] + [whole_array(part) for part in parts],
        [(shape(parts[0].shape), whole(*parts[0].shape))], name="add",
    )
    return block


def share_of_sum(block, axes):
    count = lax.axis_size(axes)
    rows, columns = block.shape
    parts = block.reshape(count, rows // count, columns)
    return lax.all_to_all(parts, axes, split_axis=0, concat_axis=0, tiled=True)


def whole_parts(parts):
    return parts, pl.BlockSpec(parts.shape, lambda step: (0, 0, 0))


def sum_by_steps(block, axes, after):
    parts = [block]
    for axis in axes:
        parts = add_split(parts, axis, after)
    halfway = parts[0]
    block = add(parts, after)
    for axis in reversed(axes):
        block = gather(block, axis)
    return block, halfway


def sum_at_once(block, axes, after, also):
    parts = share_of_sum(block, axes)
    (spread,) = call(
        spread_kernel, 1, [(after, ANY), (also, ANY), whole_parts(parts)], [(shape(parts.shape), whole_parts(parts)[1])], name="add_spread",
    )
    told = lax.all_to_all(spread, axes, split_axis=0, concat_axis=0, tiled=True)
    return told.reshape(block.shape)


def bind(kernel, *fixed):
    def bound(*refs):
        kernel(*fixed, *refs)

    return bound


def body(tokens, rotation, qkv_weight, proj_weight, up_weight, down_weight, cotangent):
    rows, width = tokens.shape
    half = width // 2
    third = 3 * half
    head_size = width // HEADS
    peers = lax.axis_size(("z", "x", "core"))
    group_size = lax.axis_size("narrow")
    capacity = rows // peers + rows // peers // 2
    stride = capacity + 8
    slots = peers * capacity
    wide_slots = peers * stride
    hidden = group_size * up_weight.shape[1]
    balls = rows // BALL
    core = lax.axis_index("core")
    flag = (core.astype(jnp.int32).reshape(1), FLAG)
    own_weight = jnp.where(core == 0, up_weight, down_weight)
    all_weights = lax.all_gather(own_weight, ("core", "narrow"), axis=0, tiled=True)
    all_up = (all_weights, whole(hidden, width))

    send, slot = call(
        bind(route_kernel, peers, group_size, capacity, stride), wide_slots // BALL,
        [(rotation.reshape(1, rows), whole(1, rows)), (tokens, whole(rows, width))],
        [(shape((wide_slots, width)), by_row(width)), (shape((1, rows), jnp.int32), whole(1, rows))],
        scratch=[pltpu.VMEM((1, rows), jnp.int32), pltpu.VMEM((peers, 2 * LANES), BF16)],
        flops=LONG, name="route",
    )
    got = exchange(send, peers)
    part = (slot, by_column(1, BALL))

    normed, packed, local_heads = call(
        bind(first_local_kernel, head_size), balls,
        [(tokens, by_row(width)), (qkv_weight, whole(width, third))],
        [(shape((rows, width)), by_row(width)), (shape((rows, third)), by_row(third)), (shape((rows, half)), by_row(half))],
        name="first_local",
    )
    moved_weight = (qkv_weight, whole(width, third, 0, 1))
    moved_normed, moved_packed, arrived, outgoing = call(
        bind(moved_kernel, head_size, peers, capacity), balls,
        [(local_heads, ANY), (got, whole(wide_slots, width)), moved_weight],
        [
            (shape((rows, width)), by_row(width)), (shape((rows, third)), by_row(third)),
            (shape((1, slots), jnp.int32), whole(1, slots)), (shape((slots, half)), whole(slots, half)),
        ],
        scratch=[pltpu.VMEM((1, wide_slots), jnp.int32), pltpu.VMEM((rows, half), BF16)],
        flops=LONG, name="moved", vmem=VMEM_BYTES,
    )
    returned = exchange(outgoing, peers)
    (grad_act,) = call(
        grad_act_kernel, balls,
        [(cotangent, by_row(width)), (all_weights, whole(hidden, width, 1))],
        [(shape((rows, hidden)), by_row(hidden))],
        name="grad_act",
    )
    mixed_heads, middle, second_normed, activated, grad_pre, grad_middle, grad_local, send_grad = call(
        middle_kernel, balls,
        [
            (tokens, by_row(width)), (local_heads, by_row(half)), (returned, whole(slots, half)),
            part, (slot, whole(1, rows)), (proj_weight, whole(width, width)), all_up,
            (cotangent, by_row(width)), (grad_act, by_row(hidden)),
        ],
        [
            (shape((rows, width)), by_row(width)), (shape((rows, width)), by_row(width)),
            (shape((rows, width)), by_row(width)), (shape((rows, hidden)), by_row(hidden)),
            (shape((rows, hidden)), by_row(hidden)), (shape((rows, width)), by_row(width)),
            (shape((rows, half)), by_row(half)), (shape((slots, half)), whole(slots, half)),
        ],
        scratch=[pltpu.VMEM((rows, half), BF16)], flops=LONG, name="middle", vmem=VMEM_BYTES,
    )
    got_grad = exchange(send_grad, peers)
    output, mlp_both = call(
        weights_kernel, group_size,
        [
            (middle, whole(rows, width)), (activated, by_column(rows, width)),
            (all_weights, pl.BlockSpec((width, width), lambda step: (group_size + step, 0))),
            (cotangent, whole(rows, width)), (second_normed, whole(rows, width)),
            (grad_pre, by_column(rows, width)),
        ],
        [
            (shape((rows, width)), whole(rows, width)),
            (shape((2, hidden, width)), pl.BlockSpec((2, width, width), lambda step: (0, step, 0))),
        ],
        scratch=[pltpu.VMEM((width, rows), BF16), pltpu.VMEM((width, rows), BF16), pltpu.VMEM((rows, width), F32)],
        name="mlp_weights", vmem=VMEM_BYTES,
    )
    mlp_part = lax.psum_scatter(
        mlp_both.reshape(2 * hidden, width), ("core", "narrow"), scatter_dimension=0, tiled=True
    )
    first_local, qkv_local, proj_local = call(
        bind(local_back_kernel, head_size), balls,
        [
            (packed, by_row(third)), (grad_local, by_row(half)), (normed, whole(rows, width)),
            (qkv_weight, whole(width, third)), (mixed_heads, whole(rows, width)), (grad_middle, whole(rows, width)),
        ],
        [
            (shape((rows, width), F32), by_row(width)),
            (shape((width, third)), whole(width, third)), (shape((width, width)), whole(width, width)),
        ],
        scratch=[pltpu.VMEM((rows, third), BF16)],
        name="local_back", vmem=VMEM_BYTES,
    )
    moved_grad_packed, grad_outgoing = call(
        bind(moved_back_kernel, head_size), balls,
        [(output, ANY), (got_grad, whole(slots, half)), (arrived, whole(1, slots)), (moved_packed, by_row(third)), moved_weight],
        [(shape((rows, third)), by_row(third)), (shape((slots, width)), whole(slots, width))],
        scratch=[pltpu.VMEM((rows, width), BF16)], flops=LONG, name="moved_back", vmem=VMEM_BYTES,
    )
    grad_returned = exchange(grad_outgoing, peers)
    stacked = (shape((2 * width, width)), whole(2 * width, width))
    keep, send = call(
        moved_weights_kernel, 1,
        [flag, whole_array(moved_normed), whole_array(moved_grad_packed), whole_array(qkv_local), whole_array(proj_local)],
        [stacked, stacked],
        scratch=[pltpu.VMEM((width, 2 * third + width), BF16)], name="moved_weights",
    )
    (grad_tokens,) = call(
        last_kernel, balls,
        [(mlp_part, ANY), (tokens, by_row(width)), (grad_middle, by_row(width)), (first_local, by_row(width)), (grad_returned, whole(slots, width)), part],
        [(shape((rows, width)), by_row(width))],
        flops=LONG, name="last",
    )

    pair = add([keep, swap_core(send)], grad_returned)
    mlp_mine, halfway = sum_by_steps(mlp_part, ("x", "z"), pair)
    mlp_other = swap_core(mlp_mine)
    grad_up, grad_down = call(
        finish_mlp_kernel, 1, [flag, whole_array(mlp_mine), whole_array(mlp_other)],
        [(shape((width, width), F32), whole(width, width)), (shape((width, width), F32), whole(width, width))],
        name="finish_mlp",
    )
    mine = add([sum_at_once(pair, ("narrow", "x", "z"), grad_tokens, halfway)], mlp_mine)
    grad_qkv, grad_proj = call(
        finish_attention_kernel, 1, [flag, whole_array(mine), whole_array(swap_core(mine))],
        [(shape((width, 2 * third), F32), whole(width, 2 * third)), (shape((width, width), F32), whole(width, width))],
        name="finish_attention",
    )
    return output, grad_tokens, grad_qkv, grad_proj, grad_up, grad_down


def solution(mesh):
    wide, narrow = mesh.devices.shape
    axes = ("z", "x", "core", "narrow")
    mesh = Mesh(mesh.devices.reshape(wide // 8, 4, 2, narrow), axes)
    rows = axes
    return jax.shard_map(
        body,
        mesh=mesh,
        in_specs=(
            P(rows, None),
            P(rows),
            P(),
            P(),
            P(None, "narrow"),
            P("narrow", None),
            P(rows, None),
        ),
        out_specs=(
            P(rows, None),
            P(rows, None),
            P(),
            P(),
            P(None, "narrow"),
            P("narrow", None),
        ),
        check_vma=False,
    )
```

```python
import jax
import jax.numpy as jnp
from jax import lax
from jax.experimental import pallas as pl
from jax.experimental.pallas import tpu as pltpu
from jax.sharding import Mesh
from jax.sharding import PartitionSpec as P

HEADS = 8
BALL = 256
EPSILON = 1e-06
LANES = 128
VMEM_BYTES = 60 * 1024 * 1024
SMALL_BYTES = 16 * 1024 * 1024

LONG = 10**11

F32 = jnp.float32
BF16 = jnp.bfloat16


def mm(left, right):
    return lax.dot_general(left, right, (((1,), (0,)), ((), ())), preferred_element_type=F32)


def mm_nt(left, right):
    return lax.dot_general(left, right, (((1,), (1,)), ((), ())), preferred_element_type=F32)


def mm_tn(left, right):
    return lax.dot_general(left, right, (((0,), (0,)), ((), ())), preferred_element_type=F32)


def iota(shape, dimension):
    return lax.broadcasted_iota(jnp.int32, shape, dimension)


def row_scale(values):
    return lax.rsqrt(jnp.mean(values * values, axis=-1, keepdims=True) + EPSILON)


def norm_back(values, scaling, gradient):
    unit = values * scaling
    return scaling * (gradient - unit * jnp.mean(gradient * unit, axis=-1, keepdims=True))


def flip(block):
    return block.astype(F32).T.astype(BF16)


def as_column(row):
    return jnp.broadcast_to(row, (8, row.shape[1])).T[:, :1]


def onehot(condition):
    return jnp.where(condition, 1.0, 0.0).astype(BF16)


def head_mask(columns, head, head_size, value):
    lane = iota((1, columns), 1)
    inside = (lane >= head * head_size) & (lane < (head + 1) * head_size)
    return jnp.where(inside, value, 0.0).astype(BF16)


def by_head(rows, head_size, value):
    columns = rows.shape[1]
    heads = [rows * head_mask(columns, head, head_size, value) for head in range(columns // head_size)]
    return jnp.concatenate(heads, axis=0)


def ball_weights(key_rows, asked):
    scores = mm_nt(key_rows, asked)
    raised = jnp.exp(scores - jnp.max(scores, axis=0, keepdims=True))
    return raised * (1.0 / jnp.sum(raised, axis=0, keepdims=True))


def ball_attend(packed, head_size):
    columns = packed.shape[1] // 3
    queries, key_rows = packed[:, :columns], packed[:, columns : 2 * columns]
    rounded = ball_weights(key_rows, by_head(queries, head_size, head_size ** (-0.5))).astype(BF16)
    return per_head(flip(packed[:, 2 * columns :]), rounded, head_size).astype(BF16)


def per_head(rows_t, weights, head_size):
    columns, count = rows_t.shape
    parts = [
        mm(rows_t[head * head_size : (head + 1) * head_size], weights[:, head * count : (head + 1) * count])
        for head in range(columns // head_size)
    ]
    return jnp.concatenate(parts, axis=0).T


def ball_attend_back(packed, grad_out, head_size):
    columns = packed.shape[1] // 3
    queries, key_rows = packed[:, :columns], packed[:, columns : 2 * columns]
    asked = by_head(queries, head_size, head_size ** (-0.5))
    upstream = by_head(grad_out, head_size, 1.0)
    weights = ball_weights(key_rows, asked)
    dprob = mm_nt(packed[:, 2 * columns :], upstream)
    dscore = weights * (dprob - jnp.sum(dprob * weights, axis=0, keepdims=True))
    dscore = dscore.astype(BF16)
    grad_values = mm(weights.astype(BF16), upstream)
    grad_keys = mm(dscore, asked)
    grad_queries = per_head(flip(key_rows * jnp.asarray(head_size ** (-0.5), BF16)), dscore, head_size)
    return jnp.concatenate([grad_queries, grad_keys, grad_values], axis=1).astype(BF16)


def shape(dims, dtype=BF16):
    return jax.ShapeDtypeStruct(dims, dtype)


def by_row(columns, rows=BALL):
    return pl.BlockSpec((rows, columns), lambda step: (step, 0))


def by_column(rows, columns):
    return pl.BlockSpec((rows, columns), lambda step: (0, step))


def whole(rows, columns, row=0, column=0):
    return pl.BlockSpec((rows, columns), lambda step: (row, column))


FLAG = pl.BlockSpec(memory_space=pltpu.SMEM)
ANY = pl.BlockSpec(memory_space=pl.ANY)


def call(kernel, steps, ins, outs, scratch=(), flops=0, name=None, vmem=SMALL_BYTES):
    return pl.pallas_call(
        kernel,
        grid=(steps,),
        out_shape=[out for out, _ in outs],
        in_specs=[spec for _, spec in ins],
        out_specs=[spec for _, spec in outs],
        scratch_shapes=list(scratch),
        compiler_params=pltpu.CompilerParams(vmem_limit_bytes=vmem),
        cost_estimate=pl.CostEstimate(flops=flops, bytes_accessed=0, transcendentals=0),
        name=name,
    )(*[array for array, _ in ins])


def is_first():
    return pl.program_id(0) == 0


def is_last():
    return pl.program_id(0) == pl.num_programs(0) - 1


def late(columns, rows):
    return [pltpu.VMEM((rows, columns), BF16), pltpu.SemaphoreType.DMA(())]


def fetch(source, kept_ref, sem):
    copy = pltpu.make_async_copy(source, kept_ref, sem)

    @pl.when(is_first())
    def _():
        copy.start()

    def arrive():
        @pl.when(is_first())
        def _():
            copy.wait()

    return arrive


def route_kernel(
    peers, group_size, capacity, stride, rot_ref, all_ref, send_ref, slot_ref, wide_ref, place_ref, tok_ref, sem
):
    row_count = tok_ref.shape[0]
    step = BALL
    arrive = fetch(all_ref, tok_ref, sem)
    block = send_ref.shape[0]

    @pl.when(is_first())
    def _():
        rotation = rot_ref[...]
        target = rotation // (row_count * group_size)
        position = rotation % row_count + 1
        high = (position // 256).astype(F32)
        low = (position % 256).astype(F32)
        earlier = onehot(iota((step, step), 0) < iota((step, step), 1))
        carry = jnp.zeros((peers, 1), F32)
        sums_high = jnp.zeros((peers, LANES), F32)
        sums_low = jnp.zeros((peers, LANES), F32)
        for start in range(0, row_count, step):
            part = slice(start, start + step)
            chosen = jnp.where(iota((peers, step), 0) == target[:, part], 1.0, 0.0)
            before = mm(chosen.astype(BF16), earlier) + carry
            carry = carry + jnp.sum(chosen, axis=1, keepdims=True)
            rank = jnp.sum(chosen * before, axis=0, keepdims=True).astype(jnp.int32)
            slot_ref[:, part] = target[:, part] * capacity + rank
            wide_ref[:, part] = target[:, part] * stride + rank
            place = onehot(iota((LANES, step), 0) == rank)
            sums_high = sums_high + mm_nt((chosen * high[:, part]).astype(BF16), place)
            sums_low = sums_low + mm_nt((chosen * low[:, part]).astype(BF16), place)
        place_ref[:, :LANES] = sums_high.astype(BF16)
        place_ref[:, LANES:] = sums_low.astype(BF16)

    arrive()
    base = pl.program_id(0) * block
    pick = onehot(iota((block, row_count), 0) + base == wide_ref[...])
    rows = mm(pick, tok_ref[...])
    told = onehot(iota((block, peers), 0) + base == iota((block, peers), 1) * stride + capacity)
    extra = mm(told, place_ref[...])
    send_ref[:, : 2 * LANES] = (rows[:, : 2 * LANES] + extra).astype(BF16)
    send_ref[:, 2 * LANES :] = rows[:, 2 * LANES :].astype(BF16)


def arrived_row(place, stride):
    peers = place.shape[0]
    slots = peers * stride
    column = iota((1, slots), 1)
    source = column // stride
    spot = onehot(iota((LANES, slots), 0) == column - source * stride)
    spread = mm(place[:, :LANES], spot) * 256.0 + mm(place[:, LANES:], spot)
    own = iota((peers, slots), 0) == source
    return jnp.sum(jnp.where(own, spread, 0.0), axis=0, keepdims=True).astype(jnp.int32) - 1


def back_rows(arrived, rows_ref, out_ref):
    slots, step = out_ref.shape[0], 2 * BALL
    row_count = rows_ref.shape[0]
    arrived_col = as_column(arrived.astype(F32)).astype(jnp.int32)
    moved = rows_ref[...]
    for start in range(0, slots, step):
        pick = onehot(iota((step, row_count), 1) == arrived_col[start : start + step])
        out_ref[start : start + step, :] = mm(pick, moved).astype(BF16)


def first_local_kernel(head_size, tok_ref, wq_ref, nrm_ref, pk_ref, heads_ref):
    residual = tok_ref[...].astype(F32)
    normed = (residual * row_scale(residual)).astype(BF16)
    nrm_ref[...] = normed
    packed = mm(normed, wq_ref[...]).astype(BF16)
    pk_ref[...] = packed
    heads_ref[...] = ball_attend(packed, head_size)


def grad_act_kernel(cot_ref, down_ref, act_ref):
    act_ref[...] = mm_nt(cot_ref[...], down_ref[...]).astype(BF16)


def moved_kernel(
    head_size, peers, capacity, _, got_ref, wq_ref, nrm_ref, pk_ref, row_ref, out_ref,
    heads_ref, all_nrm_ref, all_pk_ref,
):
    slots = got_ref.shape[0]
    row_count = heads_ref.shape[0]
    stride = slots // peers

    @pl.when(is_first())
    def _():
        told = onehot(iota((peers, slots), 1) == iota((peers, slots), 0) * stride + capacity)
        place = mm(told, got_ref[:, : 2 * LANES]).astype(BF16)
        row_ref[...] = arrived_row(place, capacity)
        pick = onehot(iota((row_count, slots), 0) == arrived_row(place, stride))
        residual = mm(pick, got_ref[...])
        normed = (residual * row_scale(residual)).astype(BF16)
        all_nrm_ref[...] = normed
        all_pk_ref[...] = mm(normed, wq_ref[...]).astype(BF16)

    rows = pl.ds(pl.multiple_of(pl.program_id(0) * BALL, BALL), BALL)
    nrm_ref[...] = all_nrm_ref[rows, :]
    packed = all_pk_ref[rows, :]
    pk_ref[...] = packed
    heads_ref[rows, :] = ball_attend(packed, head_size)

    @pl.when(is_last())
    def _():
        back_rows(row_ref[...], heads_ref, out_ref)


def middle_kernel(
    tok_ref, local_ref, ret_ref, part_ref, slot_ref, proj_ref, up_ref, cot_ref, act_ref,
    mix_ref, mid_ref, sn_ref, gated_ref, pre_ref, gm_ref, gl_ref, send_ref, gh_ref,
):
    count, width = tok_ref.shape
    half = width // 2
    slots = ret_ref.shape[0]
    chunks = up_ref.shape[0] // width
    rate = 0.7978845608028654
    cubic = 0.044715 * rate
    slot_col = as_column(part_ref[...].astype(F32)).astype(jnp.int32)
    pick = onehot(iota((count, slots), 1) == slot_col)
    moved = mm(pick, ret_ref[...]).astype(BF16)
    mixed = jnp.concatenate([local_ref[...], moved], axis=1)
    mix_ref[...] = mixed
    middle = (tok_ref[...].astype(F32) + mm(mixed, proj_ref[...])).astype(BF16)
    mid_ref[...] = middle
    middle_f = middle.astype(F32)
    second_scale = row_scale(middle_f)
    normed = (middle_f * second_scale).astype(BF16)
    sn_ref[...] = normed
    grad_second = jnp.zeros((count, width), F32)
    pres = [mm(normed, up_ref[chunk * width : (chunk + 1) * width, :]) for chunk in range(chunks)]
    for chunk, pre in enumerate(pres):
        columns = slice(chunk * width, (chunk + 1) * width)
        square = pre * pre
        upper = 0.5 + 0.5 * jnp.tanh(pre * (rate + cubic * square))
        gated_ref[:, columns] = (pre * upper).astype(BF16)
        slope = upper * (1.0 + (1.0 - upper) * (pre * (2.0 * rate + 6.0 * cubic * square)))
        grad_pre = (act_ref[:, columns].astype(F32) * slope).astype(BF16)
        pre_ref[:, columns] = grad_pre
        grad_second = grad_second + mm_nt(grad_pre, up_ref[columns, :])
    grad_middle = (
        cot_ref[...].astype(F32) + norm_back(middle_f, second_scale, grad_second)
    ).astype(BF16)
    gm_ref[...] = grad_middle
    grad_heads = mm_nt(grad_middle, proj_ref[...]).astype(BF16)
    gl_ref[...] = grad_heads[:, :half]
    base = pl.multiple_of(pl.program_id(0) * count, count)
    gh_ref[pl.ds(base, count), :] = grad_heads[:, half:]

    @pl.when(is_last())
    def _():
        moved_grad = gh_ref[...]
        slot = slot_ref[...]
        step = 2 * BALL
        for start in range(0, slots, step):
            pick = onehot(iota((step, slot.shape[1]), 0) + start == slot)
            send_ref[start : start + step, :] = mm(pick, moved_grad).astype(BF16)


def weights_kernel(
    mid_ref, gated_ref, down_ref, cot_ref, sn_ref, pre_ref,
    out_ref, both_ref, sn_t_ref, cot_t_ref, sum_ref,
):
    @pl.when(is_first())
    def _():
        sn_t_ref[...] = flip(sn_ref[...])
        cot_t_ref[...] = flip(cot_ref[...])
        sum_ref[...] = mid_ref[...].astype(F32)

    gated = gated_ref[...]
    both_ref[0] = mm(sn_t_ref[...], pre_ref[...]).astype(BF16)
    both_ref[1] = mm(cot_t_ref[...], gated).astype(BF16)
    sum_ref[...] += mm(gated, down_ref[...])

    @pl.when(is_last())
    def _():
        out_ref[...] = sum_ref[...].astype(BF16)


def local_back_kernel(
    head_size, pk_ref, gl_ref, nrm_ref, wq_ref, mix_ref, gm_ref,
    first_ref, gq_ref, gp_ref, gpk_ref,
):
    grad_packed = ball_attend_back(pk_ref[...], gl_ref[...], head_size)
    base = pl.multiple_of(pl.program_id(0) * BALL, BALL)
    gpk_ref[pl.ds(base, BALL), :] = grad_packed
    first_ref[...] = mm_nt(grad_packed, wq_ref[...])

    @pl.when(is_last())
    def _():
        gq_ref[...] = mm(flip(nrm_ref[...]), gpk_ref[...]).astype(BF16)
        gp_ref[...] = mm(flip(mix_ref[...]), gm_ref[...]).astype(BF16)


def moved_back_kernel(
    head_size, _, got_ref, row_ref, pk_ref, wq_ref, gpk_ref, out_ref, first_ref, grad_ref, all_gpk_ref
):
    slots = got_ref.shape[0]

    @pl.when(is_first())
    def _():
        pick = onehot(iota((grad_ref.shape[0], slots), 0) == row_ref[...])
        grad_ref[...] = mm(pick, got_ref[...]).astype(BF16)

    rows = pl.ds(pl.multiple_of(pl.program_id(0) * BALL, BALL), BALL)
    grad_packed = ball_attend_back(pk_ref[...], grad_ref[rows, :], head_size)
    gpk_ref[...] = grad_packed
    all_gpk_ref[rows, :] = grad_packed

    @pl.when(is_last())
    def _():
        first_ref[...] = mm_nt(all_gpk_ref[...], wq_ref[...]).astype(BF16)
        back_rows(row_ref[...], first_ref, out_ref)


def moved_weights_kernel(core_ref, nrm_ref, gpk_ref, gq_ref, gp_ref, keep_ref, send_ref, all_ref):
    width, third = gq_ref.shape
    all_ref[:, :third] = gq_ref[...]
    all_ref[:, third : 2 * third] = mm(flip(nrm_ref[...]), gpk_ref[...]).astype(BF16)
    all_ref[:, 2 * third :] = gp_ref[...]
    half = width // 2
    core = core_ref[0]
    for side, out_ref in ((core, keep_ref), (1 - core, send_ref)):
        rows = pl.ds(pl.multiple_of(side * half, half), half)
        for block in range(all_ref.shape[1] // width):
            out_ref[block * half : (block + 1) * half, :] = all_ref[rows, block * width : (block + 1) * width]


def add_split_kernel(count, after, spot_ref, *refs):
    ins, outs, sum_ref = refs[: -count - 1], refs[-count - 1 : -1], refs[-1]
    total = ins[0][...].astype(F32)
    for in_ref in ins[1:]:
        total = total + in_ref[...].astype(F32)
    sum_ref[...] = total.astype(BF16)
    size = sum_ref.shape[0] // count
    for shift, out_ref in enumerate(outs):
        start = lax.rem(spot_ref[0] + shift, count) * size
        out_ref[...] = sum_ref[pl.ds(pl.multiple_of(start, size), size), :]


def add_kernel(after, also, *refs):
    total = refs[0][...].astype(F32)
    for in_ref in refs[1:-1]:
        total = total + in_ref[...].astype(F32)
    refs[-1][...] = total.astype(BF16)


def add_parts(in_ref):
    total = in_ref[0].astype(F32)
    for part in range(1, in_ref.shape[0]):
        total = total + in_ref[part].astype(F32)
    return total.astype(BF16)


def spread_kernel(after, in_ref, out_ref):
    total = add_parts(in_ref)
    for part in range(out_ref.shape[0]):
        out_ref[part] = total


def place_kernel(spot_ref, *refs):
    ins, out_ref = refs[:-1], refs[-1]
    count, size = len(ins), ins[0].shape[0]
    for shift, in_ref in enumerate(ins):
        start = lax.rem(spot_ref[0] + (count - shift), count) * size
        out_ref[pl.ds(pl.multiple_of(start, size), size), :] = in_ref[...]


def last_kernel(_, tok_ref, gm_ref, first_ref, ret_ref, part_ref, out_ref):
    slots = ret_ref.shape[0]
    slot_col = as_column(part_ref[...].astype(F32)).astype(jnp.int32)
    pick = onehot(iota((BALL, slots), 1) == slot_col)
    grad_first = first_ref[...] + mm(pick, ret_ref[...])
    residual = tok_ref[...].astype(F32)
    out_ref[...] = (
        gm_ref[...].astype(F32) + norm_back(residual, row_scale(residual), grad_first)
    ).astype(BF16)


def finish_mlp_kernel(core_ref, mine_ref, other_ref, up_ref, down_ref):
    core = core_ref[0]

    @pl.when(core == 0)
    def _():
        up_ref[...] = mine_ref[...].astype(F32)
        down_ref[...] = other_ref[...].astype(F32).T

    @pl.when(core != 0)
    def _():
        up_ref[...] = other_ref[...].astype(F32)
        down_ref[...] = mine_ref[...].astype(F32).T


def finish_attention_kernel(core_ref, mine_ref, other_ref, qkv_ref, proj_ref):
    core = core_ref[0]
    width = mine_ref.shape[1]
    half = mine_ref.shape[0] // 4
    for side, part_ref in ((core, mine_ref), (1 - core, other_ref)):
        rows = pl.ds(pl.multiple_of(side * half, half), half)
        for block in range(3):
            qkv_ref[rows, block * width : (block + 1) * width] = part_ref[block * half : (block + 1) * half, :].astype(F32)
        proj_ref[rows, :] = part_ref[3 * half :, :].astype(F32)


def exchange(rows, peers):
    slots, columns = rows.shape
    sent = rows.reshape(peers, slots // peers, columns)
    got = lax.all_to_all(sent, ("z", "x", "core"), split_axis=0, concat_axis=0, tiled=True)
    return got.reshape(slots, columns)


def swap_core(block):
    return lax.ppermute(block, "core", [(0, 1), (1, 0)])


def whole_array(array):
    return array, whole(*array.shape)


def spot_on(axis):
    return lax.axis_index(axis).astype(jnp.int32).reshape(1), FLAG


def shift_by(block, axis, shift):
    count = lax.axis_size(axis)
    return lax.ppermute(block, axis, [(place, (place + shift) % count) for place in range(count)])


def add_split(parts, axis, after):
    count = lax.axis_size(axis)
    rows, columns = parts[0].shape
    out = (shape((rows // count, columns)), whole(rows // count, columns))
    shares = call(
        bind(add_split_kernel, count), 1,
        [(after, ANY), spot_on(axis)] + [whole_array(part) for part in parts], [out] * count,
        scratch=[pltpu.VMEM((rows, columns), BF16)], name="add_split",
    )
    return [shares[0]] + [shift_by(shares[shift], axis, shift) for shift in range(1, count)]


def gather(block, axis):
    count = lax.axis_size(axis)
    rows, columns = block.shape
    parts = [block] + [shift_by(block, axis, shift) for shift in range(1, count)]
    (joined,) = call(
        place_kernel, 1, [spot_on(axis)] + [whole_array(part) for part in parts],
        [(shape((count * rows, columns)), whole(count * rows, columns))], name="gather",
    )
    return joined


def add(parts, after, also=None):
    also = after if also is None else also
    (block,) = call(
        add_kernel, 1, [(after, ANY), (also, ANY)] + [whole_array(part) for part in parts],
        [(shape(parts[0].shape), whole(*parts[0].shape))], name="add",
    )
    return block


def share_of_sum(block, axes):
    count = lax.axis_size(axes)
    rows, columns = block.shape
    parts = block.reshape(count, rows // count, columns)
    return lax.all_to_all(parts, axes, split_axis=0, concat_axis=0, tiled=True)


def whole_parts(parts):
    return parts, pl.BlockSpec(parts.shape, lambda step: (0, 0, 0))


def sum_by_steps(block, axes, after):
    parts = [block]
    for axis in axes:
        parts = add_split(parts, axis, after)
    halfway = parts[0]
    block = add(parts, after)
    for axis in reversed(axes):
        block = gather(block, axis)
    return block, halfway


def sum_at_once(block, axes, after):
    parts = share_of_sum(block, axes)
    (spread,) = call(
        spread_kernel, 1, [(after, ANY), whole_parts(parts)], [(shape(parts.shape), whole_parts(parts)[1])], name="add_spread",
    )
    told = lax.all_to_all(spread, axes, split_axis=0, concat_axis=0, tiled=True)
    return told.reshape(block.shape)


def bind(kernel, *fixed):
    def bound(*refs):
        kernel(*fixed, *refs)

    return bound


def body(tokens, rotation, qkv_weight, proj_weight, up_weight, down_weight, cotangent):
    rows, width = tokens.shape
    half = width // 2
    third = 3 * half
    head_size = width // HEADS
    peers = lax.axis_size(("z", "x", "core"))
    group_size = lax.axis_size("narrow")
    capacity = rows // peers + rows // peers // 2
    stride = capacity + 8
    slots = peers * capacity
    wide_slots = peers * stride
    hidden = group_size * up_weight.shape[1]
    balls = rows // BALL
    block = 2 * BALL
    core = lax.axis_index("core")
    flag = (core.astype(jnp.int32).reshape(1), FLAG)
    own_weight = jnp.where(core == 0, up_weight, down_weight)
    all_weights = lax.all_gather(own_weight, ("core", "narrow"), axis=0, tiled=True)
    all_up = (all_weights, whole(hidden, width))

    send, slot = call(
        bind(route_kernel, peers, group_size, capacity, stride), 2,
        [(rotation.reshape(1, rows), whole(1, rows)), (tokens, ANY)],
        [(shape((wide_slots, width)), by_row(width, wide_slots // 2)), (shape((1, rows), jnp.int32), whole(1, rows))],
        scratch=[pltpu.VMEM((1, rows), jnp.int32), pltpu.VMEM((peers, 2 * LANES), BF16)] + late(width, rows),
        flops=LONG, name="route", vmem=VMEM_BYTES,
    )
    got = exchange(send, peers)
    part = (slot, by_column(1, BALL))

    normed, packed, local_heads = call(
        bind(first_local_kernel, head_size), balls,
        [(tokens, by_row(width)), (qkv_weight, whole(width, third))],
        [(shape((rows, width)), by_row(width)), (shape((rows, third)), by_row(third)), (shape((rows, half)), by_row(half))],
        name="first_local",
    )
    moved_weight = (qkv_weight, whole(width, third, 0, 1))
    moved_normed, moved_packed, arrived, outgoing = call(
        bind(moved_kernel, head_size, peers, capacity), balls,
        [(local_heads, ANY), (got, whole(wide_slots, width)), moved_weight],
        [
            (shape((rows, width)), by_row(width)), (shape((rows, third)), by_row(third)),
            (shape((1, slots), jnp.int32), whole(1, slots)), (shape((slots, half)), whole(slots, half)),
        ],
        scratch=[pltpu.VMEM((rows, half), BF16), pltpu.VMEM((rows, width), BF16), pltpu.VMEM((rows, third), BF16)],
        flops=LONG, name="moved", vmem=VMEM_BYTES,
    )
    returned = exchange(outgoing, peers)
    (grad_act,) = call(
        grad_act_kernel, balls,
        [(cotangent, by_row(width)), (all_weights, whole(hidden, width, 1))],
        [(shape((rows, hidden)), by_row(hidden))],
        name="grad_act",
    )
    mixed_heads, middle, second_normed, activated, grad_pre, grad_middle, grad_local, send_grad = call(
        middle_kernel, rows // block,
        [
            (tokens, by_row(width, block)), (local_heads, by_row(half, block)), (returned, whole(slots, half)),
            (slot, by_column(1, block)), (slot, whole(1, rows)), (proj_weight, whole(width, width)), all_up,
            (cotangent, by_row(width, block)), (grad_act, by_row(hidden, block)),
        ],
        [
            (shape((rows, width)), by_row(width, block)), (shape((rows, width)), by_row(width, block)),
            (shape((rows, width)), by_row(width, block)), (shape((rows, hidden)), by_row(hidden, block)),
            (shape((rows, hidden)), by_row(hidden, block)), (shape((rows, width)), by_row(width, block)),
            (shape((rows, half)), by_row(half, block)), (shape((slots, half)), whole(slots, half)),
        ],
        scratch=[pltpu.VMEM((rows, half), BF16)], flops=LONG, name="middle", vmem=VMEM_BYTES,
    )
    got_grad = exchange(send_grad, peers)
    output, mlp_both = call(
        weights_kernel, group_size,
        [
            (middle, whole(rows, width)), (activated, by_column(rows, width)),
            (all_weights, pl.BlockSpec((width, width), lambda step: (group_size + step, 0))),
            (cotangent, whole(rows, width)), (second_normed, whole(rows, width)),
            (grad_pre, by_column(rows, width)),
        ],
        [
            (shape((rows, width)), whole(rows, width)),
            (shape((2, hidden, width)), pl.BlockSpec((2, width, width), lambda step: (0, step, 0))),
        ],
        scratch=[pltpu.VMEM((width, rows), BF16), pltpu.VMEM((width, rows), BF16), pltpu.VMEM((rows, width), F32)],
        name="mlp_weights", vmem=VMEM_BYTES,
    )
    mlp_part = lax.psum_scatter(
        mlp_both.reshape(2 * hidden, width), ("core", "narrow"), scatter_dimension=0, tiled=True
    )
    first_local, qkv_local, proj_local = call(
        bind(local_back_kernel, head_size), balls,
        [
            (packed, by_row(third)), (grad_local, by_row(half)), (normed, whole(rows, width)),
            (qkv_weight, whole(width, third)), (mixed_heads, whole(rows, width)), (grad_middle, whole(rows, width)),
        ],
        [
            (shape((rows, width), F32), by_row(width)),
            (shape((width, third)), whole(width, third)), (shape((width, width)), whole(width, width)),
        ],
        scratch=[pltpu.VMEM((rows, third), BF16)],
        name="local_back", vmem=VMEM_BYTES,
    )
    moved_grad_packed, grad_outgoing = call(
        bind(moved_back_kernel, head_size), balls,
        [(output, ANY), (got_grad, whole(slots, half)), (arrived, whole(1, slots)), (moved_packed, by_row(third)), moved_weight],
        [(shape((rows, third)), by_row(third)), (shape((slots, width)), whole(slots, width))],
        scratch=[pltpu.VMEM((rows, width), BF16), pltpu.VMEM((rows, half), BF16), pltpu.VMEM((rows, third), BF16)],
        flops=LONG, name="moved_back", vmem=VMEM_BYTES,
    )
    grad_returned = exchange(grad_outgoing, peers)
    stacked = (shape((2 * width, width)), whole(2 * width, width))
    keep, send = call(
        moved_weights_kernel, 1,
        [flag, whole_array(moved_normed), whole_array(moved_grad_packed), whole_array(qkv_local), whole_array(proj_local)],
        [stacked, stacked],
        scratch=[pltpu.VMEM((width, 2 * third + width), BF16)], name="moved_weights",
    )
    pair = add([keep, swap_core(send)], grad_returned)
    mlp_mine, halfway = sum_by_steps(mlp_part, ("x", "z"), pair)
    (grad_tokens,) = call(
        last_kernel, balls,
        [(halfway, ANY), (tokens, by_row(width)), (grad_middle, by_row(width)), (first_local, by_row(width)), (grad_returned, whole(slots, width)), part],
        [(shape((rows, width)), by_row(width))],
        flops=LONG, name="last",
    )
    mlp_other = swap_core(mlp_mine)
    grad_up, grad_down = call(
        finish_mlp_kernel, 1, [flag, whole_array(mlp_mine), whole_array(mlp_other)],
        [(shape((width, width), F32), whole(width, width)), (shape((width, width), F32), whole(width, width))],
        name="finish_mlp",
    )
    mine = add([sum_at_once(pair, ("narrow", "x", "z"), halfway)], mlp_mine, grad_tokens)
    grad_qkv, grad_proj = call(
        finish_attention_kernel, 1, [flag, whole_array(mine), whole_array(swap_core(mine))],
        [(shape((width, 2 * third), F32), whole(width, 2 * third)), (shape((width, width), F32), whole(width, width))],
        name="finish_attention",
    )
    return output, grad_tokens, grad_qkv, grad_proj, grad_up, grad_down


def solution(mesh):
    wide, narrow = mesh.devices.shape
    axes = ("z", "x", "core", "narrow")
    mesh = Mesh(mesh.devices.reshape(wide // 8, 4, 2, narrow), axes)
    rows = axes
    return jax.shard_map(
        body,
        mesh=mesh,
        in_specs=(
            P(rows, None),
            P(rows),
            P(),
            P(),
            P(None, "narrow"),
            P("narrow", None),
            P(rows, None),
        ),
        out_specs=(
            P(rows, None),
            P(rows, None),
            P(),
            P(),
            P(None, "narrow"),
            P("narrow", None),
        ),
        check_vma=False,
    )
```

```python
import jax
import jax.numpy as jnp
from jax import lax
from jax.experimental import pallas as pl
from jax.experimental.pallas import tpu as pltpu
from jax.sharding import Mesh
from jax.sharding import PartitionSpec as P

HEADS = 8
BALL = 256
EPSILON = 1e-06
LANES = 128
VMEM_BYTES = 60 * 1024 * 1024
SMALL_BYTES = 16 * 1024 * 1024

LONG = 10**11

F32 = jnp.float32
BF16 = jnp.bfloat16


def mm(left, right):
    return lax.dot_general(left, right, (((1,), (0,)), ((), ())), preferred_element_type=F32)


def mm_nt(left, right):
    return lax.dot_general(left, right, (((1,), (1,)), ((), ())), preferred_element_type=F32)


def mm_tn(left, right):
    return lax.dot_general(left, right, (((0,), (0,)), ((), ())), preferred_element_type=F32)


def iota(shape, dimension):
    return lax.broadcasted_iota(jnp.int32, shape, dimension)


def row_scale(values):
    return lax.rsqrt(jnp.mean(values * values, axis=-1, keepdims=True) + EPSILON)


def norm_back(values, scaling, gradient):
    unit = values * scaling
    return scaling * (gradient - unit * jnp.mean(gradient * unit, axis=-1, keepdims=True))


def flip(block):
    return block.astype(F32).T.astype(BF16)


def as_column(row):
    return jnp.broadcast_to(row, (8, row.shape[1])).T[:, :1]


def onehot(condition):
    return jnp.where(condition, 1.0, 0.0).astype(BF16)


def head_mask(columns, head, head_size, value):
    lane = iota((1, columns), 1)
    inside = (lane >= head * head_size) & (lane < (head + 1) * head_size)
    return jnp.where(inside, value, 0.0).astype(BF16)


def by_head(rows, head_size, value):
    columns = rows.shape[1]
    heads = [rows * head_mask(columns, head, head_size, value) for head in range(columns // head_size)]
    return jnp.concatenate(heads, axis=0)


def ball_weights(key_rows, asked):
    scores = mm_nt(key_rows, asked)
    raised = jnp.exp(scores - jnp.max(scores, axis=0, keepdims=True))
    return raised * (1.0 / jnp.sum(raised, axis=0, keepdims=True))


def ball_attend(packed, head_size):
    columns = packed.shape[1] // 3
    queries, key_rows = packed[:, :columns], packed[:, columns : 2 * columns]
    rounded = ball_weights(key_rows, by_head(queries, head_size, head_size ** (-0.5))).astype(BF16)
    return per_head(flip(packed[:, 2 * columns :]), rounded, head_size).astype(BF16)


def per_head(rows_t, weights, head_size):
    columns, count = rows_t.shape
    parts = [
        mm(rows_t[head * head_size : (head + 1) * head_size], weights[:, head * count : (head + 1) * count])
        for head in range(columns // head_size)
    ]
    return jnp.concatenate(parts, axis=0).T


def ball_attend_back(packed, grad_out, head_size):
    columns = packed.shape[1] // 3
    queries, key_rows = packed[:, :columns], packed[:, columns : 2 * columns]
    asked = by_head(queries, head_size, head_size ** (-0.5))
    upstream = by_head(grad_out, head_size, 1.0)
    weights = ball_weights(key_rows, asked)
    dprob = mm_nt(packed[:, 2 * columns :], upstream)
    dscore = weights * (dprob - jnp.sum(dprob * weights, axis=0, keepdims=True))
    dscore = dscore.astype(BF16)
    grad_values = mm(weights.astype(BF16), upstream)
    grad_keys = mm(dscore, asked)
    grad_queries = per_head(flip(key_rows * jnp.asarray(head_size ** (-0.5), BF16)), dscore, head_size)
    return jnp.concatenate([grad_queries, grad_keys, grad_values], axis=1).astype(BF16)


def shape(dims, dtype=BF16):
    return jax.ShapeDtypeStruct(dims, dtype)


def by_row(columns, rows=BALL):
    return pl.BlockSpec((rows, columns), lambda step: (step, 0))


def by_column(rows, columns):
    return pl.BlockSpec((rows, columns), lambda step: (0, step))


def whole(rows, columns, row=0, column=0):
    return pl.BlockSpec((rows, columns), lambda step: (row, column))


FLAG = pl.BlockSpec(memory_space=pltpu.SMEM)
ANY = pl.BlockSpec(memory_space=pl.ANY)


def call(kernel, steps, ins, outs, scratch=(), flops=0, name=None, vmem=SMALL_BYTES):
    return pl.pallas_call(
        kernel,
        grid=(steps,),
        out_shape=[out for out, _ in outs],
        in_specs=[spec for _, spec in ins],
        out_specs=[spec for _, spec in outs],
        scratch_shapes=list(scratch),
        compiler_params=pltpu.CompilerParams(vmem_limit_bytes=vmem),
        cost_estimate=pl.CostEstimate(flops=flops, bytes_accessed=0, transcendentals=0),
        name=name,
    )(*[array for array, _ in ins])


def is_first():
    return pl.program_id(0) == 0


def is_last():
    return pl.program_id(0) == pl.num_programs(0) - 1


def late(columns, rows):
    return [pltpu.VMEM((rows, columns), BF16), pltpu.SemaphoreType.DMA(())]


def fetch(source, kept_ref, sem):
    copy = pltpu.make_async_copy(source, kept_ref, sem)

    @pl.when(is_first())
    def _():
        copy.start()

    def arrive():
        @pl.when(is_first())
        def _():
            copy.wait()

    return arrive


def route_kernel(
    peers, group_size, capacity, stride, rot_ref, all_ref, send_ref, slot_ref, wide_ref, place_ref, tok_ref, sem
):
    row_count = tok_ref.shape[0]
    step = BALL
    arrive = fetch(all_ref, tok_ref, sem)
    block = send_ref.shape[0]

    @pl.when(is_first())
    def _():
        rotation = rot_ref[...]
        target = rotation // (row_count * group_size)
        position = rotation % row_count + 1
        high = (position // 256).astype(F32)
        low = (position % 256).astype(F32)
        earlier = onehot(iota((step, step), 0) < iota((step, step), 1))
        carry = jnp.zeros((peers, 1), F32)
        sums_high = jnp.zeros((peers, LANES), F32)
        sums_low = jnp.zeros((peers, LANES), F32)
        for start in range(0, row_count, step):
            part = slice(start, start + step)
            chosen = jnp.where(iota((peers, step), 0) == target[:, part], 1.0, 0.0)
            before = mm(chosen.astype(BF16), earlier) + carry
            carry = carry + jnp.sum(chosen, axis=1, keepdims=True)
            rank = jnp.sum(chosen * before, axis=0, keepdims=True).astype(jnp.int32)
            slot_ref[:, part] = target[:, part] * capacity + rank
            wide_ref[:, part] = target[:, part] * stride + rank
            place = onehot(iota((LANES, step), 0) == rank)
            sums_high = sums_high + mm_nt((chosen * high[:, part]).astype(BF16), place)
            sums_low = sums_low + mm_nt((chosen * low[:, part]).astype(BF16), place)
        place_ref[:, :LANES] = sums_high.astype(BF16)
        place_ref[:, LANES:] = sums_low.astype(BF16)

    arrive()
    base = pl.program_id(0) * block
    pick = onehot(iota((block, row_count), 0) + base == wide_ref[...])
    rows = mm(pick, tok_ref[...])
    told = onehot(iota((block, peers), 0) + base == iota((block, peers), 1) * stride + capacity)
    extra = mm(told, place_ref[...])
    send_ref[:, : 2 * LANES] = (rows[:, : 2 * LANES] + extra).astype(BF16)
    send_ref[:, 2 * LANES :] = rows[:, 2 * LANES :].astype(BF16)


def arrived_row(place, stride):
    peers = place.shape[0]
    slots = peers * stride
    column = iota((1, slots), 1)
    source = column // stride
    spot = onehot(iota((LANES, slots), 0) == column - source * stride)
    spread = mm(place[:, :LANES], spot) * 256.0 + mm(place[:, LANES:], spot)
    own = iota((peers, slots), 0) == source
    return jnp.sum(jnp.where(own, spread, 0.0), axis=0, keepdims=True).astype(jnp.int32) - 1


def back_rows(arrived, rows_ref, out_ref):
    slots, step = out_ref.shape[0], 2 * BALL
    row_count = rows_ref.shape[0]
    arrived_col = as_column(arrived.astype(F32)).astype(jnp.int32)
    moved = rows_ref[...]
    for start in range(0, slots, step):
        pick = onehot(iota((step, row_count), 1) == arrived_col[start : start + step])
        out_ref[start : start + step, :] = mm(pick, moved).astype(BF16)


def first_local_kernel(head_size, tok_ref, wq_ref, nrm_ref, pk_ref, heads_ref):
    residual = tok_ref[...].astype(F32)
    normed = (residual * row_scale(residual)).astype(BF16)
    nrm_ref[...] = normed
    packed = mm(normed, wq_ref[...]).astype(BF16)
    pk_ref[...] = packed
    heads_ref[...] = ball_attend(packed, head_size)


def grad_act_kernel(cot_ref, down_ref, act_ref):
    act_ref[...] = mm_nt(cot_ref[...], down_ref[...]).astype(BF16)


def moved_kernel(
    head_size, peers, capacity, _, got_ref, wq_ref, nrm_ref, pk_ref, row_ref, out_ref,
    heads_ref, all_nrm_ref, all_pk_ref,
):
    slots = got_ref.shape[0]
    row_count = heads_ref.shape[0]
    stride = slots // peers

    @pl.when(is_first())
    def _():
        told = onehot(iota((peers, slots), 1) == iota((peers, slots), 0) * stride + capacity)
        place = mm(told, got_ref[:, : 2 * LANES]).astype(BF16)
        row_ref[...] = arrived_row(place, capacity)
        pick = onehot(iota((row_count, slots), 0) == arrived_row(place, stride))
        residual = mm(pick, got_ref[...])
        normed = (residual * row_scale(residual)).astype(BF16)
        all_nrm_ref[...] = normed
        all_pk_ref[...] = mm(normed, wq_ref[...]).astype(BF16)

    rows = pl.ds(pl.multiple_of(pl.program_id(0) * BALL, BALL), BALL)
    nrm_ref[...] = all_nrm_ref[rows, :]
    packed = all_pk_ref[rows, :]
    pk_ref[...] = packed
    heads_ref[rows, :] = ball_attend(packed, head_size)

    @pl.when(is_last())
    def _():
        back_rows(row_ref[...], heads_ref, out_ref)


def middle_kernel(
    tok_ref, local_ref, ret_ref, part_ref, slot_ref, proj_ref, up_ref, cot_ref, act_ref,
    mix_ref, mid_ref, sn_ref, gated_ref, pre_ref, gm_ref, gl_ref, send_ref, gh_ref,
):
    count, width = tok_ref.shape
    half = width // 2
    slots = ret_ref.shape[0]
    chunks = up_ref.shape[0] // width
    rate = 0.7978845608028654
    cubic = 0.044715 * rate
    slot_col = as_column(part_ref[...].astype(F32)).astype(jnp.int32)
    pick = onehot(iota((count, slots), 1) == slot_col)
    moved = mm(pick, ret_ref[...]).astype(BF16)
    mixed = jnp.concatenate([local_ref[...], moved], axis=1)
    mix_ref[...] = mixed
    middle = (tok_ref[...].astype(F32) + mm(mixed, proj_ref[...])).astype(BF16)
    mid_ref[...] = middle
    middle_f = middle.astype(F32)
    second_scale = row_scale(middle_f)
    normed = (middle_f * second_scale).astype(BF16)
    sn_ref[...] = normed
    grad_second = jnp.zeros((count, width), F32)
    pres = [mm(normed, up_ref[chunk * width : (chunk + 1) * width, :]) for chunk in range(chunks)]
    for chunk, pre in enumerate(pres):
        columns = slice(chunk * width, (chunk + 1) * width)
        square = pre * pre
        upper = 0.5 + 0.5 * jnp.tanh(pre * (rate + cubic * square))
        gated_ref[:, columns] = (pre * upper).astype(BF16)
        slope = upper * (1.0 + (1.0 - upper) * (pre * (2.0 * rate + 6.0 * cubic * square)))
        grad_pre = (act_ref[:, columns].astype(F32) * slope).astype(BF16)
        pre_ref[:, columns] = grad_pre
        grad_second = grad_second + mm_nt(grad_pre, up_ref[columns, :])
    grad_middle = (
        cot_ref[...].astype(F32) + norm_back(middle_f, second_scale, grad_second)
    ).astype(BF16)
    gm_ref[...] = grad_middle
    grad_heads = mm_nt(grad_middle, proj_ref[...]).astype(BF16)
    gl_ref[...] = grad_heads[:, :half]
    base = pl.multiple_of(pl.program_id(0) * count, count)
    gh_ref[pl.ds(base, count), :] = grad_heads[:, half:]

    @pl.when(is_last())
    def _():
        moved_grad = gh_ref[...]
        slot = slot_ref[...]
        step = 2 * BALL
        for start in range(0, slots, step):
            pick = onehot(iota((step, slot.shape[1]), 0) + start == slot)
            send_ref[start : start + step, :] = mm(pick, moved_grad).astype(BF16)


def weights_kernel(
    mid_ref, gated_ref, down_ref, cot_ref, sn_ref, pre_ref,
    out_ref, both_ref, sn_t_ref, cot_t_ref, sum_ref,
):
    @pl.when(is_first())
    def _():
        sn_t_ref[...] = flip(sn_ref[...])
        cot_t_ref[...] = flip(cot_ref[...])
        sum_ref[...] = mid_ref[...].astype(F32)

    gated = gated_ref[...]
    both_ref[0, 0] = mm(sn_t_ref[...], pre_ref[...]).astype(BF16)
    both_ref[0, 1] = mm(cot_t_ref[...], gated).astype(BF16)
    sum_ref[...] += mm(gated, down_ref[...])

    @pl.when(is_last())
    def _():
        out_ref[...] = sum_ref[...].astype(BF16)


def local_back_kernel(
    head_size, pk_ref, gl_ref, nrm_ref, wq_ref, mix_ref, gm_ref,
    first_ref, gq_ref, gp_ref, gpk_ref,
):
    grad_packed = ball_attend_back(pk_ref[...], gl_ref[...], head_size)
    base = pl.multiple_of(pl.program_id(0) * BALL, BALL)
    gpk_ref[pl.ds(base, BALL), :] = grad_packed
    first_ref[...] = mm_nt(grad_packed, wq_ref[...])

    @pl.when(is_last())
    def _():
        gq_ref[...] = mm(flip(nrm_ref[...]), gpk_ref[...]).astype(BF16)
        gp_ref[...] = mm(flip(mix_ref[...]), gm_ref[...]).astype(BF16)


def moved_back_kernel(
    head_size, _, got_ref, row_ref, pk_ref, wq_ref, gpk_ref, out_ref, first_ref, grad_ref, all_gpk_ref
):
    slots = got_ref.shape[0]

    @pl.when(is_first())
    def _():
        pick = onehot(iota((grad_ref.shape[0], slots), 0) == row_ref[...])
        grad_ref[...] = mm(pick, got_ref[...]).astype(BF16)

    rows = pl.ds(pl.multiple_of(pl.program_id(0) * BALL, BALL), BALL)
    grad_packed = ball_attend_back(pk_ref[...], grad_ref[rows, :], head_size)
    gpk_ref[...] = grad_packed
    all_gpk_ref[rows, :] = grad_packed

    @pl.when(is_last())
    def _():
        first_ref[...] = mm_nt(all_gpk_ref[...], wq_ref[...]).astype(BF16)
        back_rows(row_ref[...], first_ref, out_ref)


def moved_weights_kernel(core_ref, nrm_ref, gpk_ref, gq_ref, gp_ref, keep_ref, send_ref, all_ref):
    width, third = gq_ref.shape
    all_ref[:, :third] = gq_ref[...]
    all_ref[:, third : 2 * third] = mm(flip(nrm_ref[...]), gpk_ref[...]).astype(BF16)
    all_ref[:, 2 * third :] = gp_ref[...]
    half = width // 2
    core = core_ref[0]
    for side, out_ref in ((core, keep_ref), (1 - core, send_ref)):
        rows = pl.ds(pl.multiple_of(side * half, half), half)
        for block in range(all_ref.shape[1] // width):
            out_ref[block * half : (block + 1) * half, :] = all_ref[rows, block * width : (block + 1) * width]


def add_split_kernel(count, after, spot_ref, *refs):
    ins, outs, sum_ref = refs[: -count - 1], refs[-count - 1 : -1], refs[-1]
    total = ins[0][...].astype(F32)
    for in_ref in ins[1:]:
        total = total + in_ref[...].astype(F32)
    sum_ref[...] = total.astype(BF16)
    size = sum_ref.shape[0] // count
    for shift, out_ref in enumerate(outs):
        start = lax.rem(spot_ref[0] + shift, count) * size
        out_ref[...] = sum_ref[pl.ds(pl.multiple_of(start, size), size), :]


def add_kernel(after, also, *refs):
    total = refs[0][...].astype(F32)
    for in_ref in refs[1:-1]:
        total = total + in_ref[...].astype(F32)
    refs[-1][...] = total.astype(BF16)


def add_parts(in_ref):
    total = in_ref[0].astype(F32)
    for part in range(1, in_ref.shape[0]):
        total = total + in_ref[part].astype(F32)
    return total.astype(BF16)


def spread_kernel(after, in_ref, out_ref):
    total = add_parts(in_ref)
    for part in range(out_ref.shape[0]):
        out_ref[part] = total


def place_kernel(spot_ref, *refs):
    ins, out_ref = refs[:-1], refs[-1]
    count, size = len(ins), ins[0].shape[0]
    for shift, in_ref in enumerate(ins):
        start = lax.rem(spot_ref[0] + (count - shift), count) * size
        out_ref[pl.ds(pl.multiple_of(start, size), size), :] = in_ref[...]


def last_kernel(_, tok_ref, gm_ref, first_ref, ret_ref, part_ref, out_ref):
    slots = ret_ref.shape[0]
    slot_col = as_column(part_ref[...].astype(F32)).astype(jnp.int32)
    pick = onehot(iota((BALL, slots), 1) == slot_col)
    grad_first = first_ref[...] + mm(pick, ret_ref[...])
    residual = tok_ref[...].astype(F32)
    out_ref[...] = (
        gm_ref[...].astype(F32) + norm_back(residual, row_scale(residual), grad_first)
    ).astype(BF16)


def finish_mlp_kernel(core_ref, mine_ref, other_ref, up_ref, down_ref):
    core = core_ref[0]

    @pl.when(core == 0)
    def _():
        up_ref[...] = mine_ref[...].astype(F32)
        down_ref[...] = other_ref[...].astype(F32).T

    @pl.when(core != 0)
    def _():
        up_ref[...] = other_ref[...].astype(F32)
        down_ref[...] = mine_ref[...].astype(F32).T


def finish_attention_kernel(core_ref, mine_ref, other_ref, qkv_ref, proj_ref):
    core = core_ref[0]
    width = mine_ref.shape[1]
    half = mine_ref.shape[0] // 4
    for side, part_ref in ((core, mine_ref), (1 - core, other_ref)):
        rows = pl.ds(pl.multiple_of(side * half, half), half)
        for block in range(3):
            qkv_ref[rows, block * width : (block + 1) * width] = part_ref[block * half : (block + 1) * half, :].astype(F32)
        proj_ref[rows, :] = part_ref[3 * half :, :].astype(F32)


def exchange(rows, peers):
    slots, columns = rows.shape
    sent = rows.reshape(peers, slots // peers, columns)
    got = lax.all_to_all(sent, ("z", "x", "core"), split_axis=0, concat_axis=0, tiled=True)
    return got.reshape(slots, columns)


def swap_core(block):
    return lax.ppermute(block, "core", [(0, 1), (1, 0)])


def whole_array(array):
    return array, whole(*array.shape)


def spot_on(axis):
    return lax.axis_index(axis).astype(jnp.int32).reshape(1), FLAG


def shift_by(block, axis, shift):
    count = lax.axis_size(axis)
    return lax.ppermute(block, axis, [(place, (place + shift) % count) for place in range(count)])


def add_split(parts, axis, after):
    count = lax.axis_size(axis)
    rows, columns = parts[0].shape
    out = (shape((rows // count, columns)), whole(rows // count, columns))
    shares = call(
        bind(add_split_kernel, count), 1,
        [(after, ANY), spot_on(axis)] + [whole_array(part) for part in parts], [out] * count,
        scratch=[pltpu.VMEM((rows, columns), BF16)], name="add_split",
    )
    return [shares[0]] + [shift_by(shares[shift], axis, shift) for shift in range(1, count)]


def gather(block, axis):
    count = lax.axis_size(axis)
    rows, columns = block.shape
    parts = [block] + [shift_by(block, axis, shift) for shift in range(1, count)]
    (joined,) = call(
        place_kernel, 1, [spot_on(axis)] + [whole_array(part) for part in parts],
        [(shape((count * rows, columns)), whole(count * rows, columns))], name="gather",
    )
    return joined


def add(parts, after, also=None):
    also = after if also is None else also
    (block,) = call(
        add_kernel, 1, [(after, ANY), (also, ANY)] + [whole_array(part) for part in parts],
        [(shape(parts[0].shape), whole(*parts[0].shape))], name="add",
    )
    return block


def share_of_sum(block, axes):
    count = lax.axis_size(axes)
    rows, columns = block.shape
    parts = block.reshape(count, rows // count, columns)
    return lax.all_to_all(parts, axes, split_axis=0, concat_axis=0, tiled=True)


def whole_parts(parts):
    return parts, pl.BlockSpec(parts.shape, lambda step: (0, 0, 0))


def sum_by_steps(block, axes, after):
    parts = [block]
    for axis in axes:
        parts = add_split(parts, axis, after)
    halfway = parts[0]
    block = add(parts, after)
    for axis in reversed(axes):
        block = gather(block, axis)
    return block, halfway


def sum_at_once(block, axes, after):
    parts = share_of_sum(block, axes)
    (spread,) = call(
        spread_kernel, 1, [(after, ANY), whole_parts(parts)], [(shape(parts.shape), whole_parts(parts)[1])], name="add_spread",
    )
    told = lax.all_to_all(spread, axes, split_axis=0, concat_axis=0, tiled=True)
    return told.reshape(block.shape)


def bind(kernel, *fixed):
    def bound(*refs):
        kernel(*fixed, *refs)

    return bound


def body(tokens, rotation, qkv_weight, proj_weight, up_weight, down_weight, cotangent):
    rows, width = tokens.shape
    half = width // 2
    third = 3 * half
    head_size = width // HEADS
    peers = lax.axis_size(("z", "x", "core"))
    group_size = lax.axis_size("narrow")
    capacity = rows // peers + rows // peers // 2
    stride = capacity + 8
    slots = peers * capacity
    wide_slots = peers * stride
    hidden = group_size * up_weight.shape[1]
    balls = rows // BALL
    block = 2 * BALL
    core = lax.axis_index("core")
    flag = (core.astype(jnp.int32).reshape(1), FLAG)
    own_weight = jnp.where(core == 0, up_weight, down_weight)
    all_weights = lax.all_gather(own_weight, ("core", "narrow"), axis=0, tiled=True)
    all_up = (all_weights, whole(hidden, width))

    send, slot = call(
        bind(route_kernel, peers, group_size, capacity, stride), 2,
        [(rotation.reshape(1, rows), whole(1, rows)), (tokens, ANY)],
        [(shape((wide_slots, width)), by_row(width, wide_slots // 2)), (shape((1, rows), jnp.int32), whole(1, rows))],
        scratch=[pltpu.VMEM((1, rows), jnp.int32), pltpu.VMEM((peers, 2 * LANES), BF16)] + late(width, rows),
        flops=LONG, name="route", vmem=VMEM_BYTES,
    )
    got = exchange(send, peers)
    part = (slot, by_column(1, BALL))

    normed, packed, local_heads = call(
        bind(first_local_kernel, head_size), balls,
        [(tokens, by_row(width)), (qkv_weight, whole(width, third))],
        [(shape((rows, width)), by_row(width)), (shape((rows, third)), by_row(third)), (shape((rows, half)), by_row(half))],
        name="first_local",
    )
    moved_weight = (qkv_weight, whole(width, third, 0, 1))
    moved_normed, moved_packed, arrived, outgoing = call(
        bind(moved_kernel, head_size, peers, capacity), balls,
        [(local_heads, ANY), (got, whole(wide_slots, width)), moved_weight],
        [
            (shape((rows, width)), by_row(width)), (shape((rows, third)), by_row(third)),
            (shape((1, slots), jnp.int32), whole(1, slots)), (shape((slots, half)), whole(slots, half)),
        ],
        scratch=[pltpu.VMEM((rows, half), BF16), pltpu.VMEM((rows, width), BF16), pltpu.VMEM((rows, third), BF16)],
        flops=LONG, name="moved", vmem=VMEM_BYTES,
    )
    returned = exchange(outgoing, peers)
    (grad_act,) = call(
        grad_act_kernel, balls,
        [(cotangent, by_row(width)), (all_weights, whole(hidden, width, 1))],
        [(shape((rows, hidden)), by_row(hidden))],
        name="grad_act",
    )
    mixed_heads, middle, second_normed, activated, grad_pre, grad_middle, grad_local, send_grad = call(
        middle_kernel, rows // block,
        [
            (tokens, by_row(width, block)), (local_heads, by_row(half, block)), (returned, whole(slots, half)),
            (slot, by_column(1, block)), (slot, whole(1, rows)), (proj_weight, whole(width, width)), all_up,
            (cotangent, by_row(width, block)), (grad_act, by_row(hidden, block)),
        ],
        [
            (shape((rows, width)), by_row(width, block)), (shape((rows, width)), by_row(width, block)),
            (shape((rows, width)), by_row(width, block)), (shape((rows, hidden)), by_row(hidden, block)),
            (shape((rows, hidden)), by_row(hidden, block)), (shape((rows, width)), by_row(width, block)),
            (shape((rows, half)), by_row(half, block)), (shape((slots, half)), whole(slots, half)),
        ],
        scratch=[pltpu.VMEM((rows, half), BF16)], flops=LONG, name="middle", vmem=VMEM_BYTES,
    )
    got_grad = exchange(send_grad, peers)
    output, mlp_both = call(
        weights_kernel, group_size,
        [
            (middle, whole(rows, width)), (activated, by_column(rows, width)),
            (all_weights, pl.BlockSpec((width, width), lambda step: (group_size + step, 0))),
            (cotangent, whole(rows, width)), (second_normed, whole(rows, width)),
            (grad_pre, by_column(rows, width)),
        ],
        [
            (shape((rows, width)), whole(rows, width)),
            (shape((group_size, 2, width, width)), pl.BlockSpec((1, 2, width, width), lambda step: (step, 0, 0, 0))),
        ],
        scratch=[pltpu.VMEM((width, rows), BF16), pltpu.VMEM((width, rows), BF16), pltpu.VMEM((rows, width), F32)],
        name="mlp_weights", vmem=VMEM_BYTES,
    )
    mlp_part = lax.psum_scatter(
        mlp_both.reshape(2 * hidden, width), ("narrow", "core"), scatter_dimension=0, tiled=True
    )
    first_local, qkv_local, proj_local = call(
        bind(local_back_kernel, head_size), balls,
        [
            (packed, by_row(third)), (grad_local, by_row(half)), (normed, whole(rows, width)),
            (qkv_weight, whole(width, third)), (mixed_heads, whole(rows, width)), (grad_middle, whole(rows, width)),
        ],
        [
            (shape((rows, width), F32), by_row(width)),
            (shape((width, third)), whole(width, third)), (shape((width, width)), whole(width, width)),
        ],
        scratch=[pltpu.VMEM((rows, third), BF16)],
        name="local_back", vmem=VMEM_BYTES,
    )
    moved_grad_packed, grad_outgoing = call(
        bind(moved_back_kernel, head_size), balls,
        [(output, ANY), (got_grad, whole(slots, half)), (arrived, whole(1, slots)), (moved_packed, by_row(third)), moved_weight],
        [(shape((rows, third)), by_row(third)), (shape((slots, width)), whole(slots, width))],
        scratch=[pltpu.VMEM((rows, width), BF16), pltpu.VMEM((rows, half), BF16), pltpu.VMEM((rows, third), BF16)],
        flops=LONG, name="moved_back", vmem=VMEM_BYTES,
    )
    grad_returned = exchange(grad_outgoing, peers)
    stacked = (shape((2 * width, width)), whole(2 * width, width))
    keep, send = call(
        moved_weights_kernel, 1,
        [flag, whole_array(moved_normed), whole_array(moved_grad_packed), whole_array(qkv_local), whole_array(proj_local)],
        [stacked, stacked],
        scratch=[pltpu.VMEM((width, 2 * third + width), BF16)], name="moved_weights",
    )
    pair = add([keep, swap_core(send)], grad_returned)
    mlp_mine, halfway = sum_by_steps(mlp_part, ("x", "z"), pair)
    (grad_tokens,) = call(
        last_kernel, balls,
        [(halfway, ANY), (tokens, by_row(width)), (grad_middle, by_row(width)), (first_local, by_row(width)), (grad_returned, whole(slots, width)), part],
        [(shape((rows, width)), by_row(width))],
        flops=LONG, name="last",
    )
    mlp_other = swap_core(mlp_mine)
    grad_up, grad_down = call(
        finish_mlp_kernel, 1, [flag, whole_array(mlp_mine), whole_array(mlp_other)],
        [(shape((width, width), F32), whole(width, width)), (shape((width, width), F32), whole(width, width))],
        name="finish_mlp",
    )
    mine = add([sum_at_once(pair, ("narrow", "x", "z"), halfway)], mlp_mine, grad_tokens)
    grad_qkv, grad_proj = call(
        finish_attention_kernel, 1, [flag, whole_array(mine), whole_array(swap_core(mine))],
        [(shape((width, 2 * third), F32), whole(width, 2 * third)), (shape((width, width), F32), whole(width, width))],
        name="finish_attention",
    )
    return output, grad_tokens, grad_qkv, grad_proj, grad_up, grad_down


def solution(mesh):
    wide, narrow = mesh.devices.shape
    axes = ("z", "x", "core", "narrow")
    mesh = Mesh(mesh.devices.reshape(wide // 8, 4, 2, narrow), axes)
    rows = axes
    return jax.shard_map(
        body,
        mesh=mesh,
        in_specs=(
            P(rows, None),
            P(rows),
            P(),
            P(),
            P(None, "narrow"),
            P("narrow", None),
            P(rows, None),
        ),
        out_specs=(
            P(rows, None),
            P(rows, None),
            P(),
            P(),
            P(None, "narrow"),
            P("narrow", None),
        ),
        check_vma=False,
    )
```

```python
import jax
import jax.numpy as jnp
from jax import lax
from jax.experimental import pallas as pl
from jax.experimental.pallas import tpu as pltpu
from jax.sharding import Mesh
from jax.sharding import PartitionSpec as P

HEADS = 8
BALL = 256
EPSILON = 1e-06
LANES = 128
VMEM_BYTES = 60 * 1024 * 1024
SMALL_BYTES = 16 * 1024 * 1024

LONG = 10**11

F32 = jnp.float32
BF16 = jnp.bfloat16


def mm(left, right):
    return lax.dot_general(left, right, (((1,), (0,)), ((), ())), preferred_element_type=F32)


def mm_nt(left, right):
    return lax.dot_general(left, right, (((1,), (1,)), ((), ())), preferred_element_type=F32)


def mm_tn(left, right):
    return lax.dot_general(left, right, (((0,), (0,)), ((), ())), preferred_element_type=F32)


def iota(shape, dimension):
    return lax.broadcasted_iota(jnp.int32, shape, dimension)


def row_scale(values):
    return lax.rsqrt(jnp.mean(values * values, axis=-1, keepdims=True) + EPSILON)


def norm_back(values, scaling, gradient):
    unit = values * scaling
    return scaling * (gradient - unit * jnp.mean(gradient * unit, axis=-1, keepdims=True))


def flip(block):
    return block.astype(F32).T.astype(BF16)


def as_column(row):
    return jnp.broadcast_to(row, (8, row.shape[1])).T[:, :1]


def onehot(condition):
    return jnp.where(condition, 1.0, 0.0).astype(BF16)


def head_mask(columns, head, head_size, value):
    lane = iota((1, columns), 1)
    inside = (lane >= head * head_size) & (lane < (head + 1) * head_size)
    return jnp.where(inside, value, 0.0).astype(BF16)


def by_head(rows, head_size, value):
    columns = rows.shape[1]
    heads = [rows * head_mask(columns, head, head_size, value) for head in range(columns // head_size)]
    return jnp.concatenate(heads, axis=0)


def ball_weights(key_rows, asked):
    scores = mm_nt(key_rows, asked)
    raised = jnp.exp(scores - jnp.max(scores, axis=0, keepdims=True))
    return raised * (1.0 / jnp.sum(raised, axis=0, keepdims=True))


def ball_attend(packed, head_size):
    columns = packed.shape[1] // 3
    queries, key_rows = packed[:, :columns], packed[:, columns : 2 * columns]
    rounded = ball_weights(key_rows, by_head(queries, head_size, head_size ** (-0.5))).astype(BF16)
    return per_head(flip(packed[:, 2 * columns :]), rounded, head_size).astype(BF16)


def per_head(rows_t, weights, head_size):
    columns, count = rows_t.shape
    parts = [
        mm(rows_t[head * head_size : (head + 1) * head_size], weights[:, head * count : (head + 1) * count])
        for head in range(columns // head_size)
    ]
    return jnp.concatenate(parts, axis=0).T


def ball_attend_back(packed, grad_out, head_size):
    columns = packed.shape[1] // 3
    queries, key_rows = packed[:, :columns], packed[:, columns : 2 * columns]
    asked = by_head(queries, head_size, head_size ** (-0.5))
    upstream = by_head(grad_out, head_size, 1.0)
    weights = ball_weights(key_rows, asked)
    dprob = mm_nt(packed[:, 2 * columns :], upstream)
    dscore = weights * (dprob - jnp.sum(dprob * weights, axis=0, keepdims=True))
    dscore = dscore.astype(BF16)
    grad_values = mm(weights.astype(BF16), upstream)
    grad_keys = mm(dscore, asked)
    grad_queries = per_head(flip(key_rows * jnp.asarray(head_size ** (-0.5), BF16)), dscore, head_size)
    return jnp.concatenate([grad_queries, grad_keys, grad_values], axis=1).astype(BF16)


def shape(dims, dtype=BF16):
    return jax.ShapeDtypeStruct(dims, dtype)


def by_row(columns, rows=BALL):
    return pl.BlockSpec((rows, columns), lambda step: (step, 0))


def by_column(rows, columns):
    return pl.BlockSpec((rows, columns), lambda step: (0, step))


def whole(rows, columns, row=0, column=0):
    return pl.BlockSpec((rows, columns), lambda step: (row, column))


FLAG = pl.BlockSpec(memory_space=pltpu.SMEM)
ANY = pl.BlockSpec(memory_space=pl.ANY)


def call(kernel, steps, ins, outs, scratch=(), flops=0, name=None, vmem=SMALL_BYTES):
    return pl.pallas_call(
        kernel,
        grid=(steps,),
        out_shape=[out for out, _ in outs],
        in_specs=[spec for _, spec in ins],
        out_specs=[spec for _, spec in outs],
        scratch_shapes=list(scratch),
        compiler_params=pltpu.CompilerParams(vmem_limit_bytes=vmem),
        cost_estimate=pl.CostEstimate(flops=flops, bytes_accessed=0, transcendentals=0),
        name=name,
    )(*[array for array, _ in ins])


def is_first():
    return pl.program_id(0) == 0


def is_last():
    return pl.program_id(0) == pl.num_programs(0) - 1


def late(columns, rows):
    return [pltpu.VMEM((rows, columns), BF16), pltpu.SemaphoreType.DMA(())]


def fetch(source, kept_ref, sem):
    copy = pltpu.make_async_copy(source, kept_ref, sem)

    @pl.when(is_first())
    def _():
        copy.start()

    def arrive():
        @pl.when(is_first())
        def _():
            copy.wait()

    return arrive


def route_kernel(
    peers, group_size, capacity, stride, rot_ref, all_ref, send_ref, slot_ref, wide_ref, place_ref, tok_ref, sem
):
    row_count = tok_ref.shape[0]
    step = BALL
    arrive = fetch(all_ref, tok_ref, sem)
    block = send_ref.shape[0]

    @pl.when(is_first())
    def _():
        rotation = rot_ref[...]
        target = rotation // (row_count * group_size)
        position = rotation % row_count + 1
        high = (position // 256).astype(F32)
        low = (position % 256).astype(F32)
        earlier = onehot(iota((step, step), 0) < iota((step, step), 1))
        carry = jnp.zeros((peers, 1), F32)
        sums_high = jnp.zeros((peers, LANES), F32)
        sums_low = jnp.zeros((peers, LANES), F32)
        for start in range(0, row_count, step):
            part = slice(start, start + step)
            chosen = jnp.where(iota((peers, step), 0) == target[:, part], 1.0, 0.0)
            before = mm(chosen.astype(BF16), earlier) + carry
            carry = carry + jnp.sum(chosen, axis=1, keepdims=True)
            rank = jnp.sum(chosen * before, axis=0, keepdims=True).astype(jnp.int32)
            slot_ref[:, part] = target[:, part] * capacity + rank
            wide_ref[:, part] = target[:, part] * stride + rank
            place = onehot(iota((LANES, step), 0) == rank)
            sums_high = sums_high + mm_nt((chosen * high[:, part]).astype(BF16), place)
            sums_low = sums_low + mm_nt((chosen * low[:, part]).astype(BF16), place)
        place_ref[:, :LANES] = sums_high.astype(BF16)
        place_ref[:, LANES:] = sums_low.astype(BF16)

    arrive()
    base = pl.program_id(0) * block
    pick = onehot(iota((block, row_count), 0) + base == wide_ref[...])
    rows = mm(pick, tok_ref[...])
    told = onehot(iota((block, peers), 0) + base == iota((block, peers), 1) * stride + capacity)
    extra = mm(told, place_ref[...])
    send_ref[:, : 2 * LANES] = (rows[:, : 2 * LANES] + extra).astype(BF16)
    send_ref[:, 2 * LANES :] = rows[:, 2 * LANES :].astype(BF16)


def arrived_row(place, stride):
    peers = place.shape[0]
    slots = peers * stride
    column = iota((1, slots), 1)
    source = column // stride
    spot = onehot(iota((LANES, slots), 0) == column - source * stride)
    spread = mm(place[:, :LANES], spot) * 256.0 + mm(place[:, LANES:], spot)
    own = iota((peers, slots), 0) == source
    return jnp.sum(jnp.where(own, spread, 0.0), axis=0, keepdims=True).astype(jnp.int32) - 1


def back_rows(arrived, rows_ref, out_ref):
    slots, step = out_ref.shape[0], 2 * BALL
    row_count = rows_ref.shape[0]
    arrived_col = as_column(arrived.astype(F32)).astype(jnp.int32)
    moved = rows_ref[...]
    for start in range(0, slots, step):
        pick = onehot(iota((step, row_count), 1) == arrived_col[start : start + step])
        out_ref[start : start + step, :] = mm(pick, moved).astype(BF16)


def first_local_kernel(head_size, tok_ref, wq_ref, nrm_ref, pk_ref, heads_ref):
    residual = tok_ref[...].astype(F32)
    normed = (residual * row_scale(residual)).astype(BF16)
    nrm_ref[...] = normed
    packed = mm(normed, wq_ref[...]).astype(BF16)
    pk_ref[...] = packed
    heads_ref[...] = ball_attend(packed, head_size)


def grad_act_kernel(cot_ref, down_ref, act_ref):
    act_ref[...] = mm_nt(cot_ref[...], down_ref[...]).astype(BF16)


def moved_kernel(
    head_size, peers, capacity, _, got_ref, wq_ref, nrm_ref, pk_ref, row_ref, out_ref,
    heads_ref, all_nrm_ref, all_pk_ref,
):
    slots = got_ref.shape[0]
    row_count = heads_ref.shape[0]
    stride = slots // peers

    @pl.when(is_first())
    def _():
        told = onehot(iota((peers, slots), 1) == iota((peers, slots), 0) * stride + capacity)
        place = mm(told, got_ref[:, : 2 * LANES]).astype(BF16)
        row_ref[...] = arrived_row(place, capacity)
        pick = onehot(iota((row_count, slots), 0) == arrived_row(place, stride))
        residual = mm(pick, got_ref[...])
        normed = (residual * row_scale(residual)).astype(BF16)
        all_nrm_ref[...] = normed
        all_pk_ref[...] = mm(normed, wq_ref[...]).astype(BF16)

    rows = pl.ds(pl.multiple_of(pl.program_id(0) * BALL, BALL), BALL)
    nrm_ref[...] = all_nrm_ref[rows, :]
    packed = all_pk_ref[rows, :]
    pk_ref[...] = packed
    heads_ref[rows, :] = ball_attend(packed, head_size)

    @pl.when(is_last())
    def _():
        back_rows(row_ref[...], heads_ref, out_ref)


def middle_kernel(
    tok_ref, local_ref, ret_ref, part_ref, slot_ref, proj_ref, up_ref, cot_ref, act_ref,
    mix_ref, mid_ref, sn_ref, gated_ref, pre_ref, gm_ref, gl_ref, send_ref, gh_ref,
):
    count, width = tok_ref.shape
    half = width // 2
    slots = ret_ref.shape[0]
    chunks = up_ref.shape[0] // width
    rate = 0.7978845608028654
    cubic = 0.044715 * rate
    slot_col = as_column(part_ref[...].astype(F32)).astype(jnp.int32)
    pick = onehot(iota((count, slots), 1) == slot_col)
    moved = mm(pick, ret_ref[...]).astype(BF16)
    mixed = jnp.concatenate([local_ref[...], moved], axis=1)
    mix_ref[...] = mixed
    middle = (tok_ref[...].astype(F32) + mm(mixed, proj_ref[...])).astype(BF16)
    mid_ref[...] = middle
    middle_f = middle.astype(F32)
    second_scale = row_scale(middle_f)
    normed = (middle_f * second_scale).astype(BF16)
    sn_ref[...] = normed
    grad_second = jnp.zeros((count, width), F32)
    pres = [mm(normed, up_ref[chunk * width : (chunk + 1) * width, :]) for chunk in range(chunks)]
    for chunk, pre in enumerate(pres):
        columns = slice(chunk * width, (chunk + 1) * width)
        square = pre * pre
        upper = 0.5 + 0.5 * jnp.tanh(pre * (rate + cubic * square))
        gated_ref[:, columns] = (pre * upper).astype(BF16)
        slope = upper * (1.0 + (1.0 - upper) * (pre * (2.0 * rate + 6.0 * cubic * square)))
        grad_pre = (act_ref[:, columns].astype(F32) * slope).astype(BF16)
        pre_ref[:, columns] = grad_pre
        grad_second = grad_second + mm_nt(grad_pre, up_ref[columns, :])
    grad_middle = (
        cot_ref[...].astype(F32) + norm_back(middle_f, second_scale, grad_second)
    ).astype(BF16)
    gm_ref[...] = grad_middle
    grad_heads = mm_nt(grad_middle, proj_ref[...]).astype(BF16)
    gl_ref[...] = grad_heads[:, :half]
    base = pl.multiple_of(pl.program_id(0) * count, count)
    gh_ref[pl.ds(base, count), :] = grad_heads[:, half:]

    @pl.when(is_last())
    def _():
        moved_grad = gh_ref[...]
        slot = slot_ref[...]
        step = 2 * BALL
        for start in range(0, slots, step):
            pick = onehot(iota((step, slot.shape[1]), 0) + start == slot)
            send_ref[start : start + step, :] = mm(pick, moved_grad).astype(BF16)


def weights_kernel(
    mid_ref, gated_ref, down_ref, cot_ref, sn_ref, pre_ref,
    out_ref, both_ref, sn_t_ref, cot_t_ref, sum_ref,
):
    @pl.when(is_first())
    def _():
        sn_t_ref[...] = flip(sn_ref[...])
        cot_t_ref[...] = flip(cot_ref[...])
        sum_ref[...] = mid_ref[...].astype(F32)

    gated = gated_ref[...]
    both_ref[0, 0] = mm(sn_t_ref[...], pre_ref[...]).astype(BF16)
    both_ref[0, 1] = mm(cot_t_ref[...], gated).astype(BF16)
    sum_ref[...] += mm(gated, down_ref[...])

    @pl.when(is_last())
    def _():
        out_ref[...] = sum_ref[...].astype(BF16)


def local_back_kernel(
    head_size, pk_ref, gl_ref, nrm_ref, wq_ref, mix_ref, gm_ref,
    first_ref, gq_ref, gp_ref, gpk_ref,
):
    grad_packed = ball_attend_back(pk_ref[...], gl_ref[...], head_size)
    base = pl.multiple_of(pl.program_id(0) * BALL, BALL)
    gpk_ref[pl.ds(base, BALL), :] = grad_packed
    first_ref[...] = mm_nt(grad_packed, wq_ref[...])

    @pl.when(is_last())
    def _():
        gq_ref[...] = mm(flip(nrm_ref[...]), gpk_ref[...]).astype(BF16)
        gp_ref[...] = mm(flip(mix_ref[...]), gm_ref[...]).astype(BF16)


def moved_back_kernel(
    head_size, _, got_ref, row_ref, pk_ref, wq_ref, gpk_ref, out_ref, first_ref, grad_ref, all_gpk_ref
):
    slots = got_ref.shape[0]

    @pl.when(is_first())
    def _():
        pick = onehot(iota((grad_ref.shape[0], slots), 0) == row_ref[...])
        grad_ref[...] = mm(pick, got_ref[...]).astype(BF16)

    rows = pl.ds(pl.multiple_of(pl.program_id(0) * BALL, BALL), BALL)
    grad_packed = ball_attend_back(pk_ref[...], grad_ref[rows, :], head_size)
    gpk_ref[...] = grad_packed
    all_gpk_ref[rows, :] = grad_packed

    @pl.when(is_last())
    def _():
        first_ref[...] = mm_nt(all_gpk_ref[...], wq_ref[...]).astype(BF16)
        back_rows(row_ref[...], first_ref, out_ref)


def moved_weights_kernel(core_ref, nrm_ref, gpk_ref, gq_ref, gp_ref, keep_ref, send_ref, all_ref):
    width, third = gq_ref.shape
    all_ref[:, :third] = gq_ref[...]
    all_ref[:, third : 2 * third] = mm(flip(nrm_ref[...]), gpk_ref[...]).astype(BF16)
    all_ref[:, 2 * third :] = gp_ref[...]
    half = width // 2
    core = core_ref[0]
    for side, out_ref in ((core, keep_ref), (1 - core, send_ref)):
        rows = pl.ds(pl.multiple_of(side * half, half), half)
        for block in range(all_ref.shape[1] // width):
            out_ref[block * half : (block + 1) * half, :] = all_ref[rows, block * width : (block + 1) * width]


def add_split_kernel(count, after, spot_ref, *refs):
    ins, outs, sum_ref = refs[: -count - 1], refs[-count - 1 : -1], refs[-1]
    total = ins[0][...].astype(F32)
    for in_ref in ins[1:]:
        total = total + in_ref[...].astype(F32)
    sum_ref[...] = total.astype(BF16)
    size = sum_ref.shape[0] // count
    for shift, out_ref in enumerate(outs):
        start = lax.rem(spot_ref[0] + shift, count) * size
        out_ref[...] = sum_ref[pl.ds(pl.multiple_of(start, size), size), :]


def add_kernel(after, also, *refs):
    total = refs[0][...].astype(F32)
    for in_ref in refs[1:-1]:
        total = total + in_ref[...].astype(F32)
    refs[-1][...] = total.astype(BF16)


def add_parts(in_ref):
    total = in_ref[0].astype(F32)
    for part in range(1, in_ref.shape[0]):
        total = total + in_ref[part].astype(F32)
    return total.astype(BF16)


def spread_kernel(after, also, in_ref, out_ref):
    total = add_parts(in_ref)
    for part in range(out_ref.shape[0]):
        out_ref[part] = total


def place_kernel(spot_ref, *refs):
    ins, out_ref = refs[:-1], refs[-1]
    count, size = len(ins), ins[0].shape[0]
    for shift, in_ref in enumerate(ins):
        start = lax.rem(spot_ref[0] + (count - shift), count) * size
        out_ref[pl.ds(pl.multiple_of(start, size), size), :] = in_ref[...]


def last_kernel(_, tok_ref, gm_ref, first_ref, ret_ref, part_ref, out_ref):
    slots = ret_ref.shape[0]
    slot_col = as_column(part_ref[...].astype(F32)).astype(jnp.int32)
    pick = onehot(iota((BALL, slots), 1) == slot_col)
    grad_first = first_ref[...] + mm(pick, ret_ref[...])
    residual = tok_ref[...].astype(F32)
    out_ref[...] = (
        gm_ref[...].astype(F32) + norm_back(residual, row_scale(residual), grad_first)
    ).astype(BF16)


def finish_mlp_kernel(core_ref, mine_ref, other_ref, up_ref, down_ref):
    core = core_ref[0]

    @pl.when(core == 0)
    def _():
        up_ref[...] = mine_ref[...].astype(F32)
        down_ref[...] = other_ref[...].astype(F32).T

    @pl.when(core != 0)
    def _():
        up_ref[...] = other_ref[...].astype(F32)
        down_ref[...] = mine_ref[...].astype(F32).T


def finish_attention_kernel(core_ref, mine_ref, other_ref, qkv_ref, proj_ref):
    core = core_ref[0]
    width = mine_ref.shape[1]
    half = mine_ref.shape[0] // 4
    for side, part_ref in ((core, mine_ref), (1 - core, other_ref)):
        rows = pl.ds(pl.multiple_of(side * half, half), half)
        for block in range(3):
            qkv_ref[rows, block * width : (block + 1) * width] = part_ref[block * half : (block + 1) * half, :].astype(F32)
        proj_ref[rows, :] = part_ref[3 * half :, :].astype(F32)


def exchange(rows, peers):
    slots, columns = rows.shape
    sent = rows.reshape(peers, slots // peers, columns)
    got = lax.all_to_all(sent, ("z", "x", "core"), split_axis=0, concat_axis=0, tiled=True)
    return got.reshape(slots, columns)


def swap_core(block):
    return lax.ppermute(block, "core", [(0, 1), (1, 0)])


def whole_array(array):
    return array, whole(*array.shape)


def spot_on(axis):
    return lax.axis_index(axis).astype(jnp.int32).reshape(1), FLAG


def shift_by(block, axis, shift):
    count = lax.axis_size(axis)
    return lax.ppermute(block, axis, [(place, (place + shift) % count) for place in range(count)])


def add_split(parts, axis, after):
    count = lax.axis_size(axis)
    rows, columns = parts[0].shape
    out = (shape((rows // count, columns)), whole(rows // count, columns))
    shares = call(
        bind(add_split_kernel, count), 1,
        [(after, ANY), spot_on(axis)] + [whole_array(part) for part in parts], [out] * count,
        scratch=[pltpu.VMEM((rows, columns), BF16)], name="add_split",
    )
    return [shares[0]] + [shift_by(shares[shift], axis, shift) for shift in range(1, count)]


def gather(block, axis):
    count = lax.axis_size(axis)
    rows, columns = block.shape
    parts = [block] + [shift_by(block, axis, shift) for shift in range(1, count)]
    (joined,) = call(
        place_kernel, 1, [spot_on(axis)] + [whole_array(part) for part in parts],
        [(shape((count * rows, columns)), whole(count * rows, columns))], name="gather",
    )
    return joined


def add(parts, after, also=None):
    also = after if also is None else also
    (block,) = call(
        add_kernel, 1, [(after, ANY), (also, ANY)] + [whole_array(part) for part in parts],
        [(shape(parts[0].shape), whole(*parts[0].shape))], name="add",
    )
    return block


def share_of_sum(block, axes):
    count = lax.axis_size(axes)
    rows, columns = block.shape
    parts = block.reshape(count, rows // count, columns)
    return lax.all_to_all(parts, axes, split_axis=0, concat_axis=0, tiled=True)


def whole_parts(parts):
    return parts, pl.BlockSpec(parts.shape, lambda step: (0, 0, 0))


def sum_by_steps(block, axes, after):
    parts = [block]
    begun = None
    for axis in axes:
        parts = add_split(parts, axis, after)
        begun = parts[0] if begun is None else begun
    halfway = parts[1]
    block = add(parts, after)
    for axis in reversed(axes):
        block = gather(block, axis)
    return block, begun, halfway


def sum_at_once(block, axes, after, also):
    parts = share_of_sum(block, axes)
    (spread,) = call(
        spread_kernel, 1, [(after, ANY), (also, ANY), whole_parts(parts)], [(shape(parts.shape), whole_parts(parts)[1])], name="add_spread",
    )
    told = lax.all_to_all(spread, axes, split_axis=0, concat_axis=0, tiled=True)
    return told.reshape(block.shape)


def bind(kernel, *fixed):
    def bound(*refs):
        kernel(*fixed, *refs)

    return bound


def body(tokens, rotation, qkv_weight, proj_weight, up_weight, down_weight, cotangent):
    rows, width = tokens.shape
    half = width // 2
    third = 3 * half
    head_size = width // HEADS
    peers = lax.axis_size(("z", "x", "core"))
    group_size = lax.axis_size("narrow")
    capacity = rows // peers + rows // peers // 2
    stride = capacity + 8
    slots = peers * capacity
    wide_slots = peers * stride
    hidden = group_size * up_weight.shape[1]
    balls = rows // BALL
    block = 2 * BALL
    core = lax.axis_index("core")
    flag = (core.astype(jnp.int32).reshape(1), FLAG)
    own_weight = jnp.where(core == 0, up_weight, down_weight)
    all_weights = lax.all_gather(own_weight, ("core", "narrow"), axis=0, tiled=True)
    all_up = (all_weights, whole(hidden, width))

    send, slot = call(
        bind(route_kernel, peers, group_size, capacity, stride), 2,
        [(rotation.reshape(1, rows), whole(1, rows)), (tokens, ANY)],
        [(shape((wide_slots, width)), by_row(width, wide_slots // 2)), (shape((1, rows), jnp.int32), whole(1, rows))],
        scratch=[pltpu.VMEM((1, rows), jnp.int32), pltpu.VMEM((peers, 2 * LANES), BF16)] + late(width, rows),
        flops=LONG, name="route", vmem=VMEM_BYTES,
    )
    got = exchange(send, peers)
    part = (slot, by_column(1, BALL))

    normed, packed, local_heads = call(
        bind(first_local_kernel, head_size), balls,
        [(tokens, by_row(width)), (qkv_weight, whole(width, third))],
        [(shape((rows, width)), by_row(width)), (shape((rows, third)), by_row(third)), (shape((rows, half)), by_row(half))],
        name="first_local",
    )
    moved_weight = (qkv_weight, whole(width, third, 0, 1))
    moved_normed, moved_packed, arrived, outgoing = call(
        bind(moved_kernel, head_size, peers, capacity), balls,
        [(local_heads, ANY), (got, whole(wide_slots, width)), moved_weight],
        [
            (shape((rows, width)), by_row(width)), (shape((rows, third)), by_row(third)),
            (shape((1, slots), jnp.int32), whole(1, slots)), (shape((slots, half)), whole(slots, half)),
        ],
        scratch=[pltpu.VMEM((rows, half), BF16), pltpu.VMEM((rows, width), BF16), pltpu.VMEM((rows, third), BF16)],
        flops=LONG, name="moved", vmem=VMEM_BYTES,
    )
    returned = exchange(outgoing, peers)
    (grad_act,) = call(
        grad_act_kernel, balls,
        [(cotangent, by_row(width)), (all_weights, whole(hidden, width, 1))],
        [(shape((rows, hidden)), by_row(hidden))],
        name="grad_act",
    )
    mixed_heads, middle, second_normed, activated, grad_pre, grad_middle, grad_local, send_grad = call(
        middle_kernel, rows // block,
        [
            (tokens, by_row(width, block)), (local_heads, by_row(half, block)), (returned, whole(slots, half)),
            (slot, by_column(1, block)), (slot, whole(1, rows)), (proj_weight, whole(width, width)), all_up,
            (cotangent, by_row(width, block)), (grad_act, by_row(hidden, block)),
        ],
        [
            (shape((rows, width)), by_row(width, block)), (shape((rows, width)), by_row(width, block)),
            (shape((rows, width)), by_row(width, block)), (shape((rows, hidden)), by_row(hidden, block)),
            (shape((rows, hidden)), by_row(hidden, block)), (shape((rows, width)), by_row(width, block)),
            (shape((rows, half)), by_row(half, block)), (shape((slots, half)), whole(slots, half)),
        ],
        scratch=[pltpu.VMEM((rows, half), BF16)], flops=LONG, name="middle", vmem=VMEM_BYTES,
    )
    got_grad = exchange(send_grad, peers)
    output, mlp_both = call(
        weights_kernel, group_size,
        [
            (middle, whole(rows, width)), (activated, by_column(rows, width)),
            (all_weights, pl.BlockSpec((width, width), lambda step: (group_size + step, 0))),
            (cotangent, whole(rows, width)), (second_normed, whole(rows, width)),
            (grad_pre, by_column(rows, width)),
        ],
        [
            (shape((rows, width)), whole(rows, width)),
            (shape((group_size, 2, width, width)), pl.BlockSpec((1, 2, width, width), lambda step: (step, 0, 0, 0))),
        ],
        scratch=[pltpu.VMEM((width, rows), BF16), pltpu.VMEM((width, rows), BF16), pltpu.VMEM((rows, width), F32)],
        name="mlp_weights", vmem=VMEM_BYTES,
    )
    mlp_part = lax.psum_scatter(
        mlp_both.reshape(2 * hidden, width), ("narrow", "core"), scatter_dimension=0, tiled=True
    )
    first_local, qkv_local, proj_local = call(
        bind(local_back_kernel, head_size), balls,
        [
            (packed, by_row(third)), (grad_local, by_row(half)), (normed, whole(rows, width)),
            (qkv_weight, whole(width, third)), (mixed_heads, whole(rows, width)), (grad_middle, whole(rows, width)),
        ],
        [
            (shape((rows, width), F32), by_row(width)),
            (shape((width, third)), whole(width, third)), (shape((width, width)), whole(width, width)),
        ],
        scratch=[pltpu.VMEM((rows, third), BF16)],
        name="local_back", vmem=VMEM_BYTES,
    )
    moved_grad_packed, grad_outgoing = call(
        bind(moved_back_kernel, head_size), balls,
        [(output, ANY), (got_grad, whole(slots, half)), (arrived, whole(1, slots)), (moved_packed, by_row(third)), moved_weight],
        [(shape((rows, third)), by_row(third)), (shape((slots, width)), whole(slots, width))],
        scratch=[pltpu.VMEM((rows, width), BF16), pltpu.VMEM((rows, half), BF16), pltpu.VMEM((rows, third), BF16)],
        flops=LONG, name="moved_back", vmem=VMEM_BYTES,
    )
    grad_returned = exchange(grad_outgoing, peers)
    stacked = (shape((2 * width, width)), whole(2 * width, width))
    keep, send = call(
        moved_weights_kernel, 1,
        [flag, whole_array(moved_normed), whole_array(moved_grad_packed), whole_array(qkv_local), whole_array(proj_local)],
        [stacked, stacked],
        scratch=[pltpu.VMEM((width, 2 * third + width), BF16)], name="moved_weights",
    )
    pair = add([keep, swap_core(send)], grad_returned)
    mlp_mine, begun, halfway = sum_by_steps(mlp_part, ("x", "z"), pair)
    (grad_tokens,) = call(
        last_kernel, balls,
        [(begun, ANY), (tokens, by_row(width)), (grad_middle, by_row(width)), (first_local, by_row(width)), (grad_returned, whole(slots, width)), part],
        [(shape((rows, width)), by_row(width))],
        flops=LONG, name="last",
    )
    mlp_other = swap_core(mlp_mine)
    grad_up, grad_down = call(
        finish_mlp_kernel, 1, [flag, whole_array(mlp_mine), whole_array(mlp_other)],
        [(shape((width, width), F32), whole(width, width)), (shape((width, width), F32), whole(width, width))],
        name="finish_mlp",
    )
    mine = add([sum_at_once(pair, ("narrow", "x", "z"), halfway, grad_tokens)], mlp_mine)
    grad_qkv, grad_proj = call(
        finish_attention_kernel, 1, [flag, whole_array(mine), whole_array(swap_core(mine))],
        [(shape((width, 2 * third), F32), whole(width, 2 * third)), (shape((width, width), F32), whole(width, width))],
        name="finish_attention",
    )
    return output, grad_tokens, grad_qkv, grad_proj, grad_up, grad_down


def solution(mesh):
    wide, narrow = mesh.devices.shape
    axes = ("z", "x", "core", "narrow")
    mesh = Mesh(mesh.devices.reshape(wide // 8, 4, 2, narrow), axes)
    rows = axes
    return jax.shard_map(
        body,
        mesh=mesh,
        in_specs=(
            P(rows, None),
            P(rows),
            P(),
            P(),
            P(None, "narrow"),
            P("narrow", None),
            P(rows, None),
        ),
        out_specs=(
            P(rows, None),
            P(rows, None),
            P(),
            P(),
            P(None, "narrow"),
            P("narrow", None),
        ),
        check_vma=False,
    )
```

```python
import jax
import jax.numpy as jnp
from jax import lax
from jax.experimental import pallas as pl
from jax.experimental.pallas import tpu as pltpu
from jax.sharding import Mesh
from jax.sharding import PartitionSpec as P

HEADS = 8
BALL = 256
EPSILON = 1e-06
LANES = 128
VMEM_BYTES = 60 * 1024 * 1024
SMALL_BYTES = 16 * 1024 * 1024

LONG = 10**11

F32 = jnp.float32
BF16 = jnp.bfloat16


def mm(left, right):
    return lax.dot_general(left, right, (((1,), (0,)), ((), ())), preferred_element_type=F32)


def mm_nt(left, right):
    return lax.dot_general(left, right, (((1,), (1,)), ((), ())), preferred_element_type=F32)


def mm_tn(left, right):
    return lax.dot_general(left, right, (((0,), (0,)), ((), ())), preferred_element_type=F32)


def iota(shape, dimension):
    return lax.broadcasted_iota(jnp.int32, shape, dimension)


def row_scale(values):
    return lax.rsqrt(jnp.mean(values * values, axis=-1, keepdims=True) + EPSILON)


def norm_back(values, scaling, gradient):
    unit = values * scaling
    return scaling * (gradient - unit * jnp.mean(gradient * unit, axis=-1, keepdims=True))


def flip(block):
    return block.astype(F32).T.astype(BF16)


def as_column(row):
    return jnp.broadcast_to(row, (8, row.shape[1])).T[:, :1]


def onehot(condition):
    return jnp.where(condition, 1.0, 0.0).astype(BF16)


def head_mask(columns, head, head_size, value):
    lane = iota((1, columns), 1)
    inside = (lane >= head * head_size) & (lane < (head + 1) * head_size)
    return jnp.where(inside, value, 0.0).astype(BF16)


def by_head(rows, head_size, value):
    columns = rows.shape[1]
    heads = [rows * head_mask(columns, head, head_size, value) for head in range(columns // head_size)]
    return jnp.concatenate(heads, axis=0)


def ball_weights(key_rows, asked):
    scores = mm_nt(key_rows, asked)
    raised = jnp.exp(scores - jnp.max(scores, axis=0, keepdims=True))
    return raised * (1.0 / jnp.sum(raised, axis=0, keepdims=True))


def ball_attend(packed, head_size):
    columns = packed.shape[1] // 3
    queries, key_rows = packed[:, :columns], packed[:, columns : 2 * columns]
    rounded = ball_weights(key_rows, by_head(queries, head_size, head_size ** (-0.5))).astype(BF16)
    return per_head(flip(packed[:, 2 * columns :]), rounded, head_size).astype(BF16)


def per_head(rows_t, weights, head_size):
    columns, count = rows_t.shape
    parts = [
        mm(rows_t[head * head_size : (head + 1) * head_size], weights[:, head * count : (head + 1) * count])
        for head in range(columns // head_size)
    ]
    return jnp.concatenate(parts, axis=0).T


def ball_attend_back(packed, grad_out, head_size):
    columns = packed.shape[1] // 3
    queries, key_rows = packed[:, :columns], packed[:, columns : 2 * columns]
    asked = by_head(queries, head_size, head_size ** (-0.5))
    upstream = by_head(grad_out, head_size, 1.0)
    weights = ball_weights(key_rows, asked)
    dprob = mm_nt(packed[:, 2 * columns :], upstream)
    dscore = weights * (dprob - jnp.sum(dprob * weights, axis=0, keepdims=True))
    dscore = dscore.astype(BF16)
    grad_values = mm(weights.astype(BF16), upstream)
    grad_keys = mm(dscore, asked)
    grad_queries = per_head(flip(key_rows * jnp.asarray(head_size ** (-0.5), BF16)), dscore, head_size)
    return jnp.concatenate([grad_queries, grad_keys, grad_values], axis=1).astype(BF16)


def shape(dims, dtype=BF16):
    return jax.ShapeDtypeStruct(dims, dtype)


def by_row(columns, rows=BALL):
    return pl.BlockSpec((rows, columns), lambda step: (step, 0))


def by_column(rows, columns):
    return pl.BlockSpec((rows, columns), lambda step: (0, step))


def whole(rows, columns, row=0, column=0):
    return pl.BlockSpec((rows, columns), lambda step: (row, column))


FLAG = pl.BlockSpec(memory_space=pltpu.SMEM)
ANY = pl.BlockSpec(memory_space=pl.ANY)


def call(kernel, steps, ins, outs, scratch=(), flops=0, name=None, vmem=SMALL_BYTES):
    return pl.pallas_call(
        kernel,
        grid=(steps,),
        out_shape=[out for out, _ in outs],
        in_specs=[spec for _, spec in ins],
        out_specs=[spec for _, spec in outs],
        scratch_shapes=list(scratch),
        compiler_params=pltpu.CompilerParams(vmem_limit_bytes=vmem),
        cost_estimate=pl.CostEstimate(flops=flops, bytes_accessed=0, transcendentals=0),
        name=name,
    )(*[array for array, _ in ins])


def is_first():
    return pl.program_id(0) == 0


def is_last():
    return pl.program_id(0) == pl.num_programs(0) - 1


def late(columns, rows):
    return [pltpu.VMEM((rows, columns), BF16), pltpu.SemaphoreType.DMA(())]


def fetch(source, kept_ref, sem):
    copy = pltpu.make_async_copy(source, kept_ref, sem)

    @pl.when(is_first())
    def _():
        copy.start()

    def arrive():
        @pl.when(is_first())
        def _():
            copy.wait()

    return arrive


def route_kernel(
    peers, group_size, capacity, stride, rot_ref, all_ref, send_ref, slot_ref, wide_ref, place_ref, tok_ref, sem
):
    row_count = tok_ref.shape[0]
    step = BALL
    arrive = fetch(all_ref, tok_ref, sem)
    block = send_ref.shape[0]

    @pl.when(is_first())
    def _():
        rotation = rot_ref[...]
        target = rotation // (row_count * group_size)
        position = rotation % row_count + 1
        high = (position // 256).astype(F32)
        low = (position % 256).astype(F32)
        earlier = onehot(iota((step, step), 0) < iota((step, step), 1))
        carry = jnp.zeros((peers, 1), F32)
        sums_high = jnp.zeros((peers, LANES), F32)
        sums_low = jnp.zeros((peers, LANES), F32)
        for start in range(0, row_count, step):
            part = slice(start, start + step)
            chosen = jnp.where(iota((peers, step), 0) == target[:, part], 1.0, 0.0)
            before = mm(chosen.astype(BF16), earlier) + carry
            carry = carry + jnp.sum(chosen, axis=1, keepdims=True)
            rank = jnp.sum(chosen * before, axis=0, keepdims=True).astype(jnp.int32)
            slot_ref[:, part] = target[:, part] * capacity + rank
            wide_ref[:, part] = target[:, part] * stride + rank
            place = onehot(iota((LANES, step), 0) == rank)
            sums_high = sums_high + mm_nt((chosen * high[:, part]).astype(BF16), place)
            sums_low = sums_low + mm_nt((chosen * low[:, part]).astype(BF16), place)
        place_ref[:, :LANES] = sums_high.astype(BF16)
        place_ref[:, LANES:] = sums_low.astype(BF16)

    arrive()
    base = pl.program_id(0) * block
    pick = onehot(iota((block, row_count), 0) + base == wide_ref[...])
    rows = mm(pick, tok_ref[...])
    told = onehot(iota((block, peers), 0) + base == iota((block, peers), 1) * stride + capacity)
    extra = mm(told, place_ref[...])
    send_ref[:, : 2 * LANES] = (rows[:, : 2 * LANES] + extra).astype(BF16)
    send_ref[:, 2 * LANES :] = rows[:, 2 * LANES :].astype(BF16)


def arrived_row(place, stride):
    peers = place.shape[0]
    slots = peers * stride
    column = iota((1, slots), 1)
    source = column // stride
    spot = onehot(iota((LANES, slots), 0) == column - source * stride)
    spread = mm(place[:, :LANES], spot) * 256.0 + mm(place[:, LANES:], spot)
    own = iota((peers, slots), 0) == source
    return jnp.sum(jnp.where(own, spread, 0.0), axis=0, keepdims=True).astype(jnp.int32) - 1


def back_rows(arrived, rows_ref, out_ref):
    slots, step = out_ref.shape[0], 2 * BALL
    row_count = rows_ref.shape[0]
    arrived_col = as_column(arrived.astype(F32)).astype(jnp.int32)
    moved = rows_ref[...]
    for start in range(0, slots, step):
        pick = onehot(iota((step, row_count), 1) == arrived_col[start : start + step])
        out_ref[start : start + step, :] = mm(pick, moved).astype(BF16)


def first_local_kernel(head_size, tok_ref, wq_ref, nrm_ref, pk_ref, heads_ref):
    residual = tok_ref[...].astype(F32)
    normed = (residual * row_scale(residual)).astype(BF16)
    nrm_ref[...] = normed
    packed = mm(normed, wq_ref[...]).astype(BF16)
    pk_ref[...] = packed
    heads_ref[...] = ball_attend(packed, head_size)


def grad_act_kernel(cot_ref, down_ref, act_ref):
    act_ref[...] = mm_nt(cot_ref[...], down_ref[...]).astype(BF16)


def moved_kernel(
    head_size, peers, capacity, _, got_ref, wq_ref, nrm_ref, pk_ref, row_ref, out_ref,
    heads_ref, all_nrm_ref, all_pk_ref,
):
    slots = got_ref.shape[0]
    row_count = heads_ref.shape[0]
    stride = slots // peers

    @pl.when(is_first())
    def _():
        told = onehot(iota((peers, slots), 1) == iota((peers, slots), 0) * stride + capacity)
        place = mm(told, got_ref[:, : 2 * LANES]).astype(BF16)
        row_ref[...] = arrived_row(place, capacity)
        pick = onehot(iota((row_count, slots), 0) == arrived_row(place, stride))
        residual = mm(pick, got_ref[...])
        normed = (residual * row_scale(residual)).astype(BF16)
        all_nrm_ref[...] = normed
        all_pk_ref[...] = mm(normed, wq_ref[...]).astype(BF16)

    rows = pl.ds(pl.multiple_of(pl.program_id(0) * BALL, BALL), BALL)
    nrm_ref[...] = all_nrm_ref[rows, :]
    packed = all_pk_ref[rows, :]
    pk_ref[...] = packed
    heads_ref[rows, :] = ball_attend(packed, head_size)

    @pl.when(is_last())
    def _():
        back_rows(row_ref[...], heads_ref, out_ref)


def middle_kernel(
    tok_ref, local_ref, ret_ref, part_ref, slot_ref, proj_ref, up_ref, cot_ref, act_ref,
    mix_ref, mid_ref, sn_ref, gated_ref, pre_ref, gm_ref, gl_ref, send_ref, gh_ref,
):
    count, width = tok_ref.shape
    half = width // 2
    slots = ret_ref.shape[0]
    chunks = up_ref.shape[0] // width
    rate = 0.7978845608028654
    cubic = 0.044715 * rate
    slot_col = as_column(part_ref[...].astype(F32)).astype(jnp.int32)
    pick = onehot(iota((count, slots), 1) == slot_col)
    moved = mm(pick, ret_ref[...]).astype(BF16)
    mixed = jnp.concatenate([local_ref[...], moved], axis=1)
    mix_ref[...] = mixed
    middle = (tok_ref[...].astype(F32) + mm(mixed, proj_ref[...])).astype(BF16)
    mid_ref[...] = middle
    middle_f = middle.astype(F32)
    second_scale = row_scale(middle_f)
    normed = (middle_f * second_scale).astype(BF16)
    sn_ref[...] = normed
    grad_second = jnp.zeros((count, width), F32)
    pres = [mm(normed, up_ref[chunk * width : (chunk + 1) * width, :]) for chunk in range(chunks)]
    for chunk, pre in enumerate(pres):
        columns = slice(chunk * width, (chunk + 1) * width)
        square = pre * pre
        upper = 0.5 + 0.5 * jnp.tanh(pre * (rate + cubic * square))
        gated_ref[:, columns] = (pre * upper).astype(BF16)
        slope = upper * (1.0 + (1.0 - upper) * (pre * (2.0 * rate + 6.0 * cubic * square)))
        grad_pre = (act_ref[:, columns].astype(F32) * slope).astype(BF16)
        pre_ref[:, columns] = grad_pre
        grad_second = grad_second + mm_nt(grad_pre, up_ref[columns, :])
    grad_middle = (
        cot_ref[...].astype(F32) + norm_back(middle_f, second_scale, grad_second)
    ).astype(BF16)
    gm_ref[...] = grad_middle
    grad_heads = mm_nt(grad_middle, proj_ref[...]).astype(BF16)
    gl_ref[...] = grad_heads[:, :half]
    base = pl.multiple_of(pl.program_id(0) * count, count)
    gh_ref[pl.ds(base, count), :] = grad_heads[:, half:]

    @pl.when(is_last())
    def _():
        moved_grad = gh_ref[...]
        slot = slot_ref[...]
        step = 2 * BALL
        for start in range(0, slots, step):
            pick = onehot(iota((step, slot.shape[1]), 0) + start == slot)
            send_ref[start : start + step, :] = mm(pick, moved_grad).astype(BF16)


def weights_kernel(
    mid_ref, gated_ref, down_ref, cot_ref, sn_ref, pre_ref,
    out_ref, both_ref, sn_t_ref, cot_t_ref, sum_ref,
):
    @pl.when(is_first())
    def _():
        sn_t_ref[...] = flip(sn_ref[...])
        cot_t_ref[...] = flip(cot_ref[...])
        sum_ref[...] = mid_ref[...].astype(F32)

    gated = gated_ref[...]
    both_ref[0, 0] = mm(sn_t_ref[...], pre_ref[...]).astype(BF16)
    both_ref[0, 1] = mm(cot_t_ref[...], gated).astype(BF16)
    sum_ref[...] += mm(gated, down_ref[...])

    @pl.when(is_last())
    def _():
        out_ref[...] = sum_ref[...].astype(BF16)


def local_back_kernel(
    head_size, pk_ref, gl_ref, nrm_ref, wq_ref, mix_ref, gm_ref,
    first_ref, gq_ref, gp_ref, gpk_ref,
):
    grad_packed = ball_attend_back(pk_ref[...], gl_ref[...], head_size)
    base = pl.multiple_of(pl.program_id(0) * BALL, BALL)
    gpk_ref[pl.ds(base, BALL), :] = grad_packed
    first_ref[...] = mm_nt(grad_packed, wq_ref[...])

    @pl.when(is_last())
    def _():
        gq_ref[...] = mm(flip(nrm_ref[...]), gpk_ref[...]).astype(BF16)
        gp_ref[...] = mm(flip(mix_ref[...]), gm_ref[...]).astype(BF16)


def moved_back_kernel(
    head_size, _, got_ref, row_ref, pk_ref, wq_ref, gpk_ref, out_ref, first_ref, grad_ref, all_gpk_ref
):
    slots = got_ref.shape[0]

    @pl.when(is_first())
    def _():
        pick = onehot(iota((grad_ref.shape[0], slots), 0) == row_ref[...])
        grad_ref[...] = mm(pick, got_ref[...]).astype(BF16)

    rows = pl.ds(pl.multiple_of(pl.program_id(0) * BALL, BALL), BALL)
    grad_packed = ball_attend_back(pk_ref[...], grad_ref[rows, :], head_size)
    gpk_ref[...] = grad_packed
    all_gpk_ref[rows, :] = grad_packed

    @pl.when(is_last())
    def _():
        first_ref[...] = mm_nt(all_gpk_ref[...], wq_ref[...]).astype(BF16)
        back_rows(row_ref[...], first_ref, out_ref)


def moved_weights_kernel(core_ref, nrm_ref, gpk_ref, gq_ref, gp_ref, keep_ref, send_ref, all_ref):
    width, third = gq_ref.shape
    all_ref[:, :third] = gq_ref[...]
    all_ref[:, third : 2 * third] = mm(flip(nrm_ref[...]), gpk_ref[...]).astype(BF16)
    all_ref[:, 2 * third :] = gp_ref[...]
    half = width // 2
    core = core_ref[0]
    for side, out_ref in ((core, keep_ref), (1 - core, send_ref)):
        rows = pl.ds(pl.multiple_of(side * half, half), half)
        for block in range(all_ref.shape[1] // width):
            out_ref[block * half : (block + 1) * half, :] = all_ref[rows, block * width : (block + 1) * width]


def add_split_kernel(count, after, spot_ref, *refs):
    ins, outs, sum_ref = refs[: -count - 1], refs[-count - 1 : -1], refs[-1]
    total = ins[0][...].astype(F32)
    for in_ref in ins[1:]:
        total = total + in_ref[...].astype(F32)
    sum_ref[...] = total.astype(BF16)
    size = sum_ref.shape[0] // count
    for shift, out_ref in enumerate(outs):
        start = lax.rem(spot_ref[0] + shift, count) * size
        out_ref[...] = sum_ref[pl.ds(pl.multiple_of(start, size), size), :]


def add_kernel(after, also, *refs):
    total = refs[0][...].astype(F32)
    for in_ref in refs[1:-1]:
        total = total + in_ref[...].astype(F32)
    refs[-1][...] = total.astype(BF16)


def add_parts(in_ref):
    total = in_ref[0].astype(F32)
    for part in range(1, in_ref.shape[0]):
        total = total + in_ref[part].astype(F32)
    return total.astype(BF16)


def spread_kernel(after, in_ref, out_ref):
    total = add_parts(in_ref)
    for part in range(out_ref.shape[0]):
        out_ref[part] = total


def place_kernel(spot_ref, *refs):
    ins, out_ref = refs[:-1], refs[-1]
    count, size = len(ins), ins[0].shape[0]
    for shift, in_ref in enumerate(ins):
        start = lax.rem(spot_ref[0] + (count - shift), count) * size
        out_ref[pl.ds(pl.multiple_of(start, size), size), :] = in_ref[...]


def last_kernel(_, tok_ref, gm_ref, first_ref, ret_ref, part_ref, out_ref):
    slots = ret_ref.shape[0]
    slot_col = as_column(part_ref[...].astype(F32)).astype(jnp.int32)
    pick = onehot(iota((BALL, slots), 1) == slot_col)
    grad_first = first_ref[...] + mm(pick, ret_ref[...])
    residual = tok_ref[...].astype(F32)
    out_ref[...] = (
        gm_ref[...].astype(F32) + norm_back(residual, row_scale(residual), grad_first)
    ).astype(BF16)


def finish_mlp_kernel(core_ref, mine_ref, other_ref, up_ref, down_ref):
    core = core_ref[0]

    @pl.when(core == 0)
    def _():
        up_ref[...] = mine_ref[...].astype(F32)
        down_ref[...] = other_ref[...].astype(F32).T

    @pl.when(core != 0)
    def _():
        up_ref[...] = other_ref[...].astype(F32)
        down_ref[...] = mine_ref[...].astype(F32).T


def finish_attention_kernel(core_ref, mine_ref, other_ref, qkv_ref, proj_ref):
    core = core_ref[0]
    width = mine_ref.shape[1]
    half = mine_ref.shape[0] // 4
    for side, part_ref in ((core, mine_ref), (1 - core, other_ref)):
        rows = pl.ds(pl.multiple_of(side * half, half), half)
        for block in range(3):
            qkv_ref[rows, block * width : (block + 1) * width] = part_ref[block * half : (block + 1) * half, :].astype(F32)
        proj_ref[rows, :] = part_ref[3 * half :, :].astype(F32)


def exchange(rows, peers):
    slots, columns = rows.shape
    sent = rows.reshape(peers, slots // peers, columns)
    got = lax.all_to_all(sent, ("z", "x", "core"), split_axis=0, concat_axis=0, tiled=True)
    return got.reshape(slots, columns)


def swap_core(block):
    return lax.ppermute(block, "core", [(0, 1), (1, 0)])


def whole_array(array):
    return array, whole(*array.shape)


def spot_on(axis):
    return lax.axis_index(axis).astype(jnp.int32).reshape(1), FLAG


def shift_by(block, axis, shift):
    count = lax.axis_size(axis)
    return lax.ppermute(block, axis, [(place, (place + shift) % count) for place in range(count)])


def add_split(parts, axis, after):
    count = lax.axis_size(axis)
    rows, columns = parts[0].shape
    out = (shape((rows // count, columns)), whole(rows // count, columns))
    shares = call(
        bind(add_split_kernel, count), 1,
        [(after, ANY), spot_on(axis)] + [whole_array(part) for part in parts], [out] * count,
        scratch=[pltpu.VMEM((rows, columns), BF16)], name="add_split",
    )
    return [shares[0]] + [shift_by(shares[shift], axis, shift) for shift in range(1, count)]


def gather(block, axis):
    count = lax.axis_size(axis)
    rows, columns = block.shape
    parts = [block] + [shift_by(block, axis, shift) for shift in range(1, count)]
    (joined,) = call(
        place_kernel, 1, [spot_on(axis)] + [whole_array(part) for part in parts],
        [(shape((count * rows, columns)), whole(count * rows, columns))], name="gather",
    )
    return joined


def add(parts, after, also=None):
    also = after if also is None else also
    (block,) = call(
        add_kernel, 1, [(after, ANY), (also, ANY)] + [whole_array(part) for part in parts],
        [(shape(parts[0].shape), whole(*parts[0].shape))], name="add",
    )
    return block


def share_of_sum(block, axes):
    count = lax.axis_size(axes)
    rows, columns = block.shape
    parts = block.reshape(count, rows // count, columns)
    return lax.all_to_all(parts, axes, split_axis=0, concat_axis=0, tiled=True)


def whole_parts(parts):
    return parts, pl.BlockSpec(parts.shape, lambda step: (0, 0, 0))


def sum_by_steps(block, axes, after):
    parts = [block]
    for axis in axes:
        parts = add_split(parts, axis, after)
    halfway = parts[0]
    block = add(parts, after)
    for axis in reversed(axes):
        block = gather(block, axis)
    return block, halfway


def sum_at_once(block, axes, after):
    parts = share_of_sum(block, axes)
    (spread,) = call(
        spread_kernel, 1, [(after, ANY), whole_parts(parts)], [(shape(parts.shape), whole_parts(parts)[1])], name="add_spread",
    )
    told = lax.all_to_all(spread, axes, split_axis=0, concat_axis=0, tiled=True)
    return told.reshape(block.shape)


def bind(kernel, *fixed):
    def bound(*refs):
        kernel(*fixed, *refs)

    return bound


def body(tokens, rotation, qkv_weight, proj_weight, up_weight, down_weight, cotangent):
    rows, width = tokens.shape
    half = width // 2
    third = 3 * half
    head_size = width // HEADS
    peers = lax.axis_size(("z", "x", "core"))
    group_size = lax.axis_size("narrow")
    capacity = rows // peers + rows // peers // 2
    stride = capacity + 8
    slots = peers * capacity
    wide_slots = peers * stride
    hidden = group_size * up_weight.shape[1]
    balls = rows // BALL
    block = 2 * BALL
    core = lax.axis_index("core")
    flag = (core.astype(jnp.int32).reshape(1), FLAG)
    own_weight = jnp.where(core == 0, up_weight, down_weight)
    all_weights = lax.all_gather(own_weight, ("core", "narrow"), axis=0, tiled=True)
    all_up = (all_weights, whole(hidden, width))

    send, slot = call(
        bind(route_kernel, peers, group_size, capacity, stride), 2,
        [(rotation.reshape(1, rows), whole(1, rows)), (tokens, ANY)],
        [(shape((wide_slots, width)), by_row(width, wide_slots // 2)), (shape((1, rows), jnp.int32), whole(1, rows))],
        scratch=[pltpu.VMEM((1, rows), jnp.int32), pltpu.VMEM((peers, 2 * LANES), BF16)] + late(width, rows),
        flops=LONG, name="route", vmem=VMEM_BYTES,
    )
    got = exchange(send, peers)
    part = (slot, by_column(1, BALL))

    normed, packed, local_heads = call(
        bind(first_local_kernel, head_size), balls,
        [(tokens, by_row(width)), (qkv_weight, whole(width, third))],
        [(shape((rows, width)), by_row(width)), (shape((rows, third)), by_row(third)), (shape((rows, half)), by_row(half))],
        name="first_local",
    )
    moved_weight = (qkv_weight, whole(width, third, 0, 1))
    moved_normed, moved_packed, arrived, outgoing = call(
        bind(moved_kernel, head_size, peers, capacity), balls,
        [(local_heads, ANY), (got, whole(wide_slots, width)), moved_weight],
        [
            (shape((rows, width)), by_row(width)), (shape((rows, third)), by_row(third)),
            (shape((1, slots), jnp.int32), whole(1, slots)), (shape((slots, half)), whole(slots, half)),
        ],
        scratch=[pltpu.VMEM((rows, half), BF16), pltpu.VMEM((rows, width), BF16), pltpu.VMEM((rows, third), BF16)],
        flops=LONG, name="moved", vmem=VMEM_BYTES,
    )
    returned = exchange(outgoing, peers)
    (grad_act,) = call(
        grad_act_kernel, balls,
        [(cotangent, by_row(width)), (all_weights, whole(hidden, width, 1))],
        [(shape((rows, hidden)), by_row(hidden))],
        name="grad_act",
    )
    mixed_heads, middle, second_normed, activated, grad_pre, grad_middle, grad_local, send_grad = call(
        middle_kernel, rows // block,
        [
            (tokens, by_row(width, block)), (local_heads, by_row(half, block)), (returned, whole(slots, half)),
            (slot, by_column(1, block)), (slot, whole(1, rows)), (proj_weight, whole(width, width)), all_up,
            (cotangent, by_row(width, block)), (grad_act, by_row(hidden, block)),
        ],
        [
            (shape((rows, width)), by_row(width, block)), (shape((rows, width)), by_row(width, block)),
            (shape((rows, width)), by_row(width, block)), (shape((rows, hidden)), by_row(hidden, block)),
            (shape((rows, hidden)), by_row(hidden, block)), (shape((rows, width)), by_row(width, block)),
            (shape((rows, half)), by_row(half, block)), (shape((slots, half)), whole(slots, half)),
        ],
        scratch=[pltpu.VMEM((rows, half), BF16)], flops=LONG, name="middle", vmem=VMEM_BYTES,
    )
    got_grad = exchange(send_grad, peers)
    output, mlp_both = call(
        weights_kernel, group_size,
        [
            (middle, whole(rows, width)), (activated, by_column(rows, width)),
            (all_weights, pl.BlockSpec((width, width), lambda step: (group_size + step, 0))),
            (cotangent, whole(rows, width)), (second_normed, whole(rows, width)),
            (grad_pre, by_column(rows, width)),
        ],
        [
            (shape((rows, width)), whole(rows, width)),
            (shape((group_size, 2, width, width)), pl.BlockSpec((1, 2, width, width), lambda step: (step, 0, 0, 0))),
        ],
        scratch=[pltpu.VMEM((width, rows), BF16), pltpu.VMEM((width, rows), BF16), pltpu.VMEM((rows, width), F32)],
        name="mlp_weights", vmem=VMEM_BYTES,
    )
    mlp_part = lax.psum_scatter(
        mlp_both.reshape(2 * hidden, width), ("narrow", "core"), scatter_dimension=0, tiled=True
    )
    first_local, qkv_local, proj_local = call(
        bind(local_back_kernel, head_size), balls,
        [
            (packed, by_row(third)), (grad_local, by_row(half)), (normed, whole(rows, width)),
            (qkv_weight, whole(width, third)), (mixed_heads, whole(rows, width)), (grad_middle, whole(rows, width)),
        ],
        [
            (shape((rows, width), F32), by_row(width)),
            (shape((width, third)), whole(width, third)), (shape((width, width)), whole(width, width)),
        ],
        scratch=[pltpu.VMEM((rows, third), BF16)],
        name="local_back", vmem=VMEM_BYTES,
    )
    moved_grad_packed, grad_outgoing = call(
        bind(moved_back_kernel, head_size), balls,
        [(output, ANY), (got_grad, whole(slots, half)), (arrived, whole(1, slots)), (moved_packed, by_row(third)), moved_weight],
        [(shape((rows, third)), by_row(third)), (shape((slots, width)), whole(slots, width))],
        scratch=[pltpu.VMEM((rows, width), BF16), pltpu.VMEM((rows, half), BF16), pltpu.VMEM((rows, third), BF16)],
        flops=LONG, name="moved_back", vmem=VMEM_BYTES,
    )
    grad_returned = exchange(grad_outgoing, peers)
    stacked = (shape((2 * width, width)), whole(2 * width, width))
    keep, send = call(
        moved_weights_kernel, 1,
        [flag, whole_array(moved_normed), whole_array(moved_grad_packed), whole_array(qkv_local), whole_array(proj_local)],
        [stacked, stacked],
        scratch=[pltpu.VMEM((width, 2 * third + width), BF16)], name="moved_weights",
    )
    pair = add([keep, swap_core(send)], grad_returned)
    mlp_mine, halfway = sum_by_steps(mlp_part, ("x", "z"), pair)
    (grad_tokens,) = call(
        last_kernel, balls,
        [(halfway, ANY), (tokens, by_row(width)), (grad_middle, by_row(width)), (first_local, by_row(width)), (grad_returned, whole(slots, width)), part],
        [(shape((rows, width)), by_row(width))],
        flops=LONG, name="last",
    )
    mlp_other = swap_core(mlp_mine)
    grad_up, grad_down = call(
        finish_mlp_kernel, 1, [flag, whole_array(mlp_mine), whole_array(mlp_other)],
        [(shape((width, width), F32), whole(width, width)), (shape((width, width), F32), whole(width, width))],
        name="finish_mlp",
    )
    mine = add([sum_at_once(pair, ("z", "x", "narrow"), halfway)], mlp_mine, grad_tokens)
    grad_qkv, grad_proj = call(
        finish_attention_kernel, 1, [flag, whole_array(mine), whole_array(swap_core(mine))],
        [(shape((width, 2 * third), F32), whole(width, 2 * third)), (shape((width, width), F32), whole(width, width))],
        name="finish_attention",
    )
    return output, grad_tokens, grad_qkv, grad_proj, grad_up, grad_down


def solution(mesh):
    wide, narrow = mesh.devices.shape
    axes = ("z", "x", "core", "narrow")
    mesh = Mesh(mesh.devices.reshape(wide // 8, 4, 2, narrow), axes)
    rows = axes
    return jax.shard_map(
        body,
        mesh=mesh,
        in_specs=(
            P(rows, None),
            P(rows),
            P(),
            P(),
            P(None, "narrow"),
            P("narrow", None),
            P(rows, None),
        ),
        out_specs=(
            P(rows, None),
            P(rows, None),
            P(),
            P(),
            P(None, "narrow"),
            P("narrow", None),
        ),
        check_vma=False,
    )
```
